128 devices in a mesh: dp: 8 (over y_lo, z), ctx: 16 (over y_hi, x, core).
Axes of the slice: x: 4, y: 4 (y_hi: 2, y_lo: 2; y = y_hi * 2 + y_lo), z: 4, core: 2. Of those that a mesh axis runs over, the one named last changes fastest.
Arguments:
- tokens: bfloat16 [16384, 1024], P(('dp', 'ctx')), may hold values from -6 to 6
- cotangent: bfloat16 [16384, 1024], P(('dp', 'ctx')), may hold values from -6 to 6
- block_order: int32 [16], replicated, may hold values from 0 to 15, each once
- routes: int32 [16384, 8], P(('dp', 'ctx')), may hold values from 0 to 31, all different within a row; in each aligned block of 128 rows (0 to 127, 128 to 255, ...) at most 48 rows name the same one
- norm_one: bfloat16 [1024], P(('dp', 'ctx')), may hold values from 0.099609375 to 1.8984375
- w_query: bfloat16 [1024, 1024], P(('dp', 'ctx')), may hold values from -0.1875 to 0.1875
- w_key: bfloat16 [1024, 512], P(('dp', 'ctx')), may hold values from -0.1875 to 0.1875
- w_value: bfloat16 [1024, 512], P(('dp', 'ctx')), may hold values from -0.1875 to 0.1875
- w_out: bfloat16 [1024, 1024], P(('dp', 'ctx')), may hold values from -3 to 3
- norm_two: bfloat16 [1024], P(('dp', 'ctx')), may hold values from 0.099609375 to 1.8984375
- w_router: bfloat16 [1024, 32], P(('dp', 'ctx')), may hold values from -0.09375 to 0.09375
- expert_in: bfloat16 [32, 1024, 1024], P('ctx', 'dp'), may hold values from -0.1875 to 0.1875
- expert_out: bfloat16 [32, 512, 1024], P('ctx', None, 'dp'), may hold values from -1 to 1
Outputs:
- output: float32 [16384, 1024], P(('dp', 'ctx'))
- input_grad: float32 [16384, 1024], P(('dp', 'ctx'))
- grad_norm_one: float32 [1024], P(('dp', 'ctx'))
- grad_w_query: float32 [1024, 1024], P(('dp', 'ctx'))
- grad_w_key: float32 [1024, 512], P(('dp', 'ctx'))
- grad_w_value: float32 [1024, 512], P(('dp', 'ctx'))
- grad_w_out: float32 [1024, 1024], P(('dp', 'ctx'))
- grad_norm_two: float32 [1024], P(('dp', 'ctx'))
- grad_w_router: float32 [1024, 32], P(('dp', 'ctx'))
- grad_expert_in: float32 [32, 1024, 1024], P('ctx', 'dp')
- grad_expert_out: float32 [32, 512, 1024], P('ctx', None, 'dp')
The draws below stay inside these ranges and needn't reach their ends.
Inputs may be any that keep to these rules, and one draw needn't show every extreme that they name: `routes`: each row names 8 different experts; the rows of one device name any expert at most 48 times, a bound that some block reaches. A permutation; ctx index c holds, in this order, blocks block_order[c] and 31 - block_order[c] of its sequence's 2 * 16 blocks.
All inputs are finite; a program needn't handle non-finite values.
Results may differ from the reference program's by a relative error of at most 0.024.
Values may be sent and summed in bfloat16 or wider, within the bound.
A program may use at most 128 MiB of HBM per device.

```python
import math
import jax
import jax.numpy as jnp
import numpy as np
from jax import lax

D = 1024
HEADS = 16
KV_HEADS = 8
HEAD_DIM = 64
EXPERTS = 32
FF = 512
TOP = 8
TOK_DEV = 128
SEQ = 2048
TOKENS = 16384
MOST = 48
N_DP = 8
N_CTX = 16


def levels(rng, shape, shards, low, high):
    def one(position, parts):
        steps = jax.random.uniform(jax.random.fold_in(jax.random.fold_in(rng, 6), position), (parts,), jnp.float32, low / len(shards), high / len(shards))
        return jnp.repeat(jnp.exp(steps), shape[position] // parts).reshape((-1,) + (1,) * (len(shape) - position - 1))

    factor_of = one(*shards[0])
    for cut in shards[1:]:
        factor_of = factor_of * one(*cut)
    return factor_of


def shared_out(own_key, own, number, rows, count, top, reach, skew):
    sequence = jax.random.permutation(own_key, count)
    crowded, ordinary = load_shares(count, rows * top, reach, skew, True), load_shares(count, rows * top, reach, skew, False)
    places = jnp.arange(count)

    def named(sizes, rotation):
        used = int((sizes > 0).sum())
        fixed = max(1, used // 4)
        shifted = fixed + (places - fixed + rotation * (used - fixed)) % max(1, count - fixed)
        return jnp.zeros((count,), jnp.int32).at[sequence[jnp.where(places < fixed, places, shifted)]].set(jnp.asarray(sizes, jnp.int32))

    sizes = jnp.where(number % 4 == 0, named(crowded, number // 4), named(ordinary, number - number // 4 - 1))
    mixed = jax.random.permutation(jax.random.fold_in(own, 3), count)
    giver, sink = mixed[0:count // 2 * 2:2], mixed[1:count // 2 * 2:2]
    margin = jnp.minimum(sizes[giver] - 1, reach - sizes[sink]) // 2
    margin = jnp.where((giver == sequence[0]) | (sink == sequence[0]) | (sizes[sink] == 0), 0, jnp.maximum(margin, 0))
    shifted = jax.random.randint(jax.random.fold_in(own, 4), (count // 2,), 0, 1 << 20) % (margin + 1)
    sizes = sizes.at[giver].add(-shifted).at[sink].add(shifted)
    items = jnp.searchsorted(jnp.cumsum(sizes), jnp.arange(rows * top), side="right").astype(jnp.int32)
    grid = items.reshape(top, rows).T
    grid = grid[jax.random.permutation(jax.random.fold_in(own, 1), rows)]
    rotation = jax.random.randint(jax.random.fold_in(own, 2), (rows, 1), 0, top)
    return jnp.take_along_axis(grid, (jnp.arange(top)[None, :] + rotation) % top, axis=1)


def load_shares(number_of, total, reach, slope, full):
    portions = [(1 << 20) // math.isqrt(rank ** slope) + 1 for rank in range(1, number_of + 1)]
    largest = reach if full else min(reach, max(-(-total // number_of), total * portions[0] // sum(portions)))
    least = 1 if total - largest >= number_of - 1 else 0
    holding, rest = [largest] + [least] * (number_of - 1), total - largest - least * (number_of - 1)
    while rest > 0:
        candidates = [i for i in range(1, number_of) if holding[i] < largest] or [i for i in range(1, number_of) if holding[i] < reach]
        mass, remaining = sum([portions[i] for i in candidates]), rest
        for i in candidates:
            addition = min(reach - holding[i], max(1, remaining * portions[i] // mass), rest)
            holding[i] = holding[i] + addition
            rest = rest - addition
    return np.array(holding)


def scatter_about(key, extent, spread, bound, cuts=(), kind=jnp.bfloat16):
    array = spread * jax.random.normal(key, extent, jnp.float32)
    if cuts:
        array = array * levels(key, extent, cuts, -0.22, 0.18)
    return jnp.clip(array, -bound, bound).astype(kind)


def setup_inputs(seed: int = 0) -> dict:
    key_list = jax.random.split(jax.random.key(seed), 14)
    tokens = scatter_about(key_list[0], (TOKENS, D), 1.0, 6.0, ((0, 128),))
    cotangent = scatter_about(key_list[1], (TOKENS, D), 1.0, 6.0, ((0, 128),))
    block_order = jax.random.permutation(key_list[2], N_CTX).astype(jnp.int32)
    routes_keys = jax.random.split(jax.random.fold_in(key_list[3], 1), TOKENS // TOK_DEV)
    routes_turns = jax.random.permutation(jax.random.fold_in(key_list[3], 3), TOKENS // TOK_DEV)
    routes = jax.vmap(lambda own, number: shared_out(jax.random.fold_in(key_list[3], 2), own, number, TOK_DEV, EXPERTS, TOP, MOST, 1))(routes_keys, routes_turns).reshape((TOKENS, TOP))
    norm_one = jnp.clip(1.0 + 0.18 * jax.random.normal(key_list[4], (D,), jnp.float32), 0.099609375, 1.8984375).astype(jnp.bfloat16)
    w_query = scatter_about(key_list[5], (D, HEADS * HEAD_DIM), D ** -0.5, 0.1875, ((0, 128),))
    w_key = scatter_about(key_list[6], (D, KV_HEADS * HEAD_DIM), D ** -0.5, 0.1875, ((0, 128),))
    w_value = scatter_about(key_list[7], (D, KV_HEADS * HEAD_DIM), D ** -0.5, 0.1875, ((0, 128),))
    w_out = scatter_about(key_list[8], (HEADS * HEAD_DIM, D), (max(1, 8 * D // SEQ)) ** -0.5, 3.0, ((0, 128),))
    norm_two = jnp.clip(1.0 + 0.18 * jax.random.normal(key_list[9], (D,), jnp.float32), 0.099609375, 1.8984375).astype(jnp.bfloat16)
    w_router = scatter_about(key_list[10], (D, EXPERTS), (4 * D) ** -0.5, 0.09375, ((0, 128),))
    expert_in = scatter_about(key_list[11], (EXPERTS, D, 2 * FF), D ** -0.5, 0.1875, ((0, 16), (1, 8)))
    expert_out = scatter_about(key_list[12], (EXPERTS, FF, D), (FF // 16) ** -0.5, 1.0, ((0, 16), (2, 8)))
    return dict(tokens=tokens, cotangent=cotangent, block_order=block_order, routes=routes, norm_one=norm_one, w_query=w_query, w_key=w_key, w_value=w_value, w_out=w_out, norm_two=norm_two, w_router=w_router, expert_in=expert_in, expert_out=expert_out)


@jax.custom_vjp
def low(v):
    return lax.optimization_barrier(v.astype(jnp.bfloat16)).astype(jnp.float32)

@jax.custom_vjp
def low_back(v):
    return v

def low_keep(v):
    return (low(v), None)

def low_pass(kept, grad):
    return (grad,)

def back_keep(v):
    return (v, None)

def back_low(kept, grad):
    return (low(grad),)
low.defvjp(low_keep, low_pass)
low_back.defvjp(back_keep, back_low)
epsilon = 1e-06
highest = lax.Precision.HIGHEST

def product(left_operand, right_operand):
    return jnp.dot(left_operand, right_operand, precision=highest, preferred_element_type=jnp.float32)

def rotary(values, places, direction):
    half_dim = values.shape[-1] // 2
    inverse = 10000.0 ** (-jnp.arange(half_dim, dtype=jnp.float32) * 2.0 / values.shape[-1])
    angles = places.astype(jnp.float32)[:, None] * inverse[None, :]
    cosine = jnp.cos(angles)[:, None, :]
    sine_part = direction * jnp.sin(angles)[:, None, :]
    front_half = values[..., :half_dim]
    back_half = values[..., half_dim:]
    return jnp.concatenate([front_half * cosine - back_half * sine_part, back_half * cosine + front_half * sine_part], axis=-1)

def layout_positions(block_order, ctx_count, half_rows):
    front_block = block_order.astype(jnp.int32)
    block_pair = jnp.stack([front_block, 2 * ctx_count - 1 - front_block], axis=1)
    within = jnp.arange(half_rows, dtype=jnp.int32)
    return (block_pair[:, :, None] * half_rows + within[None, None, :]).reshape(-1).astype(jnp.int32)

def slot_destination(routes_seq):
    per_device = routes_seq.reshape(N_CTX, TOK_DEV * TOP)
    onehot = (per_device[:, :, None] == jnp.arange(EXPERTS, dtype=jnp.int32)[None, None, :]).astype(jnp.int32)
    before = (jnp.cumsum(onehot, axis=1) - onehot).astype(jnp.int32)
    slot_index = lax.optimization_barrier(jnp.sum(before * onehot, axis=2)).astype(jnp.int32)
    device_index = jnp.arange(N_CTX, dtype=jnp.int32)[:, None]
    return (per_device * (N_CTX * MOST) + device_index * MOST + slot_index).reshape(-1).astype(jnp.int32)

def attend(query_block, query_places, key_rot, values, places):
    scores = jnp.einsum('tgrd,sgd->tgrs', query_block, key_rot, precision=highest) / math.sqrt(HEAD_DIM)
    scores = low_back(scores)
    allowed = (places[None, :] <= query_places[:, None])[:, None, None, :]
    masked = jnp.where(allowed, scores, -1e+30)
    row_max = lax.optimization_barrier(jnp.max(masked, axis=-1, keepdims=True))
    weights = jnp.where(allowed, jnp.exp(masked - row_max), 0.0)
    probabilities = weights / lax.optimization_barrier(jnp.sum(weights, axis=-1, keepdims=True))
    return jnp.einsum('tgrs,sgd->tgrd', low(probabilities), values, precision=highest)

def expert_layer(expert_rows, weight_in, weight_out):
    gate_up = product(expert_rows, weight_in)
    gate_part = low_back(gate_up[:, :FF])
    up_part = low_back(gate_up[:, FF:])
    hidden = low(jax.nn.silu(gate_part) * up_part)
    return low_back(low(product(hidden, weight_out)))

def sequence_layer(parameters, tokens_seq, routes_seq, places):
    norm_one, w_query, w_key, w_value, w_out, norm_two, w_router, expert_in, expert_out = parameters
    group_size = HEADS // KV_HEADS
    scale_one = lax.rsqrt(lax.optimization_barrier(jnp.mean(tokens_seq * tokens_seq, axis=-1, keepdims=True)) + epsilon)
    hidden_one = low(tokens_seq * scale_one * norm_one)
    query_flat = low_back(product(hidden_one, w_query)).reshape(SEQ, HEADS, HEAD_DIM)
    key_flat = low_back(product(hidden_one, w_key)).reshape(SEQ, KV_HEADS, HEAD_DIM)
    values = low_back(low(product(hidden_one, w_value))).reshape(SEQ, KV_HEADS, HEAD_DIM)
    query_rot = low(rotary(query_flat, places, 1.0)).reshape(SEQ, KV_HEADS, group_size, HEAD_DIM)
    key_rot = low(rotary(key_flat, places, 1.0))
    block_rows = math.gcd(SEQ, 512)

    def query_step(pieces):
        return jax.checkpoint(attend)(pieces[0], pieces[1], key_rot, values, places)
    attended = lax.map(query_step, (query_rot.reshape(SEQ // block_rows, block_rows, KV_HEADS, group_size, HEAD_DIM), places.reshape(SEQ // block_rows, block_rows)))
    attended = low_back(low(attended.reshape(SEQ, HEADS * HEAD_DIM)))
    residual = tokens_seq + low_back(product(attended, w_out))
    scale_two = lax.rsqrt(lax.optimization_barrier(jnp.mean(residual * residual, axis=-1, keepdims=True)) + epsilon)
    hidden_two = low(residual * scale_two * norm_two)
    logits = low_back(product(hidden_two, w_router))
    picked = jnp.take_along_axis(logits, routes_seq, axis=1)
    gate_weights = jax.nn.softmax(picked, axis=-1)
    destination = slot_destination(routes_seq)
    entries = jnp.arange(destination.shape[0], dtype=jnp.int32)
    slot_source = jnp.zeros((EXPERTS * N_CTX * MOST,), jnp.int32).at[destination].set(entries)
    filled = jnp.zeros((EXPERTS * N_CTX * MOST,), jnp.float32).at[destination].set(1.0)
    expert_rows = low_back(jnp.take(hidden_two, slot_source // TOP, axis=0) * filled[:, None])
    expert_rows = expert_rows.reshape(EXPERTS, N_CTX * MOST, D)

    def expert_step(pieces):
        return jax.checkpoint(expert_layer)(pieces[0], pieces[1], pieces[2])
    results = lax.map(expert_step, (expert_rows, expert_in, expert_out)).reshape(EXPERTS * N_CTX * MOST, D)
    picked_rows = jnp.take(results, destination, axis=0).reshape(SEQ, TOP, D)
    return residual + lax.optimization_barrier(jnp.sum(gate_weights[:, :, None] * picked_rows, axis=1))

def reference(tokens, cotangent, block_order, routes, norm_one, w_query, w_key, w_value, w_out, norm_two, w_router, expert_in, expert_out):
    places = layout_positions(block_order, N_CTX, TOK_DEV // 2)
    routes_all = routes.reshape(N_DP, SEQ, TOP)

    def forward(tokens_full, *parameters):

        def single(pieces):
            return jax.checkpoint(sequence_layer)(parameters, pieces[0], pieces[1], places)
        outputs = lax.map(single, (tokens_full.reshape(N_DP, SEQ, D), routes_all))
        return outputs.reshape(N_DP * SEQ, D)
    parameters = tuple((weight.astype(jnp.float32) for weight in (norm_one, w_query, w_key, w_value, w_out, norm_two, w_router, expert_in, expert_out)))
    output, pullback = jax.vjp(forward, tokens.astype(jnp.float32), *parameters)
    gradients = pullback(cotangent.astype(jnp.float32))
    return (output, gradients[0], gradients[1], gradients[2], gradients[3], gradients[4], gradients[5], gradients[6], gradients[7], gradients[8], gradients[9])
```

```python
import functools
import math

import jax
import jax.numpy as jnp
import numpy as np
from jax import lax
from jax.experimental import pallas as pl
from jax.experimental.pallas import tpu as pltpu
from jax.sharding import Mesh
from jax.sharding import PartitionSpec as P

D = 1024
HEADS = 16
KV_HEADS = 8
HEAD_DIM = 64
EXPERTS = 32
FF = 512
TOP = 8
MOST = 48
ROWS = 128
SEQ = 2048
BLOCK = 64
AXES = ("ylo", "z", "yhi", "x", "core")
DP = ("ylo", "z")
CTX = ("yhi", "x", "core")
N_DP = 8
N_CTX = 16
EXTRA = 128
MESH_ID = pl.DeviceIdType.MESH
ANY = pl.BlockSpec(memory_space=pl.ANY)
VMEM = pl.BlockSpec(memory_space=pltpu.VMEM)
SMEM = pl.BlockSpec(memory_space=pltpu.SMEM)
DMA = pltpu.SemaphoreType.DMA
bf16 = jnp.bfloat16
f32 = jnp.float32
epsilon = 1e-06
CHIPS = [(0, 1), (1, 0), (0, 3), (1, 1), (1, 3), (0, 2), (1, 2)]


def dot(a, b):
    return jnp.dot(a, b, preferred_element_type=f32)


def dot_last(a, b):
    return lax.dot_general(a, b, (((1,), (1,)), ((), ())), preferred_element_type=f32)


def dot_first(a, b):
    return lax.dot_general(a, b, (((0,), (0,)), ((), ())), preferred_element_type=f32)


def my_place():
    return tuple(lax.axis_index(a) for a in AXES)


def device_at(dp, ctx):
    return (
        lax.div(dp, 4),
        lax.rem(dp, 4),
        lax.div(ctx, 8),
        lax.rem(lax.div(ctx, 2), 4),
        lax.rem(ctx, 2),
    )


def chip_peer(place, n):
    ylo, z, yhi, x, core = place
    dy, dx = CHIPS[n]
    return (ylo, z, lax.rem(yhi + dy, 2), lax.rem(x + dx, 4), core)


def chip_from(place, n):
    ylo, z, yhi, x, core = place
    dy, dx = CHIPS[n]
    return (ylo, z, lax.rem(yhi + dy, 2), lax.rem(x + 4 - dx, 4), core)


def ctx_of(place):
    return place[2] * 8 + place[3] * 2 + place[4]


def dp_of(place):
    return place[0] * 4 + place[1]


def sibling_of(place):
    return place[:4] + (1 - place[4],)


def remote(src, dst, send, recv, device):
    return pltpu.make_async_remote_copy(
        src_ref=src, dst_ref=dst, send_sem=send, recv_sem=recv, device_id=device, device_id_type=MESH_ID
    )


def greet(devices):
    barrier = pltpu.get_barrier_semaphore()
    for device in devices:
        pl.semaphore_signal(barrier, inc=1, device_id=device, device_id_type=MESH_ID)
    return barrier


class RowGather:
    scratch = [DMA, DMA((8,)), DMA((8,)), DMA((7,)), DMA((7,))]

    def __init__(self, place, x_ref, out_ref, local, send, recv, fsend, frecv):
        me = ctx_of(place)
        sibling = sibling_of(place)
        self.own = pltpu.make_async_copy(x_ref, out_ref.at[me], local)
        self.out = [
            remote(x_ref, out_ref.at[me], send.at[n], recv.at[n], chip_peer(place, n)) for n in range(7)
        ]
        self.out.append(remote(x_ref, out_ref.at[me], send.at[7], recv.at[7], sibling))
        self.forward = []
        for n in range(7):
            piece = out_ref.at[ctx_of(chip_from(place, n))]
            self.forward.append(remote(piece, piece, fsend.at[n], frecv.at[n], sibling))

    def start(self):
        for copy in self.out:
            copy.start()
        self.own.start()

    def pass_on(self):
        for n in range(7):
            self.out[n].wait_recv()
            self.forward[n].start()

    def finish(self):
        self.own.wait()
        self.out[7].wait_recv()
        for n in range(7):
            self.forward[n].wait_recv()
        for copy in self.out + self.forward:
            copy.wait_send()


def greet_chips(place):
    barrier = greet([chip_peer(place, n) for n in range(7)] + [sibling_of(place)])
    pl.semaphore_wait(barrier, 8)


def gather_kernel(x_ref, out_ref, *sems):
    place = my_place()
    greet_chips(place)
    gather = RowGather(place, x_ref, out_ref, *sems)
    gather.start()
    gather.pass_on()
    gather.finish()


def gather_ctx(x, number):
    return pl.pallas_call(
        gather_kernel,
        out_shape=jax.ShapeDtypeStruct((N_CTX,) + x.shape, x.dtype),
        in_specs=[ANY],
        out_specs=ANY,
        scratch_shapes=RowGather.scratch,
        compiler_params=pltpu.CompilerParams(collective_id=number, has_side_effects=True),
        name="gather_rows",
    )(x)


def scatter_kernel(p_ref, out_ref, own, other, landed, own_sem, send, recv, csend, crecv):
    place = my_place()
    core = place[4]
    sibling = sibling_of(place)
    greet_chips(place)
    mine, cross = [], []
    for n in range(8):
        chip = lax.div(ctx_of(chip_peer(place, n) if n < 7 else place), 2)
        mine.append(pltpu.make_async_copy(p_ref.at[chip, core], own.at[n], own_sem.at[n]))
        cross.append(remote(p_ref.at[chip, 1 - core], other.at[n], send.at[n], recv.at[n], sibling))
    for n in range(8):
        cross[n].start()
        mine[n].start()
    out = []
    for n in range(7):
        mine[n].wait()
        cross[n].wait_recv()
        own[n] = (own[n].astype(f32) + other[n].astype(f32)).astype(bf16)
        copy = remote(own.at[n], landed.at[n], csend.at[n], crecv.at[n], chip_peer(place, n))
        copy.start()
        out.append(copy)
    mine[7].wait()
    cross[7].wait_recv()
    out_ref[...] = own[7].astype(f32) + other[7].astype(f32)
    for n in range(7):
        out[n].wait_recv()
        out_ref[...] += landed[n].astype(f32)
    for n in range(7):
        out[n].wait_send()
    for n in range(8):
        cross[n].wait_send()


def scatter_ctx(parts, number):
    rows, width = parts.shape[-2:]
    parts = parts.reshape(8, 2, rows, width)
    return pl.pallas_call(
        scatter_kernel,
        out_shape=jax.ShapeDtypeStruct((rows, width), f32),
        in_specs=[ANY],
        out_specs=VMEM,
        scratch_shapes=[
            pltpu.VMEM((8, rows, width), bf16),
            pltpu.VMEM((8, rows, width), bf16),
            pltpu.VMEM((7, rows, width), bf16),
            DMA((8,)),
            DMA((8,)),
            DMA((8,)),
            DMA((7,)),
            DMA((7,)),
        ],
        compiler_params=pltpu.CompilerParams(
            collective_id=number, has_side_effects=True, vmem_limit_bytes=24 * 2**20
        ),
        name="scatter_rows",
    )(parts)


def entry_kernel(x_ref, w_ref, o_ref, x_out, w_out, o_out, *sems):
    row_sems, rest = sems[:5], sems[5:]
    wlocal, wsend, wrecv, psend, precv, olocal, osend, orecv = rest
    place = my_place()
    dp, ctx = dp_of(place), ctx_of(place)
    barrier = greet(
        [device_at(dp, lax.rem(ctx + k, N_CTX)) for k in range(1, N_CTX)]
        + [device_at(lax.rem(dp + k, N_DP), ctx) for k in range(1, N_DP)]
    )
    o_ctx = 2 * dp + lax.div(ctx, 8)
    o_home = lax.div(ctx, 2)
    from_ctx = 8 * lax.rem(ctx, 2)
    o_self = o_ctx == ctx
    for t in range(8):
        here = jnp.logical_and(o_home == dp, from_ctx + t == ctx)

        @pl.when(jnp.logical_not(here))
        def _():
            pl.semaphore_signal(
                barrier, inc=1, device_id=device_at(o_home, from_ctx + t), device_id_type=MESH_ID
            )

    pl.semaphore_wait(barrier, 30 - jnp.where(o_self, 1, 0))

    first = []
    for k in range(1, N_CTX):
        to = lax.rem(ctx + k, N_CTX)
        first.append(
            remote(w_ref.at[to], w_out.at[dp, ctx], wsend.at[k], wrecv.at[k], device_at(dp, to))
        )
    for copy in first:
        copy.start()
    own = pltpu.make_async_copy(w_ref.at[ctx], w_out.at[dp, ctx], wlocal)
    own.start()
    rows = RowGather(place, x_ref, x_out, *row_sems)
    rows.start()
    slot = lax.rem(ctx, 8)
    o_own = pltpu.make_async_copy(o_ref, o_out.at[slot], olocal)

    def o_copy(k):
        return remote(o_ref, o_out.at[slot], osend.at[k], orecv.at[slot], device_at(k, o_ctx))

    for k in range(8):
        here = jnp.logical_and(o_self, dp == k)

        @pl.when(here)
        def _():
            o_own.start()

        @pl.when(jnp.logical_not(here))
        def _():
            o_copy(k).start()

    own.wait()
    for copy in first:
        copy.wait_recv()
    second = []
    for k in range(1, N_DP):
        to = lax.rem(dp + k, N_DP)
        second.append(remote(w_out.at[dp], w_out.at[dp], psend.at[k], precv.at[k], device_at(to, ctx)))
    for copy in second:
        copy.start()
    rows.pass_on()
    rows.finish()
    for copy in second:
        copy.wait_recv()
    for t in range(8):
        here = jnp.logical_and(o_home == dp, from_ctx + t == ctx)

        @pl.when(jnp.logical_not(here))
        def _():
            remote(o_ref, o_out.at[t], osend.at[0], orecv.at[t], device_at(dp, ctx)).wait_recv()

    for k in range(8):
        here = jnp.logical_and(o_self, dp == k)

        @pl.when(here)
        def _():
            o_own.wait()

        @pl.when(jnp.logical_not(here))
        def _():
            o_copy(k).wait_send()

    for copy in first + second:
        copy.wait_send()


def entry(x, w, o, number):
    return pl.pallas_call(
        entry_kernel,
        out_shape=(
            jax.ShapeDtypeStruct((N_CTX,) + x.shape, x.dtype),
            jax.ShapeDtypeStruct((N_DP,) + w.shape, w.dtype),
            jax.ShapeDtypeStruct((8,) + o.shape, o.dtype),
        ),
        in_specs=[ANY] * 3,
        out_specs=(ANY, ANY, ANY),
        scratch_shapes=RowGather.scratch
        + [DMA, DMA((16,)), DMA((16,)), DMA((8,)), DMA((8,)), DMA, DMA((8,)), DMA((8,))],
        compiler_params=pltpu.CompilerParams(collective_id=number, has_side_effects=True),
        name="entry_gather",
    )(x, w, o)


def grads_kernel(
    a_ref, b_ref, a_out, b_out, landed, part, wlocal, wsend, wrecv, psend, precv, olocal, osend, orecv, plocal
):
    place = my_place()
    dp, ctx = dp_of(place), ctx_of(place)
    barrier = greet(
        [device_at(dp, lax.rem(ctx + k, N_CTX)) for k in range(1, N_CTX)]
        + [device_at(lax.rem(dp + k, N_DP), ctx) for k in range(1, N_DP)]
    )
    o_ctx = 2 * dp + lax.div(ctx, 8)
    o_home = lax.div(ctx, 2)
    to_ctx = 8 * lax.rem(ctx, 2)
    o_self = o_ctx == ctx
    for k in range(8):
        here = jnp.logical_and(o_self, dp == k)

        @pl.when(jnp.logical_not(here))
        def _():
            pl.semaphore_signal(barrier, inc=1, device_id=device_at(k, o_ctx), device_id_type=MESH_ID)

    pl.semaphore_wait(barrier, 30 - jnp.where(o_self, 1, 0))

    first = []
    for k in range(1, N_DP):
        to = lax.rem(dp + k, N_DP)
        first.append(remote(a_ref.at[to], landed.at[k], wsend.at[k], wrecv.at[k], device_at(to, ctx)))
    for copy in first:
        copy.start()
    own = pltpu.make_async_copy(a_ref.at[dp], landed.at[0], wlocal)
    own.start()

    def o_copy(t):
        return remote(
            b_ref.at[t], b_out.at[dp], osend.at[t], orecv.at[dp], device_at(o_home, to_ctx + t)
        )

    o_own = pltpu.make_async_copy(b_ref.at[lax.rem(ctx, 8)], b_out.at[dp], olocal)
    for t in range(8):
        here = jnp.logical_and(o_home == dp, to_ctx + t == ctx)

        @pl.when(here)
        def _():
            o_own.start()

        @pl.when(jnp.logical_not(here))
        def _():
            o_copy(t).start()

    own.wait()
    total = landed[0].astype(f32)
    for copy in first:
        copy.wait_recv()
    for k in range(1, N_DP):
        total = total + landed[k].astype(f32)
    part[...] = total.reshape(part.shape)
    second = []
    for k in range(1, N_CTX):
        to = lax.rem(ctx + k, N_CTX)
        second.append(remote(part.at[to], a_out.at[ctx], psend.at[k], precv.at[k], device_at(dp, to)))
    for copy in second:
        copy.start()
    mine = pltpu.make_async_copy(part.at[ctx], a_out.at[ctx], plocal)
    mine.start()
    mine.wait()
    for copy in second:
        copy.wait_recv()
    for k in range(8):
        here = jnp.logical_and(o_self, dp == k)

        @pl.when(here)
        def _():
            o_own.wait()

        @pl.when(jnp.logical_not(here))
        def _():
            remote(b_ref.at[0], b_out.at[k], osend.at[0], orecv.at[k], device_at(dp, ctx)).wait_recv()

    for t in range(8):
        here = jnp.logical_and(o_home == dp, to_ctx + t == ctx)

        @pl.when(jnp.logical_not(here))
        def _():
            o_copy(t).wait_send()

    for copy in first + second:
        copy.wait_send()


def grads_out(a, b, number):
    width = a.shape[-1]
    return pl.pallas_call(
        grads_kernel,
        out_shape=(
            jax.ShapeDtypeStruct((N_CTX, 8, width), f32),
            jax.ShapeDtypeStruct((N_DP,) + b.shape[1:], f32),
        ),
        in_specs=[ANY] * 2,
        out_specs=(VMEM, VMEM),
        scratch_shapes=[pltpu.VMEM(a.shape, a.dtype), pltpu.VMEM((N_CTX, 8, width), f32)]
        + [DMA, DMA((8,)), DMA((8,)), DMA((16,)), DMA((16,)), DMA, DMA((8,)), DMA((8,)), DMA],
        compiler_params=pltpu.CompilerParams(
            collective_id=number, has_side_effects=True, vmem_limit_bytes=24 * 2**20
        ),
        name="sum_grads",
    )(a, b)


def swap_halves(u):
    lane = lax.broadcasted_iota(jnp.int32, u.shape, 1)
    return jnp.where(lax.rem(lane, 64) < 32, pltpu.roll(u, 96, 1), pltpu.roll(u, 32, 1))


def attend_kernel(src, order, raw_ref, cos_ref, sin_ref, o_ref, q_ref, k_ref, v_ref, lse_ref, out_nat):
    for b in range(SEQ // BLOCK):
        rows = pl.ds(pl.multiple_of(src[b] * BLOCK, BLOCK), BLOCK)
        here = pl.ds(b * BLOCK, BLOCK)
        qk = raw_ref[rows, 0:128]
        qk = qk * cos_ref[here, :] + swap_halves(qk) * sin_ref[here, :]
        q_ref[here, :] = (qk[:, 0:64]).astype(bf16)
        k_ref[here, :] = (qk[:, 64:128]).astype(bf16)
        v_ref[here, :] = raw_ref[rows, 128:192].astype(bf16)
    step = 256
    for i in range(SEQ // step):
        length = (i + 1) * step
        here = pl.ds(i * step, step)
        scores = dot_last(q_ref[here, :], k_ref[0:length, :]) * 0.125
        row = i * step + lax.broadcasted_iota(jnp.int32, (step, length), 0)
        column = lax.broadcasted_iota(jnp.int32, (step, length), 1)
        scores = jnp.where(column <= row, scores, -1e30)
        top = jnp.max(scores, axis=1, keepdims=True)
        weights = jnp.exp(scores - top)
        total = jnp.sum(weights, axis=1, keepdims=True)
        lse_ref[here, :] = top + jnp.log(total)
        probs = (weights * (1.0 / total)).astype(bf16)
        out_nat[here, :] = dot(probs, v_ref[0:length, :])
    for b in range(SEQ // BLOCK):
        rows = pl.ds(pl.multiple_of(order[b] * BLOCK, BLOCK), BLOCK)
        o_ref[pl.ds(b * BLOCK, BLOCK), :] = out_nat[rows, :].astype(bf16)


def attend(src, order, raw, cosine, sine):
    head = jax.ShapeDtypeStruct((SEQ, HEAD_DIM), bf16)
    return pl.pallas_call(
        attend_kernel,
        out_shape=(head, head, head, head, jax.ShapeDtypeStruct((SEQ, 1), f32)),
        in_specs=[SMEM, SMEM, VMEM, VMEM, VMEM],
        out_specs=(VMEM,) * 5,
        scratch_shapes=[pltpu.VMEM((SEQ, HEAD_DIM), f32)],
        compiler_params=pltpu.CompilerParams(vmem_limit_bytes=48 * 2**20),
        cost_estimate=pl.CostEstimate(flops=10**9, bytes_accessed=6 * 2**20, transcendentals=2**21),
        name="attention_forward",
    )(src, order, raw, cosine, sine)


def attend_back_kernel(
    src, order, q_ref, k_ref, v_ref, lse_ref, do_ref, cos_ref, sin_ref, out_ref, do_nat, acc, done
):
    for b in range(SEQ // BLOCK):
        rows = pl.ds(pl.multiple_of(src[b] * BLOCK, BLOCK), BLOCK)
        do_nat[pl.ds(b * BLOCK, BLOCK), :] = do_ref[rows, :]
    acc[...] = jnp.zeros_like(acc)
    step = 256
    for i in range(SEQ // step):
        length = (i + 1) * step
        here = pl.ds(i * step, step)
        query, d_out = q_ref[here, :], do_nat[here, :].astype(bf16)
        keys = k_ref[0:length, :]
        scores = dot_last(query, keys) * 0.125
        row = i * step + lax.broadcasted_iota(jnp.int32, (step, length), 0)
        column = lax.broadcasted_iota(jnp.int32, (step, length), 1)
        probs = jnp.where(column <= row, jnp.exp(scores - lse_ref[here, :]), 0.0)
        d_probs = dot_last(d_out, v_ref[0:length, :])
        delta = jnp.sum(probs * d_probs, axis=1, keepdims=True)
        d_scores = (probs * (d_probs - delta)).astype(bf16)
        acc[here, 0:64] = dot(d_scores, keys) * 0.125
        acc[0:length, 64:128] += dot_first(d_scores, query) * 0.125
        acc[0:length, 128:192] += dot_first(probs.astype(bf16), d_out)
    for b in range(SEQ // BLOCK):
        here = pl.ds(b * BLOCK, BLOCK)
        qk = acc[here, 0:128]
        qk = qk * cos_ref[here, :] - swap_halves(qk) * sin_ref[here, :]
        done[here, 0:128] = qk
        done[here, 128:256] = acc[here, 128:256]
    for b in range(SEQ // BLOCK):
        rows = pl.ds(pl.multiple_of(order[b] * BLOCK, BLOCK), BLOCK)
        out_ref[pl.ds(b * BLOCK, BLOCK), :] = done[rows, :].astype(bf16)


def attend_back(src, order, q, k, v, lse, d_out, cosine, sine):
    return pl.pallas_call(
        attend_back_kernel,
        out_shape=jax.ShapeDtypeStruct((SEQ, 256), bf16),
        in_specs=[SMEM, SMEM] + [VMEM] * 7,
        out_specs=VMEM,
        scratch_shapes=[
            pltpu.VMEM((SEQ, HEAD_DIM), f32),
            pltpu.VMEM((SEQ, 256), f32),
            pltpu.VMEM((SEQ, 256), f32),
        ],
        compiler_params=pltpu.CompilerParams(vmem_limit_bytes=56 * 2**20),
        cost_estimate=pl.CostEstimate(flops=3 * 10**9, bytes_accessed=6 * 2**20, transcendentals=2**21),
        name="attention_backward",
    )(src, order, q, k, v, lse, d_out, cosine, sine)


def rotary_tables():
    inverse = 10000.0 ** (-np.arange(32, dtype=np.float64) * 2.0 / HEAD_DIM)
    angles = np.arange(SEQ, dtype=np.float64)[:, None] * inverse[None, :]
    cosine, sine = np.cos(angles), np.sin(angles)
    return (
        np.tile(cosine, (1, 4)).astype(np.float32),
        np.concatenate([-sine, sine, -sine, sine], axis=1).astype(np.float32),
    )


def normalize(inputs, gain_values):
    scale_rows = lax.rsqrt(jnp.mean(inputs * inputs, axis=-1, keepdims=True) + epsilon)
    normed = inputs * scale_rows
    return (scale_rows, normed, (normed * gain_values.astype(f32)).astype(bf16))


def norm_backward(grad_in, normed, scale_rows, gain_values):
    grad_normed = grad_in * gain_values.astype(f32)
    inner = jnp.mean(grad_normed * normed, axis=-1, keepdims=True)
    return (scale_rows * (grad_normed - normed * inner), jnp.sum(grad_in * normed, axis=0))


def halves(value):
    high = lax.reduce_precision(value, 8, 7)
    return high.astype(bf16), (value - high).astype(bf16)


def local(
    tokens,
    cotangent,
    block_order,
    routes,
    norm_one,
    w_query,
    w_key,
    w_value,
    w_out,
    norm_two,
    w_router,
    expert_in,
    expert_out,
):
    ctx = lax.axis_index(CTX)
    cosine, sine = (jnp.asarray(t) for t in rotary_tables())
    order = jnp.stack([block_order, 2 * N_CTX - 1 - block_order], axis=1).reshape(-1)
    spots = jnp.arange(2 * N_CTX, dtype=jnp.int32)
    src = jnp.sum(jnp.where(order[None, :] == spots[:, None], spots[None, :], 0), axis=1)

    by_head = lambda w, heads: jnp.moveaxis(w.reshape(8, heads, HEAD_DIM), 1, 0)
    query_part = by_head(w_query, HEADS)
    key_part = jnp.repeat(by_head(w_key, KV_HEADS), 2, axis=0)
    value_part = jnp.repeat(by_head(w_value, KV_HEADS), 2, axis=0)
    small = jnp.concatenate(
        [w_router, norm_one[:, None], norm_two[:, None], jnp.zeros((8, 30), bf16)], axis=1
    )
    small = jnp.broadcast_to(small[None], (N_CTX, 8, 64))
    packed = jnp.concatenate(
        [
            jnp.concatenate([query_part, key_part], axis=2),
            jnp.concatenate([value_part, small], axis=2),
        ],
        axis=1,
    )
    tokens_all, packed_all, out_all = entry(tokens, packed, w_out.reshape(16, 512), 0)
    expert_in_all = lax.all_gather(expert_in, DP, axis=0)
    expert_out_all = lax.all_gather(expert_out, DP, axis=0)
    cotangent_all = lax.all_gather(cotangent, CTX, axis=0)
    low = packed_all[:, :, 8:, :].reshape(D, 128)
    weight = jnp.concatenate(
        [packed_all[:, :, :8, :].reshape(D, 128), low[:, :64], jnp.zeros((D, 64), bf16)], axis=1
    )
    router_weight, gain_one, gain_two = low[:, 64:96], low[:, 96], low[:, 97]
    out_weight = out_all.reshape(HEAD_DIM, D)

    tokens_float = tokens.astype(f32)
    scale_one, normed_one, _ = normalize(tokens_float, gain_one)
    _, _, hidden_one = normalize(tokens_all.reshape(SEQ, D).astype(f32), gain_one)
    raw = dot(hidden_one, weight)
    attended, query, key, value, lse = attend(src, order, raw, cosine, sine)
    partial = dot(attended, out_weight).astype(bf16).reshape(N_CTX, ROWS, D)
    residual = tokens_float + scatter_ctx(partial, 1)
    scale_two, normed_two, hidden_two = normalize(residual, gain_two)

    logits = dot(hidden_two, router_weight)
    names = jnp.arange(EXPERTS, dtype=jnp.int32)
    member = jnp.any(routes[:, :, None] == names[None, None, :], axis=1)
    picked = jnp.where(member, logits, -1e30)
    shifted = jnp.where(member, jnp.exp(picked - jnp.max(picked, axis=1, keepdims=True)), 0.0)
    gates = shifted / jnp.sum(shifted, axis=1, keepdims=True)
    high, rest = halves(gates)
    sent = jnp.concatenate(
        [hidden_two, high, rest, member.astype(bf16), jnp.zeros((ROWS, EXTRA - 96), bf16)], axis=1
    )
    all_two = gather_ctx(sent, 2)

    hidden_all = all_two[:, :, :D]
    pair = lambda at: lax.dynamic_slice_in_dim(all_two, D + at + 2 * ctx, 2, axis=2)
    gate_all = pair(0).astype(f32) + pair(32).astype(f32)
    member_all = pair(64)
    triangle = jnp.tril(jnp.ones((ROWS, ROWS), bf16), -1)
    slot = jnp.einsum("rt,cte->cer", triangle, member_all, preferred_element_type=f32)
    turned = jnp.moveaxis(member_all, 2, 1)
    onehot = jnp.where(
        slot[:, :, None, :] == jnp.arange(MOST, dtype=f32)[None, None, :, None],
        turned[:, :, None, :],
        jnp.zeros((), bf16),
    )
    expert_rows = jnp.einsum("cesr,crd->ecsd", onehot, hidden_all, preferred_element_type=f32).astype(bf16)
    expert_rows = expert_rows.reshape(2, N_CTX * MOST, D)
    d_rows_top = jnp.einsum("cesr,crd->ecsd", onehot, cotangent_all, preferred_element_type=f32)
    d_rows_top = d_rows_top.reshape(2, N_CTX * MOST, D)
    gate_slot = jnp.einsum("cesr,cre->ecs", onehot.astype(f32), gate_all, precision="highest")
    gate_slot = gate_slot.reshape(2, N_CTX * MOST, 1)
    in_weight = jnp.moveaxis(expert_in_all, 0, 1).reshape(2, D, 2 * FF)
    down_weight = jnp.moveaxis(expert_out_all, 0, 2).reshape(2, FF, D)
    gate_up = jnp.einsum("esd,edf->esf", expert_rows, in_weight, preferred_element_type=f32)
    gate_part, up_part = gate_up[..., :FF], gate_up[..., FF:]
    expert_hidden = (jax.nn.silu(gate_part) * up_part).astype(bf16)
    expert_result = jnp.einsum("esf,efd->esd", expert_hidden, down_weight, preferred_element_type=f32)
    expert_result = expert_result.astype(bf16).astype(f32)
    d_gate_slot = jnp.sum(d_rows_top * expert_result, axis=-1)
    weighted = (expert_result * gate_slot).astype(bf16).reshape(2, N_CTX, MOST, D)
    out_part = jnp.einsum("cesr,ecsd->crd", onehot, weighted, preferred_element_type=f32).astype(bf16)
    output = residual + scatter_ctx(out_part, 3)
    d_result = (d_rows_top * gate_slot).astype(bf16)
    d_hidden = jnp.einsum("esd,efd->esf", d_result, down_weight, preferred_element_type=f32)
    grad_down = jnp.einsum("esf,esd->efd", expert_hidden, d_result, preferred_element_type=f32)
    sigmoid_gate = jax.nn.sigmoid(gate_part)
    d_gate = d_hidden * up_part * (sigmoid_gate * (1.0 + gate_part * (1.0 - sigmoid_gate)))
    d_up = d_hidden * jax.nn.silu(gate_part)
    d_gate_up = jnp.concatenate([d_gate, d_up], axis=-1).astype(bf16)
    grad_in = jnp.einsum("esd,esf->edf", expert_rows, d_gate_up, preferred_element_type=f32)
    d_rows = jnp.einsum("esf,edf->esd", d_gate_up, in_weight, preferred_element_type=f32).astype(bf16)
    d_part = jnp.einsum(
        "cesr,ecsd->crd", onehot, d_rows.reshape(2, N_CTX, MOST, D), preferred_element_type=f32
    ).astype(bf16)
    d_gate_rows = jnp.sum(
        onehot.astype(f32) * jnp.moveaxis(d_gate_slot.reshape(2, N_CTX, MOST), 0, 1)[..., None], axis=2
    )
    dg_high, dg_rest = halves(jnp.moveaxis(d_gate_rows, 1, 2))
    put = lambda v: lax.dynamic_update_slice_in_dim(
        jnp.zeros((N_CTX, ROWS, EXPERTS), bf16), v, 2 * ctx, axis=2
    )
    d_part = jnp.concatenate(
        [d_part, put(dg_high), put(dg_rest), jnp.zeros((N_CTX, ROWS, EXTRA - 64), bf16)], axis=2
    )
    grad_in = lax.psum_scatter(
        jnp.moveaxis(grad_in.reshape(2, N_DP, ROWS, 2 * FF), 1, 0).astype(bf16), DP, scatter_dimension=0
    ).astype(f32)
    grad_down = lax.psum_scatter(
        jnp.moveaxis(grad_down.reshape(2, FF, N_DP, ROWS), 2, 0).astype(bf16), DP, scatter_dimension=0
    ).astype(f32)
    d_sum = scatter_ctx(d_part, 4)

    grad_top = cotangent.astype(f32)
    d_gates = d_sum[:, D : D + 32] + d_sum[:, D + 32 : D + 64]
    d_picked = gates * (d_gates - jnp.sum(gates * d_gates, axis=1, keepdims=True))
    d_logits = d_picked.astype(bf16)
    d_hidden_two = d_sum[:, :D] + dot_last(d_logits, router_weight)
    d_norm_two, grad_gain_two = norm_backward(d_hidden_two, normed_two, scale_two, gain_two)
    d_residual = grad_top + d_norm_two
    sent = jnp.concatenate(
        [d_residual.astype(bf16), d_logits, jnp.zeros((ROWS, EXTRA - 32), bf16)], axis=1
    )
    all_three = gather_ctx(sent, 5).reshape(SEQ, D + EXTRA)
    d_branch = all_three[:, :D]
    d_logits_all = all_three[:, D : D + 32]

    d_attended = dot_last(d_branch, out_weight).astype(bf16).astype(f32)
    d_raw = attend_back(src, order, query, key, value, lse, d_attended, cosine, sine)
    d_one = dot_last(d_raw, weight).astype(bf16).reshape(N_CTX, ROWS, D)
    d_hidden_one = scatter_ctx(d_one, 6)
    d_norm_one, grad_gain_one = norm_backward(d_hidden_one, normed_one, scale_one, gain_one)
    input_grad = d_residual + d_norm_one

    grad_out_weight = dot_first(attended, d_branch)
    own_columns = lax.dynamic_slice_in_dim(hidden_all.reshape(SEQ, D), ctx * 64, 64, axis=1)
    grad_router = dot_first(own_columns, d_logits_all)
    second = jnp.concatenate(
        [grad_out_weight, grad_router, jnp.zeros((64, EXTRA - 32), f32)], axis=1
    ).reshape(8, 8, D + EXTRA)
    grad_heads = dot_first(hidden_one, d_raw)
    first = jnp.concatenate(
        [
            grad_heads[:, :192],
            grad_gain_one[:, None],
            grad_gain_two[:, None],
            jnp.zeros((D, 62), f32),
        ],
        axis=1,
    ).astype(bf16)
    a, b = grads_out(first.reshape(N_DP, ROWS, 256), second, 7)
    b = jnp.sum(b, axis=0)
    side = lambda v: jnp.moveaxis(v, 0, 1).reshape(8, -1)
    pairs = a.reshape(KV_HEADS, 2, 8, 256).sum(axis=1)
    gains = jnp.sum(a[:, :, 192:194], axis=0)
    return (
        output,
        input_grad,
        gains[:, 0],
        side(a[:, :, 0:64]),
        side(pairs[:, :, 64:128]),
        side(pairs[:, :, 128:192]),
        b[:, :D],
        gains[:, 1],
        b[:, D : D + 32],
        grad_in,
        grad_down,
    )


def solution(mesh):
    split = Mesh(mesh.devices.reshape(2, 4, 2, 4, 2), AXES)
    rows = P(AXES, None)
    line = P(AXES)
    return jax.shard_map(
        local,
        mesh=split,
        in_specs=(
            rows,
            rows,
            P(),
            rows,
            line,
            rows,
            rows,
            rows,
            rows,
            line,
            rows,
            P(CTX, DP, None),
            P(CTX, None, DP),
        ),
        out_specs=(
            rows,
            rows,
            line,
            rows,
            rows,
            rows,
            rows,
            line,
            rows,
            P(CTX, DP, None),
            P(CTX, None, DP),
        ),
        check_vma=False,
    )
```

```python
import functools
import math

import jax
import jax.numpy as jnp
import numpy as np
from jax import lax
from jax.experimental import pallas as pl
from jax.experimental.pallas import tpu as pltpu
from jax.sharding import Mesh
from jax.sharding import PartitionSpec as P

D = 1024
HEADS = 16
KV_HEADS = 8
HEAD_DIM = 64
EXPERTS = 32
FF = 512
TOP = 8
MOST = 48
ROWS = 128
SEQ = 2048
BLOCK = 64
AXES = ("ylo", "z", "yhi", "x", "core")
DP = ("ylo", "z")
CTX = ("yhi", "x", "core")
N_DP = 8
N_CTX = 16
EXTRA = 128
MESH_ID = pl.DeviceIdType.MESH
ANY = pl.BlockSpec(memory_space=pl.ANY)
VMEM = pl.BlockSpec(memory_space=pltpu.VMEM)
SMEM = pl.BlockSpec(memory_space=pltpu.SMEM)
DMA = pltpu.SemaphoreType.DMA
bf16 = jnp.bfloat16
f32 = jnp.float32
epsilon = 1e-06


def dot(a, b):
    return jnp.dot(a, b, preferred_element_type=f32)


def dot_last(a, b):
    return lax.dot_general(a, b, (((1,), (1,)), ((), ())), preferred_element_type=f32)


def dot_first(a, b):
    return lax.dot_general(a, b, (((0,), (0,)), ((), ())), preferred_element_type=f32)


def my_place():
    return tuple(lax.axis_index(a) for a in AXES)


def device_at(dp, ctx):
    return (
        lax.div(dp, 4),
        lax.rem(dp, 4),
        lax.div(ctx, 8),
        lax.rem(lax.div(ctx, 2), 4),
        lax.rem(ctx, 2),
    )


def beside(place, dy, dx):
    ylo, z, yhi, x, core = place
    return (ylo, z, lax.rem(yhi + dy, 2), lax.rem(x + dx, 4), core)


def ctx_of(place):
    return place[2] * 8 + place[3] * 2 + place[4]


def dp_of(place):
    return place[0] * 4 + place[1]


def sibling_of(place):
    return place[:4] + (1 - place[4],)


def remote(src, dst, send, recv, device):
    return pltpu.make_async_remote_copy(
        src_ref=src, dst_ref=dst, send_sem=send, recv_sem=recv, device_id=device, device_id_type=MESH_ID
    )


def greet(devices):
    barrier = pltpu.get_barrier_semaphore()
    for device in devices:
        pl.semaphore_signal(barrier, inc=1, device_id=device, device_id_type=MESH_ID)
    return barrier


class RowGather:
    scratch = [DMA, DMA((9,)), DMA((9,)), DMA((10,)), DMA((10,))]
    links = [(1, 0), (0, 1), (0, 3), (0, 1), (0, 3), (0, 1), (0, 3), (0, 1), (0, 3)]
    held = [(0, 0), (0, 0), (0, 0), (1, 0), (1, 0), (0, 3), (0, 1), (1, 3), (1, 1)]
    parts = [None, None, None, None, None, 0, 1, 0, 1]
    after = {0: (3, 4), 1: (5,), 2: (6,), 3: (7,), 4: (8,)}

    def __init__(self, place, x_ref, view, half, local, send, recv, fsend, frecv):
        sibling = sibling_of(place)

        def piece(dy, dx, part):
            ref = view(beside(place, dy, dx))
            return ref if part is None else ref.at[pl.ds(part * half, half)]

        self.own = pltpu.make_async_copy(x_ref, view(place), local)
        self.out, self.landed, self.passed = [], [], []
        for n, ((ly, lx), (hy, hx), part) in enumerate(zip(self.links, self.held, self.parts)):
            source = x_ref if n < 3 else piece(hy, hx, part)
            self.out.append(
                remote(source, piece(hy, hx, part), send.at[n], recv.at[n], beside(place, ly, lx))
            )
            here = piece((hy + ly) % 2, (hx + 4 - lx) % 4, part)
            self.landed.append(remote(here, here, send.at[n], recv.at[n], beside(place, ly, lx)))
            self.passed.append(remote(here, here, fsend.at[n], frecv.at[n], sibling))
        self.passed.append(remote(x_ref, view(place), fsend.at[9], frecv.at[9], sibling))
        self.back = []
        for n in range(9):
            (ly, lx), (hy, hx), part = self.links[n], self.held[n], self.parts[n]
            ref = view(sibling_of(beside(place, (hy + ly) % 2, (hx + 4 - lx) % 4)))
            ref = ref if part is None else ref.at[pl.ds(part * half, half)]
            self.back.append(remote(ref, ref, fsend.at[n], frecv.at[n], sibling))
        ref = view(sibling)
        self.back.append(remote(ref, ref, fsend.at[9], frecv.at[9], sibling))

    def start(self):
        for n in range(3):
            self.out[n].start()
        self.passed[9].start()
        self.own.start()

    def step(self, n):
        self.landed[n].wait_recv()
        for m in self.after.get(n, ()):
            self.out[m].start()
        self.passed[n].start()

    def pass_on(self):
        for n in range(9):
            self.step(n)

    def finish(self):
        self.own.wait()
        for n in range(10):
            self.back[n].wait_recv()
        for copy in self.out + self.passed:
            copy.wait_send()


def chip_neighbours(place):
    return [beside(place, 1, 0), beside(place, 0, 1), beside(place, 0, 3), sibling_of(place)]


def gather_kernel(x_ref, out_ref, *sems):
    place = my_place()
    pl.semaphore_wait(greet(chip_neighbours(place)), 4)
    gather = RowGather(place, x_ref, lambda p: out_ref.at[ctx_of(p)], x_ref.shape[0] // 2, *sems)
    gather.start()
    gather.pass_on()
    gather.finish()


def gather_ctx(x, number):
    return pl.pallas_call(
        gather_kernel,
        out_shape=jax.ShapeDtypeStruct((N_CTX,) + x.shape, x.dtype),
        in_specs=[ANY],
        out_specs=ANY,
        scratch_shapes=RowGather.scratch,
        compiler_params=pltpu.CompilerParams(collective_id=number, has_side_effects=True),
        name="gather_rows",
    )(x)


SPREAD = [(1, 2), (0, 2), (1, 1), (1, 3), (0, 1), (0, 3), (1, 0), (0, 0)]


class RowScatter:
    @staticmethod
    def scratch(rows, width):
        return [
            pltpu.VMEM((8, rows, width), bf16),
            pltpu.VMEM((8, rows, width), bf16),
            pltpu.VMEM((4, rows // 2, width), bf16),
            pltpu.VMEM((4, rows, width), bf16),
            pltpu.VMEM((rows, width), bf16),
            DMA((8,)),
            DMA((8,)),
            DMA((8,)),
            DMA((9,)),
            DMA((9,)),
        ]

    def __init__(self, place, p_ref, own, other, halves, wholes, last, own_sem, fsend, frecv, send, recv):
        self.own, self.other, self.halves, self.wholes, self.last = own, other, halves, wholes, last
        core = place[4]
        half = own.shape[1] // 2
        self.half = half
        self.mine, self.cross = [], []
        for n, (dy, dx) in enumerate(SPREAD):
            chip = lax.div(ctx_of(beside(place, dy, dx)), 2)
            self.mine.append(pltpu.make_async_copy(p_ref.at[chip, core], own.at[n], own_sem.at[n]))
            self.cross.append(
                remote(p_ref.at[chip, 1 - core], other.at[n], fsend.at[n], frecv.at[n], sibling_of(place))
            )
        right, left = beside(place, 0, 1), beside(place, 0, 3)
        self.out = []
        for n, (source, target, device) in enumerate(
            [
                (own.at[0, pl.ds(0, half)], halves.at[0], right),
                (own.at[0, pl.ds(half, half)], halves.at[1], left),
                (own.at[1, pl.ds(0, half)], halves.at[2], right),
                (own.at[1, pl.ds(half, half)], halves.at[3], left),
                (own.at[2], wholes.at[0], right),
                (own.at[3], wholes.at[1], left),
                (own.at[4], wholes.at[2], right),
                (own.at[5], wholes.at[3], left),
                (own.at[6], last, beside(place, 1, 0)),
            ]
        ):
            self.out.append(remote(source, target, send.at[n], recv.at[n], device))

    def start(self, n):
        self.cross[n].start()
        self.mine[n].start()

    def join(self, n):
        self.mine[n].wait()
        self.cross[n].wait_recv()
        return self.own[n].astype(f32) + self.other[n].astype(f32)

    def run(self):
        for n in range(2):
            self.own[n] = self.join(n).astype(bf16)
            self.out[2 * n].start()
            self.out[2 * n + 1].start()
        half = self.half
        for n in range(2, 6):
            total = self.join(n)
            side = pl.ds(0 if n % 2 == 0 else half, half)
            self.out[n - 2].wait_recv()
            self.own[n] = total.astype(bf16)
            first = total[:half] if n % 2 == 0 else total[half:]
            self.own[n, side] = (first + self.halves[n - 2].astype(f32)).astype(bf16)
            self.out[n + 2].start()
        total = self.join(6)
        for n in (0, 1):
            self.out[4 + n].wait_recv()
            total = total + self.wholes[n].astype(f32)
        self.own[6] = total.astype(bf16)
        self.out[8].start()
        total = self.join(7)
        for n in (2, 3):
            self.out[4 + n].wait_recv()
            total = total + self.wholes[n].astype(f32)
        self.out[8].wait_recv()
        return total + self.last[...].astype(f32)

    def finish(self):
        for copy in self.out + self.cross:
            copy.wait_send()


def scatter_kernel(p_ref, out_ref, *scratch):
    place = my_place()
    pl.semaphore_wait(greet(chip_neighbours(place)), 4)
    scatter = RowScatter(place, p_ref, *scratch)
    for n in range(8):
        scatter.start(n)
    out_ref[...] = scatter.run()
    scatter.finish()


def scatter_ctx(parts, number):
    rows, width = parts.shape[-2:]
    parts = parts.reshape(8, 2, rows, width)
    return pl.pallas_call(
        scatter_kernel,
        out_shape=jax.ShapeDtypeStruct((rows, width), f32),
        in_specs=[ANY],
        out_specs=VMEM,
        scratch_shapes=RowScatter.scratch(rows, width),
        compiler_params=pltpu.CompilerParams(
            collective_id=number, has_side_effects=True, vmem_limit_bytes=24 * 2**20
        ),
        name="scatter_rows",
    )(parts)


def entry_kernel(x_ref, w_ref, o_ref, x_out, w_out, o_out, *sems):
    row_sems, rest = sems[:5], sems[5:]
    wlocal, wsend, wrecv, psend, precv, olocal, osend, orecv = rest
    place = my_place()
    dp, ctx = dp_of(place), ctx_of(place)
    barrier = greet(
        [device_at(dp, lax.rem(ctx + k, N_CTX)) for k in range(1, N_CTX)]
        + [device_at(lax.rem(dp + k, N_DP), ctx) for k in range(1, N_DP)]
    )
    o_ctx = 2 * dp + lax.div(ctx, 8)
    o_home = lax.div(ctx, 2)
    from_ctx = 8 * lax.rem(ctx, 2)
    o_self = o_ctx == ctx
    for t in range(8):
        here = jnp.logical_and(o_home == dp, from_ctx + t == ctx)

        @pl.when(jnp.logical_not(here))
        def _():
            pl.semaphore_signal(
                barrier, inc=1, device_id=device_at(o_home, from_ctx + t), device_id_type=MESH_ID
            )

    pl.semaphore_wait(barrier, 30 - jnp.where(o_self, 1, 0))

    first = []
    for k in range(1, N_CTX):
        to = lax.rem(ctx + k, N_CTX)
        first.append(
            remote(w_ref.at[to], w_out.at[dp, ctx], wsend.at[k], wrecv.at[k], device_at(dp, to))
        )
    for copy in first:
        copy.start()
    own = pltpu.make_async_copy(w_ref.at[ctx], w_out.at[dp, ctx], wlocal)
    own.start()
    rows = RowGather(place, x_ref, lambda p: x_out.at[ctx_of(p)], x_ref.shape[0] // 2, *row_sems)
    rows.start()
    slot = lax.rem(ctx, 8)
    o_own = pltpu.make_async_copy(o_ref, o_out.at[slot], olocal)

    def o_copy(k):
        return remote(o_ref, o_out.at[slot], osend.at[k], orecv.at[slot], device_at(k, o_ctx))

    for k in range(8):
        here = jnp.logical_and(o_self, dp == k)

        @pl.when(here)
        def _():
            o_own.start()

        @pl.when(jnp.logical_not(here))
        def _():
            o_copy(k).start()

    own.wait()
    for copy in first:
        copy.wait_recv()
    second = []
    for k in range(1, N_DP):
        to = lax.rem(dp + k, N_DP)
        second.append(remote(w_out.at[dp], w_out.at[dp], psend.at[k], precv.at[k], device_at(to, ctx)))
    for copy in second:
        copy.start()
    rows.pass_on()
    rows.finish()
    for copy in second:
        copy.wait_recv()
    for t in range(8):
        here = jnp.logical_and(o_home == dp, from_ctx + t == ctx)

        @pl.when(jnp.logical_not(here))
        def _():
            remote(o_ref, o_out.at[t], osend.at[0], orecv.at[t], device_at(dp, ctx)).wait_recv()

    for k in range(8):
        here = jnp.logical_and(o_self, dp == k)

        @pl.when(here)
        def _():
            o_own.wait()

        @pl.when(jnp.logical_not(here))
        def _():
            o_copy(k).wait_send()

    for copy in first + second:
        copy.wait_send()


def entry(x, w, o, number):
    return pl.pallas_call(
        entry_kernel,
        out_shape=(
            jax.ShapeDtypeStruct((N_CTX,) + x.shape, x.dtype),
            jax.ShapeDtypeStruct((N_DP,) + w.shape, w.dtype),
            jax.ShapeDtypeStruct((8,) + o.shape, o.dtype),
        ),
        in_specs=[ANY] * 3,
        out_specs=(ANY, ANY, ANY),
        scratch_shapes=RowGather.scratch
        + [DMA, DMA((16,)), DMA((16,)), DMA((8,)), DMA((8,)), DMA, DMA((8,)), DMA((8,))],
        compiler_params=pltpu.CompilerParams(collective_id=number, has_side_effects=True),
        name="entry_gather",
    )(x, w, o)


def grads_kernel(
    a_ref, b_ref, a_out, b_out, landed, part, wlocal, wsend, wrecv, psend, precv, olocal, osend, orecv, plocal
):
    place = my_place()
    dp, ctx = dp_of(place), ctx_of(place)
    barrier = greet(
        [device_at(dp, lax.rem(ctx + k, N_CTX)) for k in range(1, N_CTX)]
        + [device_at(lax.rem(dp + k, N_DP), ctx) for k in range(1, N_DP)]
    )
    o_ctx = 2 * dp + lax.div(ctx, 8)
    o_home = lax.div(ctx, 2)
    to_ctx = 8 * lax.rem(ctx, 2)
    o_self = o_ctx == ctx
    for k in range(8):
        here = jnp.logical_and(o_self, dp == k)

        @pl.when(jnp.logical_not(here))
        def _():
            pl.semaphore_signal(barrier, inc=1, device_id=device_at(k, o_ctx), device_id_type=MESH_ID)

    pl.semaphore_wait(barrier, 30 - jnp.where(o_self, 1, 0))

    first = []
    for k in range(1, N_DP):
        to = lax.rem(dp + k, N_DP)
        first.append(remote(a_ref.at[to], landed.at[k], wsend.at[k], wrecv.at[k], device_at(to, ctx)))
    for copy in first:
        copy.start()
    own = pltpu.make_async_copy(a_ref.at[dp], landed.at[0], wlocal)
    own.start()

    def o_copy(t):
        return remote(
            b_ref.at[t], b_out.at[dp], osend.at[t], orecv.at[dp], device_at(o_home, to_ctx + t)
        )

    o_own = pltpu.make_async_copy(b_ref.at[lax.rem(ctx, 8)], b_out.at[dp], olocal)
    for t in range(8):
        here = jnp.logical_and(o_home == dp, to_ctx + t == ctx)

        @pl.when(here)
        def _():
            o_own.start()

        @pl.when(jnp.logical_not(here))
        def _():
            o_copy(t).start()

    own.wait()
    total = landed[0].astype(f32)
    for copy in first:
        copy.wait_recv()
    for k in range(1, N_DP):
        total = total + landed[k].astype(f32)
    part[...] = total.reshape(part.shape)
    second = []
    for k in range(1, N_CTX):
        to = lax.rem(ctx + k, N_CTX)
        second.append(remote(part.at[to], a_out.at[ctx], psend.at[k], precv.at[k], device_at(dp, to)))
    for copy in second:
        copy.start()
    mine = pltpu.make_async_copy(part.at[ctx], a_out.at[ctx], plocal)
    mine.start()
    mine.wait()
    for copy in second:
        copy.wait_recv()
    for k in range(8):
        here = jnp.logical_and(o_self, dp == k)

        @pl.when(here)
        def _():
            o_own.wait()

        @pl.when(jnp.logical_not(here))
        def _():
            remote(b_ref.at[0], b_out.at[k], osend.at[0], orecv.at[k], device_at(dp, ctx)).wait_recv()

    for t in range(8):
        here = jnp.logical_and(o_home == dp, to_ctx + t == ctx)

        @pl.when(jnp.logical_not(here))
        def _():
            o_copy(t).wait_send()

    for copy in first + second:
        copy.wait_send()


def grads_out(a, b, number):
    width = a.shape[-1]
    return pl.pallas_call(
        grads_kernel,
        out_shape=(
            jax.ShapeDtypeStruct((N_CTX, 8, width), f32),
            jax.ShapeDtypeStruct((N_DP,) + b.shape[1:], f32),
        ),
        in_specs=[ANY] * 2,
        out_specs=(VMEM, VMEM),
        scratch_shapes=[pltpu.VMEM(a.shape, a.dtype), pltpu.VMEM((N_CTX, 8, width), f32)]
        + [DMA, DMA((8,)), DMA((8,)), DMA((16,)), DMA((16,)), DMA, DMA((8,)), DMA((8,)), DMA],
        compiler_params=pltpu.CompilerParams(
            collective_id=number, has_side_effects=True, vmem_limit_bytes=24 * 2**20
        ),
        name="sum_grads",
    )(a, b)


def experts_kernel(
    ctx_ref, two_ref, cot_ref, win_ref, wdn_ref, out_ref, d_ref, gin_ref, gdn_ref,
    two, cot, win, wdn, wide, picks, gate_slot, dg_slot, rows, tops, weighted, hidden, d_mid, d_rows,
    gin, gdn, stage, d_stage, in_sem, out_sem, d_sem, g_sem,
):
    loads = [
        pltpu.make_async_copy(two_ref, two, in_sem.at[0]),
        pltpu.make_async_copy(cot_ref, cot, in_sem.at[1]),
        pltpu.make_async_copy(win_ref, win, in_sem.at[2]),
        pltpu.make_async_copy(wdn_ref, wdn, in_sem.at[3]),
    ]
    for load in loads:
        load.start()
    ctx = ctx_ref[0]
    line = lax.broadcasted_iota(jnp.int32, (8, EXTRA), 0)
    lane = lax.broadcasted_iota(jnp.int32, (8, EXTRA), 1)
    start = jnp.where(line < 2, 64, jnp.where(line < 4, 0, 32))
    chosen = jnp.logical_and(line < 6, lane == start + 2 * ctx + lax.rem(line, 2))
    chosen = jnp.where(chosen, 1.0, 0.0).astype(bf16)
    back = jnp.logical_and(line < 4, lane == jnp.where(line < 2, 0, 32) + 2 * ctx + lax.rem(line, 2))
    back = jnp.where(back, 1.0, 0.0).astype(bf16)
    before = lax.broadcasted_iota(jnp.int32, (ROWS, ROWS), 0) < lax.broadcasted_iota(
        jnp.int32, (ROWS, ROWS), 1
    )
    before = jnp.where(before, 1.0, 0.0).astype(bf16)
    slots = lax.broadcasted_iota(jnp.int32, (MOST, ROWS), 0).astype(f32)
    loads[0].wait()
    loads[1].wait()

    def pick(c, _):
        facts = dot_last(chosen, two[c, :, D:])
        place = dot(facts.astype(bf16), before)
        both = []
        here = pl.ds(pl.multiple_of(c * MOST, MOST), MOST)
        for e in range(2):
            member = facts[e : e + 1]
            onehot = jnp.where(jnp.logical_and(place[e : e + 1] == slots, member > 0.5), 1.0, 0.0)
            gate = facts[2 + e : 3 + e] + facts[4 + e : 5 + e]
            gate_slot[e, here] = jnp.sum(onehot * gate, axis=1, keepdims=True)
            both.append(onehot.astype(bf16))
        both = jnp.concatenate(both, axis=0)
        picks[c] = both
        taken = dot(both, two[c, :, :D]).astype(bf16)
        rows[0, here] = taken[:MOST]
        rows[1, here] = taken[MOST:]
        taken = dot(both, cot[c]).astype(bf16)
        tops[0, here] = taken[:MOST]
        tops[1, here] = taken[MOST:]
        return 0

    lax.fori_loop(0, N_CTX, pick, 0)
    loads[2].wait()
    loads[3].wait()
    for e in range(2):
        for k in range(N_DP):
            wide[e, :, k * ROWS : (k + 1) * ROWS] = wdn[k, e]
    tile = 256
    for e in range(2):

        def forth(t, _):
            here = pl.ds(pl.multiple_of(t * tile, tile), tile)
            weight = win[:, e].reshape(D, 2 * FF)
            down = wide[e]
            both = dot(rows[e, here], weight)
            gate_part, up_part = both[:, :FF], both[:, FF:]
            sigmoid = 1.0 / (1.0 + jnp.exp(-gate_part))
            silu = gate_part * sigmoid
            middle = (silu * up_part).astype(bf16)
            hidden[e, here] = middle
            result = dot(middle, down).astype(bf16).astype(f32)
            gate = gate_slot[e, here]
            top = tops[e, here].astype(f32)
            dg_slot[e, here] = jnp.sum(top * result, axis=1, keepdims=True)
            weighted[e, here] = (result * gate).astype(bf16)
            d_result = (top * gate).astype(bf16)
            tops[e, here] = d_result
            d_middle = dot_last(d_result, down)
            d_mid[e, here, :FF] = (
                d_middle * up_part * (sigmoid * (1.0 + gate_part * (1.0 - sigmoid)))
            ).astype(bf16)
            d_mid[e, here, FF:] = (d_middle * silu).astype(bf16)
            d_rows[e, here] = dot_last(d_mid[e, here], weight).astype(bf16)
            return 0

        lax.fori_loop(0, N_CTX * MOST // tile, forth, 0)

    def combine(c, _):
        here = pl.ds(pl.multiple_of(c * MOST, MOST), MOST)
        both = picks[c]
        slot = lax.rem(c, 2)

        @pl.when(c >= 2)
        def _():
            pltpu.make_async_copy(stage.at[slot], out_ref.at[c], out_sem.at[slot]).wait()
            pltpu.make_async_copy(d_stage.at[slot], d_ref.at[c], d_sem.at[slot]).wait()

        found = jnp.concatenate([d_rows[0, here], d_rows[1, here]], axis=0)
        d_stage[slot, :, :D] = dot_first(both, found).astype(bf16)
        lines = [
            jnp.sum(both[e * MOST : (e + 1) * MOST].astype(f32) * dg_slot[e, here], axis=0, keepdims=True)
            for e in range(2)
        ]
        high = [v.astype(bf16).astype(f32) for v in lines]
        rest = [v - h for v, h in zip(lines, high)]
        lines = jnp.concatenate(high + rest + [jnp.zeros((4, ROWS), f32)], axis=0).astype(bf16)
        d_stage[slot, :, D:] = dot_first(lines, back).astype(bf16)
        found = jnp.concatenate([weighted[0, here], weighted[1, here]], axis=0)
        stage[slot] = dot_first(both, found).astype(bf16)
        pltpu.make_async_copy(d_stage.at[slot], d_ref.at[c], d_sem.at[slot]).start()
        pltpu.make_async_copy(stage.at[slot], out_ref.at[c], out_sem.at[slot]).start()
        return 0

    lax.fori_loop(0, N_CTX, combine, 0)
    for slot in range(2):
        pltpu.make_async_copy(stage.at[slot], out_ref.at[slot], out_sem.at[slot]).wait()
        pltpu.make_async_copy(d_stage.at[slot], d_ref.at[slot], d_sem.at[slot]).wait()
    for e in range(2):

        def weights(k, _):
            here = pl.ds(pl.multiple_of(k * 256, 256), 256)
            total = dot_first(rows[e, :, here], d_mid[e]).astype(bf16)
            gin[2 * k, e] = total[:ROWS]
            gin[2 * k + 1, e] = total[ROWS:]
            total = dot_first(hidden[e], tops[e, :, here]).astype(bf16)
            gdn[2 * k, e] = total[:, :ROWS]
            gdn[2 * k + 1, e] = total[:, ROWS:]
            return 0

        lax.fori_loop(0, D // 256, weights, 0)
    saves = [
        pltpu.make_async_copy(gin, gin_ref, g_sem.at[0]),
        pltpu.make_async_copy(gdn, gdn_ref, g_sem.at[1]),
    ]
    for save in saves:
        save.start()
    for save in saves:
        save.wait()


def experts(ctx, two, cot, expert_in, expert_out):
    slots = N_CTX * MOST
    v = lambda *shape: pltpu.VMEM(shape, bf16)
    column = pltpu.VMEM((2, slots, 1), f32)
    return pl.pallas_call(
        experts_kernel,
        out_shape=(
            jax.ShapeDtypeStruct((N_CTX, ROWS, D), bf16),
            jax.ShapeDtypeStruct((N_CTX, ROWS, D + EXTRA), bf16),
            jax.ShapeDtypeStruct(expert_in.shape, bf16),
            jax.ShapeDtypeStruct(expert_out.shape, bf16),
        ),
        in_specs=[SMEM] + [ANY] * 4,
        out_specs=(ANY,) * 4,
        scratch_shapes=[
            v(*two.shape),
            v(*cot.shape),
            v(*expert_in.shape),
            v(*expert_out.shape),
            v(2, FF, D),
            v(N_CTX, 2 * MOST, ROWS),
            column,
            column,
            v(2, slots, D),
            v(2, slots, D),
            v(2, slots, D),
            v(2, slots, FF),
            v(2, slots, 2 * FF),
            v(2, slots, D),
            v(*expert_in.shape),
            v(*expert_out.shape),
            v(2, ROWS, D),
            v(2, ROWS, D + EXTRA),
            DMA((4,)),
            DMA((2,)),
            DMA((2,)),
            DMA((2,)),
        ],
        compiler_params=pltpu.CompilerParams(vmem_limit_bytes=58 * 2**20),
        cost_estimate=pl.CostEstimate(flops=15 * 10**9, bytes_accessed=30 * 2**20, transcendentals=2**20),
        name="experts_both_ways",
    )(ctx, two, cot, expert_in, expert_out)


def swap_halves(u):
    lane = lax.broadcasted_iota(jnp.int32, u.shape, 1)
    return jnp.where(lax.rem(lane, 64) < 32, pltpu.roll(u, 96, 1), pltpu.roll(u, 32, 1))


def attend_kernel(src, order, raw_ref, cos_ref, sin_ref, o_ref, q_ref, k_ref, v_ref, lse_ref, out_nat):
    for b in range(SEQ // BLOCK):
        rows = pl.ds(pl.multiple_of(src[b] * BLOCK, BLOCK), BLOCK)
        here = pl.ds(b * BLOCK, BLOCK)
        qk = raw_ref[rows, 0:128]
        qk = qk * cos_ref[here, :] + swap_halves(qk) * sin_ref[here, :]
        q_ref[here, :] = (qk[:, 0:64]).astype(bf16)
        k_ref[here, :] = (qk[:, 64:128]).astype(bf16)
        v_ref[here, :] = raw_ref[rows, 128:192].astype(bf16)
    step = 256
    for i in range(SEQ // step):
        length = (i + 1) * step
        here = pl.ds(i * step, step)
        scores = dot_last(q_ref[here, :], k_ref[0:length, :]) * 0.125
        row = i * step + lax.broadcasted_iota(jnp.int32, (step, length), 0)
        column = lax.broadcasted_iota(jnp.int32, (step, length), 1)
        scores = jnp.where(column <= row, scores, -1e30)
        top = jnp.max(scores, axis=1, keepdims=True)
        weights = jnp.exp(scores - top)
        total = jnp.sum(weights, axis=1, keepdims=True)
        lse_ref[here, :] = top + jnp.log(total)
        probs = (weights * (1.0 / total)).astype(bf16)
        out_nat[here, :] = dot(probs, v_ref[0:length, :])
    for b in range(SEQ // BLOCK):
        rows = pl.ds(pl.multiple_of(order[b] * BLOCK, BLOCK), BLOCK)
        o_ref[pl.ds(b * BLOCK, BLOCK), :] = out_nat[rows, :].astype(bf16)


def attend(src, order, raw, cosine, sine):
    head = jax.ShapeDtypeStruct((SEQ, HEAD_DIM), bf16)
    return pl.pallas_call(
        attend_kernel,
        out_shape=(head, head, head, head, jax.ShapeDtypeStruct((SEQ, 1), f32)),
        in_specs=[SMEM, SMEM, VMEM, VMEM, VMEM],
        out_specs=(VMEM,) * 5,
        scratch_shapes=[pltpu.VMEM((SEQ, HEAD_DIM), f32)],
        compiler_params=pltpu.CompilerParams(vmem_limit_bytes=48 * 2**20),
        cost_estimate=pl.CostEstimate(flops=10**9, bytes_accessed=6 * 2**20, transcendentals=2**21),
        name="attention_forward",
    )(src, order, raw, cosine, sine)


def attend_back_kernel(
    src, order, q_ref, k_ref, v_ref, lse_ref, do_ref, cos_ref, sin_ref, out_ref, do_nat, acc, done
):
    for b in range(SEQ // BLOCK):
        rows = pl.ds(pl.multiple_of(src[b] * BLOCK, BLOCK), BLOCK)
        do_nat[pl.ds(b * BLOCK, BLOCK), :] = do_ref[rows, :]
    acc[...] = jnp.zeros_like(acc)
    step = 256
    for i in range(SEQ // step):
        length = (i + 1) * step
        here = pl.ds(i * step, step)
        query, d_out = q_ref[here, :], do_nat[here, :].astype(bf16)
        keys = k_ref[0:length, :]
        scores = dot_last(query, keys) * 0.125
        row = i * step + lax.broadcasted_iota(jnp.int32, (step, length), 0)
        column = lax.broadcasted_iota(jnp.int32, (step, length), 1)
        probs = jnp.where(column <= row, jnp.exp(scores - lse_ref[here, :]), 0.0)
        d_probs = dot_last(d_out, v_ref[0:length, :])
        delta = jnp.sum(probs * d_probs, axis=1, keepdims=True)
        d_scores = (probs * (d_probs - delta)).astype(bf16)
        acc[here, 0:64] = dot(d_scores, keys) * 0.125
        acc[0:length, 64:128] += dot_first(d_scores, query) * 0.125
        acc[0:length, 128:192] += dot_first(probs.astype(bf16), d_out)
    for b in range(SEQ // BLOCK):
        here = pl.ds(b * BLOCK, BLOCK)
        qk = acc[here, 0:128]
        qk = qk * cos_ref[here, :] - swap_halves(qk) * sin_ref[here, :]
        done[here, 0:128] = qk
        done[here, 128:256] = acc[here, 128:256]
    for b in range(SEQ // BLOCK):
        rows = pl.ds(pl.multiple_of(order[b] * BLOCK, BLOCK), BLOCK)
        out_ref[pl.ds(b * BLOCK, BLOCK), :] = done[rows, :].astype(bf16)


def attend_back(src, order, q, k, v, lse, d_out, cosine, sine):
    return pl.pallas_call(
        attend_back_kernel,
        out_shape=jax.ShapeDtypeStruct((SEQ, 256), bf16),
        in_specs=[SMEM, SMEM] + [VMEM] * 7,
        out_specs=VMEM,
        scratch_shapes=[
            pltpu.VMEM((SEQ, HEAD_DIM), f32),
            pltpu.VMEM((SEQ, 256), f32),
            pltpu.VMEM((SEQ, 256), f32),
        ],
        compiler_params=pltpu.CompilerParams(vmem_limit_bytes=56 * 2**20),
        cost_estimate=pl.CostEstimate(flops=3 * 10**9, bytes_accessed=6 * 2**20, transcendentals=2**21),
        name="attention_backward",
    )(src, order, q, k, v, lse, d_out, cosine, sine)


def rotary_tables():
    inverse = 10000.0 ** (-np.arange(32, dtype=np.float64) * 2.0 / HEAD_DIM)
    angles = np.arange(SEQ, dtype=np.float64)[:, None] * inverse[None, :]
    cosine, sine = np.cos(angles), np.sin(angles)
    return (
        np.tile(cosine, (1, 4)).astype(np.float32),
        np.concatenate([-sine, sine, -sine, sine], axis=1).astype(np.float32),
    )


def normalize(inputs, gain_values):
    scale_rows = lax.rsqrt(jnp.mean(inputs * inputs, axis=-1, keepdims=True) + epsilon)
    normed = inputs * scale_rows
    return (scale_rows, normed, (normed * gain_values.astype(f32)).astype(bf16))


def norm_backward(grad_in, normed, scale_rows, gain_values):
    grad_normed = grad_in * gain_values.astype(f32)
    inner = jnp.mean(grad_normed * normed, axis=-1, keepdims=True)
    return (scale_rows * (grad_normed - normed * inner), jnp.sum(grad_in * normed, axis=0))


def halves(value):
    high = lax.reduce_precision(value, 8, 7)
    return high.astype(bf16), (value - high).astype(bf16)


def local(
    tokens,
    cotangent,
    block_order,
    routes,
    norm_one,
    w_query,
    w_key,
    w_value,
    w_out,
    norm_two,
    w_router,
    expert_in,
    expert_out,
):
    ctx = lax.axis_index(CTX)
    cosine, sine = (jnp.asarray(t) for t in rotary_tables())
    order = jnp.stack([block_order, 2 * N_CTX - 1 - block_order], axis=1).reshape(-1)
    spots = jnp.arange(2 * N_CTX, dtype=jnp.int32)
    src = jnp.sum(jnp.where(order[None, :] == spots[:, None], spots[None, :], 0), axis=1)

    by_head = lambda w, heads: jnp.moveaxis(w.reshape(8, heads, HEAD_DIM), 1, 0)
    query_part = by_head(w_query, HEADS)
    key_part = jnp.repeat(by_head(w_key, KV_HEADS), 2, axis=0)
    value_part = jnp.repeat(by_head(w_value, KV_HEADS), 2, axis=0)
    small = jnp.concatenate(
        [w_router, norm_one[:, None], norm_two[:, None], jnp.zeros((8, 30), bf16)], axis=1
    )
    small = jnp.broadcast_to(small[None], (N_CTX, 8, 64))
    packed = jnp.concatenate(
        [
            jnp.concatenate([query_part, key_part], axis=2),
            jnp.concatenate([value_part, small], axis=2),
        ],
        axis=1,
    )
    tokens_all, packed_all, out_all = entry(tokens, packed, w_out.reshape(16, 512), 0)
    expert_in_all = lax.all_gather(expert_in, DP, axis=0)
    expert_out_all = lax.all_gather(expert_out, DP, axis=0)
    cotangent_all = lax.all_gather(cotangent, CTX, axis=0)
    low = packed_all[:, :, 8:, :].reshape(D, 128)
    weight = jnp.concatenate(
        [packed_all[:, :, :8, :].reshape(D, 128), low[:, :64], jnp.zeros((D, 64), bf16)], axis=1
    )
    router_weight, gain_one, gain_two = low[:, 64:96], low[:, 96], low[:, 97]
    out_weight = out_all.reshape(HEAD_DIM, D)

    tokens_float = tokens.astype(f32)
    scale_one, normed_one, _ = normalize(tokens_float, gain_one)
    _, _, hidden_one = normalize(tokens_all.reshape(SEQ, D).astype(f32), gain_one)
    raw = dot(hidden_one, weight)
    attended, query, key, value, lse = attend(src, order, raw, cosine, sine)
    partial = dot(attended, out_weight).astype(bf16).reshape(N_CTX, ROWS, D)
    residual = tokens_float + scatter_ctx(partial, 1)
    scale_two, normed_two, hidden_two = normalize(residual, gain_two)

    logits = dot(hidden_two, router_weight)
    names = jnp.arange(EXPERTS, dtype=jnp.int32)
    member = jnp.any(routes[:, :, None] == names[None, None, :], axis=1)
    picked = jnp.where(member, logits, -1e30)
    shifted = jnp.where(member, jnp.exp(picked - jnp.max(picked, axis=1, keepdims=True)), 0.0)
    gates = shifted / jnp.sum(shifted, axis=1, keepdims=True)
    high, rest = halves(gates)
    sent = jnp.concatenate(
        [hidden_two, high, rest, member.astype(bf16), jnp.zeros((ROWS, EXTRA - 96), bf16)], axis=1
    )
    all_two = gather_ctx(sent, 2)

    hidden_all = all_two[:, :, :D]
    out_part, d_part, grad_in, grad_down = experts(
        ctx.reshape(1), all_two, cotangent_all, expert_in_all, expert_out_all
    )
    output = residual + scatter_ctx(out_part, 3)
    grad_in = lax.psum_scatter(grad_in, DP, scatter_dimension=0).astype(f32)
    grad_down = lax.psum_scatter(grad_down, DP, scatter_dimension=0).astype(f32)
    d_sum = scatter_ctx(d_part, 4)

    grad_top = cotangent.astype(f32)
    d_gates = d_sum[:, D : D + 32] + d_sum[:, D + 32 : D + 64]
    d_picked = gates * (d_gates - jnp.sum(gates * d_gates, axis=1, keepdims=True))
    d_logits = d_picked.astype(bf16)
    d_hidden_two = d_sum[:, :D] + dot_last(d_logits, router_weight)
    d_norm_two, grad_gain_two = norm_backward(d_hidden_two, normed_two, scale_two, gain_two)
    d_residual = grad_top + d_norm_two
    sent = jnp.concatenate(
        [d_residual.astype(bf16), d_logits, jnp.zeros((ROWS, EXTRA - 32), bf16)], axis=1
    )
    all_three = gather_ctx(sent, 5).reshape(SEQ, D + EXTRA)
    d_branch = all_three[:, :D]
    d_logits_all = all_three[:, D : D + 32]

    d_attended = dot_last(d_branch, out_weight).astype(bf16).astype(f32)
    d_raw = attend_back(src, order, query, key, value, lse, d_attended, cosine, sine)
    d_one = dot_last(d_raw, weight).astype(bf16).reshape(N_CTX, ROWS, D)
    d_hidden_one = scatter_ctx(d_one, 6)
    d_norm_one, grad_gain_one = norm_backward(d_hidden_one, normed_one, scale_one, gain_one)
    input_grad = d_residual + d_norm_one

    grad_out_weight = dot_first(attended, d_branch)
    own_columns = lax.dynamic_slice_in_dim(hidden_all.reshape(SEQ, D), ctx * 64, 64, axis=1)
    grad_router = dot_first(own_columns, d_logits_all)
    second = jnp.concatenate(
        [grad_out_weight, grad_router, jnp.zeros((64, EXTRA - 32), f32)], axis=1
    ).reshape(8, 8, D + EXTRA)
    grad_heads = dot_first(hidden_one, d_raw)
    first = jnp.concatenate(
        [
            grad_heads[:, :192],
            grad_gain_one[:, None],
            grad_gain_two[:, None],
            jnp.zeros((D, 62), f32),
        ],
        axis=1,
    ).astype(bf16)
    a, b = grads_out(first.reshape(N_DP, ROWS, 256), second, 7)
    b = jnp.sum(b, axis=0)
    side = lambda v: jnp.moveaxis(v, 0, 1).reshape(8, -1)
    pairs = a.reshape(KV_HEADS, 2, 8, 256).sum(axis=1)
    gains = jnp.sum(a[:, :, 192:194], axis=0)
    return (
        output,
        input_grad,
        gains[:, 0],
        side(a[:, :, 0:64]),
        side(pairs[:, :, 64:128]),
        side(pairs[:, :, 128:192]),
        b[:, :D],
        gains[:, 1],
        b[:, D : D + 32],
        grad_in,
        grad_down,
    )


def solution(mesh):
    split = Mesh(mesh.devices.reshape(2, 4, 2, 4, 2), AXES)
    rows = P(AXES, None)
    line = P(AXES)
    return jax.shard_map(
        local,
        mesh=split,
        in_specs=(
            rows,
            rows,
            P(),
            rows,
            line,
            rows,
            rows,
            rows,
            rows,
            line,
            rows,
            P(CTX, DP, None),
            P(CTX, None, DP),
        ),
        out_specs=(
            rows,
            rows,
            line,
            rows,
            rows,
            rows,
            rows,
            line,
            rows,
            P(CTX, DP, None),
            P(CTX, None, DP),
        ),
        check_vma=False,
    )
```

```python
import functools
import math

import jax
import jax.numpy as jnp
import numpy as np
from jax import lax
from jax.experimental import pallas as pl
from jax.experimental.pallas import tpu as pltpu
from jax.sharding import Mesh
from jax.sharding import PartitionSpec as P

D = 1024
HEADS = 16
KV_HEADS = 8
HEAD_DIM = 64
EXPERTS = 32
FF = 512
TOP = 8
MOST = 48
ROWS = 128
SEQ = 2048
BLOCK = 64
AXES = ("ylo", "z", "yhi", "x", "core")
DP = ("ylo", "z")
CTX = ("yhi", "x", "core")
N_DP = 8
N_CTX = 16
EXTRA = 128
MESH_ID = pl.DeviceIdType.MESH
ANY = pl.BlockSpec(memory_space=pl.ANY)
VMEM = pl.BlockSpec(memory_space=pltpu.VMEM)
SMEM = pl.BlockSpec(memory_space=pltpu.SMEM)
DMA = pltpu.SemaphoreType.DMA
bf16 = jnp.bfloat16
f32 = jnp.float32
epsilon = 1e-06


def dot(a, b):
    return jnp.dot(a, b, preferred_element_type=f32)


def dot_last(a, b):
    return lax.dot_general(a, b, (((1,), (1,)), ((), ())), preferred_element_type=f32)


def dot_first(a, b):
    return lax.dot_general(a, b, (((0,), (0,)), ((), ())), preferred_element_type=f32)


def my_place():
    return tuple(lax.axis_index(a) for a in AXES)


def device_at(dp, ctx):
    return (
        lax.div(dp, 4),
        lax.rem(dp, 4),
        lax.div(ctx, 8),
        lax.rem(lax.div(ctx, 2), 4),
        lax.rem(ctx, 2),
    )


def beside(place, dy, dx):
    ylo, z, yhi, x, core = place
    return (ylo, z, lax.rem(yhi + dy, 2), lax.rem(x + dx, 4), core)


def ctx_of(place):
    return place[2] * 8 + place[3] * 2 + place[4]


def dp_of(place):
    return place[0] * 4 + place[1]


def sibling_of(place):
    return place[:4] + (1 - place[4],)


def remote(src, dst, send, recv, device):
    return pltpu.make_async_remote_copy(
        src_ref=src, dst_ref=dst, send_sem=send, recv_sem=recv, device_id=device, device_id_type=MESH_ID
    )


def greet(devices):
    barrier = pltpu.get_barrier_semaphore()
    for device in devices:
        pl.semaphore_signal(barrier, inc=1, device_id=device, device_id_type=MESH_ID)
    return barrier


class RowGather:
    scratch = [DMA, DMA((9,)), DMA((9,)), DMA((10,)), DMA((10,))]
    links = [(1, 0), (0, 1), (0, 3), (0, 1), (0, 3), (0, 1), (0, 3), (0, 1), (0, 3)]
    held = [(0, 0), (0, 0), (0, 0), (1, 0), (1, 0), (0, 3), (0, 1), (1, 3), (1, 1)]
    parts = [None, None, None, None, None, 0, 1, 0, 1]
    after = {0: (3, 4), 1: (5,), 2: (6,), 3: (7,), 4: (8,)}

    def __init__(self, place, x_ref, view, half, local, send, recv, fsend, frecv):
        sibling = sibling_of(place)

        def piece(dy, dx, part):
            ref = view(beside(place, dy, dx))
            return ref if part is None else ref.at[pl.ds(part * half, half)]

        self.own = pltpu.make_async_copy(x_ref, view(place), local)
        self.out, self.landed, self.passed = [], [], []
        for n, ((ly, lx), (hy, hx), part) in enumerate(zip(self.links, self.held, self.parts)):
            source = x_ref if n < 3 else piece(hy, hx, part)
            self.out.append(
                remote(source, piece(hy, hx, part), send.at[n], recv.at[n], beside(place, ly, lx))
            )
            here = piece((hy + ly) % 2, (hx + 4 - lx) % 4, part)
            self.landed.append(remote(here, here, send.at[n], recv.at[n], beside(place, ly, lx)))
            self.passed.append(remote(here, here, fsend.at[n], frecv.at[n], sibling))
        self.passed.append(remote(x_ref, view(place), fsend.at[9], frecv.at[9], sibling))
        self.back = []
        for n in range(9):
            (ly, lx), (hy, hx), part = self.links[n], self.held[n], self.parts[n]
            ref = view(sibling_of(beside(place, (hy + ly) % 2, (hx + 4 - lx) % 4)))
            ref = ref if part is None else ref.at[pl.ds(part * half, half)]
            self.back.append(remote(ref, ref, fsend.at[n], frecv.at[n], sibling))
        ref = view(sibling)
        self.back.append(remote(ref, ref, fsend.at[9], frecv.at[9], sibling))

    def start(self):
        for n in range(3):
            self.out[n].start()
        self.passed[9].start()
        self.own.start()

    def step(self, n):
        self.landed[n].wait_recv()
        for m in self.after.get(n, ()):
            self.out[m].start()
        self.passed[n].start()

    def pass_on(self):
        for n in range(9):
            self.step(n)

    def finish(self):
        self.own.wait()
        for n in range(10):
            self.back[n].wait_recv()
        for copy in self.out + self.passed:
            copy.wait_send()


def chip_neighbours(place):
    return [beside(place, 1, 0), beside(place, 0, 1), beside(place, 0, 3), sibling_of(place)]


def gather_kernel(x_ref, out_ref, *sems):
    place = my_place()
    pl.semaphore_wait(greet(chip_neighbours(place)), 4)
    gather = RowGather(place, x_ref, lambda p: out_ref.at[ctx_of(p)], x_ref.shape[0] // 2, *sems)
    gather.start()
    gather.pass_on()
    gather.finish()


def gather_ctx(x, number):
    return pl.pallas_call(
        gather_kernel,
        out_shape=jax.ShapeDtypeStruct((N_CTX,) + x.shape, x.dtype),
        in_specs=[ANY],
        out_specs=ANY,
        scratch_shapes=RowGather.scratch,
        compiler_params=pltpu.CompilerParams(collective_id=number, has_side_effects=True),
        name="gather_rows",
    )(x)


SPREAD = [(1, 2), (0, 2), (1, 1), (1, 3), (0, 1), (0, 3), (1, 0), (0, 0)]


class RowScatter:
    @staticmethod
    def scratch(rows, width):
        return [
            pltpu.VMEM((8, rows, width), bf16),
            pltpu.VMEM((8, rows, width), bf16),
            pltpu.VMEM((4, rows // 2, width), bf16),
            pltpu.VMEM((4, rows, width), bf16),
            pltpu.VMEM((rows, width), bf16),
            DMA((8,)),
            DMA((8,)),
            DMA((8,)),
            DMA((9,)),
            DMA((9,)),
        ]

    def __init__(self, place, part, own, other, halves, wholes, last, own_sem, fsend, frecv, send, recv):
        self.own, self.other, self.halves, self.wholes, self.last = own, other, halves, wholes, last
        core = place[4]
        half = own.shape[1] // 2
        self.half = half
        self.mine, self.cross = [], []
        for n, (dy, dx) in enumerate(SPREAD):
            chip = lax.div(ctx_of(beside(place, dy, dx)), 2)
            self.mine.append(pltpu.make_async_copy(part(chip, core), own.at[n], own_sem.at[n]))
            self.cross.append(
                remote(part(chip, 1 - core), other.at[n], fsend.at[n], frecv.at[n], sibling_of(place))
            )
        right, left = beside(place, 0, 1), beside(place, 0, 3)
        self.out = []
        for n, (source, target, device) in enumerate(
            [
                (own.at[0, pl.ds(0, half)], halves.at[0], right),
                (own.at[0, pl.ds(half, half)], halves.at[1], left),
                (own.at[1, pl.ds(0, half)], halves.at[2], right),
                (own.at[1, pl.ds(half, half)], halves.at[3], left),
                (own.at[2], wholes.at[0], right),
                (own.at[3], wholes.at[1], left),
                (own.at[4], wholes.at[2], right),
                (own.at[5], wholes.at[3], left),
                (own.at[6], last, beside(place, 1, 0)),
            ]
        ):
            self.out.append(remote(source, target, send.at[n], recv.at[n], device))

    def start(self, n):
        self.cross[n].start()
        self.mine[n].start()

    def join(self, n):
        self.mine[n].wait()
        self.cross[n].wait_recv()
        return self.own[n].astype(f32) + self.other[n].astype(f32)

    def step(self, n):
        if n < 2:
            self.own[n] = self.join(n).astype(bf16)
            self.out[2 * n].start()
            self.out[2 * n + 1].start()
        elif n < 6:
            total = self.join(n)
            half = self.half
            side = pl.ds(0 if n % 2 == 0 else half, half)
            self.out[n - 2].wait_recv()
            self.own[n] = total.astype(bf16)
            first = total[:half] if n % 2 == 0 else total[half:]
            self.own[n, side] = (first + self.halves[n - 2].astype(f32)).astype(bf16)
            self.out[n + 2].start()
        elif n == 6:
            total = self.join(6)
            for m in (0, 1):
                self.out[4 + m].wait_recv()
                total = total + self.wholes[m].astype(f32)
            self.own[6] = total.astype(bf16)
            self.out[8].start()
        else:
            total = self.join(7)
            for m in (2, 3):
                self.out[4 + m].wait_recv()
                total = total + self.wholes[m].astype(f32)
            self.out[8].wait_recv()
            return total + self.last[...].astype(f32)

    def finish(self):
        for copy in self.out + self.cross:
            copy.wait_send()


def scatter_kernel(p_ref, out_ref, *scratch):
    place = my_place()
    pl.semaphore_wait(greet(chip_neighbours(place)), 4)
    scatter = RowScatter(place, lambda chip, core: p_ref.at[chip, core], *scratch)
    for n in range(8):
        scatter.start(n)
    for n in range(7):
        scatter.step(n)
    out_ref[...] = scatter.step(7)
    scatter.finish()


def scatter_ctx(parts, number):
    rows, width = parts.shape[-2:]
    parts = parts.reshape(8, 2, rows, width)
    return pl.pallas_call(
        scatter_kernel,
        out_shape=jax.ShapeDtypeStruct((rows, width), f32),
        in_specs=[ANY],
        out_specs=VMEM,
        scratch_shapes=RowScatter.scratch(rows, width),
        compiler_params=pltpu.CompilerParams(
            collective_id=number, has_side_effects=True, vmem_limit_bytes=24 * 2**20
        ),
        name="scatter_rows",
    )(parts)


def entry_kernel(x_ref, w_ref, o_ref, m_ref, x_out, w_out, o_out, o_mid, *sems):
    row_sems, o_sems, rest = sems[:5], sems[5:10], sems[10:]
    wlocal, wsend, wrecv, psend, precv, olocal, osend, orecv = rest
    place = my_place()
    dp, ctx = dp_of(place), ctx_of(place)
    barrier = greet(
        [device_at(dp, lax.rem(ctx + k, N_CTX)) for k in range(1, N_CTX)]
        + [device_at(lax.rem(dp + k, N_DP), ctx) for k in range(1, N_DP)]
    )
    pl.semaphore_wait(barrier, 22)

    def o_place(k):
        return o_mid.at[pl.ds(pl.multiple_of(k * 16, 16), 16)]

    first, second, third = [], [], []
    for k in range(1, N_DP):
        to = lax.rem(dp + k, N_DP)
        third.append(remote(o_ref, o_place(dp), osend.at[k], orecv.at[k], device_at(to, ctx)))
        second.append(remote(w_out.at[dp], w_out.at[dp], psend.at[k], precv.at[k], device_at(to, ctx)))
    for k in range(1, N_CTX):
        to = lax.rem(ctx + k, N_CTX)
        first.append(
            remote(w_ref.at[to], w_out.at[dp, ctx], wsend.at[k], wrecv.at[k], device_at(dp, to))
        )
    for copy in third + first:
        copy.start()
    owns = [
        pltpu.make_async_copy(w_ref.at[ctx], w_out.at[dp, ctx], wlocal),
        pltpu.make_async_copy(o_ref, o_place(dp), olocal.at[0]),
        pltpu.make_async_copy(m_ref, o_mid.at[pl.ds(128, 32)], olocal.at[1]),
    ]
    for copy in owns:
        copy.start()
    rows = RowGather(place, x_ref, lambda p: x_out.at[ctx_of(p)], x_ref.shape[0] // 2, *row_sems)
    rows.start()
    for copy in owns:
        copy.wait()
    for copy in third:
        copy.wait_recv()
    outs = RowGather(place, o_mid, lambda p: o_out.at[ctx_of(p)], 80, *o_sems)
    outs.start()
    for copy in first:
        copy.wait_recv()
    for copy in second:
        copy.start()
    for n in range(9):
        rows.step(n)
        outs.step(n)
    rows.finish()
    outs.finish()
    for copy in second:
        copy.wait_recv()
    for copy in first + second + third:
        copy.wait_send()


def entry(x, w, o, m, number):
    return pl.pallas_call(
        entry_kernel,
        out_shape=(
            jax.ShapeDtypeStruct((N_CTX,) + x.shape, x.dtype),
            jax.ShapeDtypeStruct((N_DP,) + w.shape, w.dtype),
            jax.ShapeDtypeStruct((N_CTX, 160, 512), bf16),
        ),
        in_specs=[ANY] * 4,
        out_specs=(ANY, ANY, ANY),
        scratch_shapes=[pltpu.VMEM((160, 512), bf16)]
        + RowGather.scratch
        + RowGather.scratch
        + [DMA, DMA((16,)), DMA((16,)), DMA((8,)), DMA((8,)), DMA((2,)), DMA((8,)), DMA((8,))],
        compiler_params=pltpu.CompilerParams(collective_id=number, has_side_effects=True),
        name="entry_gather",
    )(x, w, o, m)


def grads_kernel(
    a_ref, b_ref, a_out, b_out, landed, part, wlocal, wsend, wrecv, psend, precv, olocal, osend, orecv, plocal
):
    place = my_place()
    dp, ctx = dp_of(place), ctx_of(place)
    barrier = greet(
        [device_at(dp, lax.rem(ctx + k, N_CTX)) for k in range(1, N_CTX)]
        + [device_at(lax.rem(dp + k, N_DP), ctx) for k in range(1, N_DP)]
    )
    o_ctx = 2 * dp + lax.div(ctx, 8)
    o_home = lax.div(ctx, 2)
    to_ctx = 8 * lax.rem(ctx, 2)
    o_self = o_ctx == ctx
    for k in range(8):
        here = jnp.logical_and(o_self, dp == k)

        @pl.when(jnp.logical_not(here))
        def _():
            pl.semaphore_signal(barrier, inc=1, device_id=device_at(k, o_ctx), device_id_type=MESH_ID)

    pl.semaphore_wait(barrier, 30 - jnp.where(o_self, 1, 0))

    first = []
    for k in range(1, N_DP):
        to = lax.rem(dp + k, N_DP)
        first.append(remote(a_ref.at[to], landed.at[k], wsend.at[k], wrecv.at[k], device_at(to, ctx)))
    for copy in first:
        copy.start()
    own = pltpu.make_async_copy(a_ref.at[dp], landed.at[0], wlocal)
    own.start()

    def o_copy(t):
        return remote(
            b_ref.at[t], b_out.at[dp], osend.at[t], orecv.at[dp], device_at(o_home, to_ctx + t)
        )

    o_own = pltpu.make_async_copy(b_ref.at[lax.rem(ctx, 8)], b_out.at[dp], olocal)
    for t in range(8):
        here = jnp.logical_and(o_home == dp, to_ctx + t == ctx)

        @pl.when(here)
        def _():
            o_own.start()

        @pl.when(jnp.logical_not(here))
        def _():
            o_copy(t).start()

    own.wait()
    total = landed[0].astype(f32)
    for copy in first:
        copy.wait_recv()
    for k in range(1, N_DP):
        total = total + landed[k].astype(f32)
    part[...] = total.reshape(part.shape)
    second = []
    for k in range(1, N_CTX):
        to = lax.rem(ctx + k, N_CTX)
        second.append(remote(part.at[to], a_out.at[ctx], psend.at[k], precv.at[k], device_at(dp, to)))
    for copy in second:
        copy.start()
    mine = pltpu.make_async_copy(part.at[ctx], a_out.at[ctx], plocal)
    mine.start()
    mine.wait()
    for copy in second:
        copy.wait_recv()
    for k in range(8):
        here = jnp.logical_and(o_self, dp == k)

        @pl.when(here)
        def _():
            o_own.wait()

        @pl.when(jnp.logical_not(here))
        def _():
            remote(b_ref.at[0], b_out.at[k], osend.at[0], orecv.at[k], device_at(dp, ctx)).wait_recv()

    for t in range(8):
        here = jnp.logical_and(o_home == dp, to_ctx + t == ctx)

        @pl.when(jnp.logical_not(here))
        def _():
            o_copy(t).wait_send()

    for copy in first + second:
        copy.wait_send()


def grads_out(a, b, number):
    width = a.shape[-1]
    return pl.pallas_call(
        grads_kernel,
        out_shape=(
            jax.ShapeDtypeStruct((N_CTX, 8, width), f32),
            jax.ShapeDtypeStruct((N_DP,) + b.shape[1:], f32),
        ),
        in_specs=[ANY] * 2,
        out_specs=(VMEM, VMEM),
        scratch_shapes=[pltpu.VMEM(a.shape, a.dtype), pltpu.VMEM((N_CTX, 8, width), f32)]
        + [DMA, DMA((8,)), DMA((8,)), DMA((16,)), DMA((16,)), DMA, DMA((8,)), DMA((8,)), DMA],
        compiler_params=pltpu.CompilerParams(
            collective_id=number, has_side_effects=True, vmem_limit_bytes=24 * 2**20
        ),
        name="sum_grads",
    )(a, b)


def experts_kernel(
    hid_ref, facts_ref, cot_ref, w_ref, out_ref, d_ref, g_ref, out_parts, d_parts,
    pool, facts_all, win, wide, picks, gate_slot, dg_slot, rows, tops, result, hidden, d_mid,
    stage, d_stage, in_sem, out_sem, d_sem, g_sem, *scatters,
):
    loads = [
        pltpu.make_async_copy(facts_ref, facts_all, in_sem.at[0]),
        pltpu.make_async_copy(hid_ref, pool.at[:, :, 0], in_sem.at[1]),
        pltpu.make_async_copy(w_ref, win, in_sem.at[2]),
    ]
    for load in loads:
        load.start()
    place = my_place()
    ctx = ctx_of(place)
    pl.semaphore_wait(greet(chip_neighbours(place)), 4)
    gather = RowGather(
        place, cot_ref, lambda p: pool.at[p[2] * 4 + p[3], p[4], 1], ROWS // 2, *scatters[20:]
    )
    gather.start()
    line = lax.broadcasted_iota(jnp.int32, (8, EXTRA), 0)
    lane = lax.broadcasted_iota(jnp.int32, (8, EXTRA), 1)
    start = jnp.where(line < 2, 64, jnp.where(line < 4, 0, 32))
    chosen = jnp.logical_and(line < 6, lane == start + 2 * ctx + lax.rem(line, 2))
    chosen = jnp.where(chosen, 1.0, 0.0).astype(bf16)
    back = jnp.logical_and(line < 4, lane == jnp.where(line < 2, 0, 32) + 2 * ctx + lax.rem(line, 2))
    back = jnp.where(back, 1.0, 0.0).astype(bf16)
    before = lax.broadcasted_iota(jnp.int32, (ROWS, ROWS), 0) < lax.broadcasted_iota(
        jnp.int32, (ROWS, ROWS), 1
    )
    before = jnp.where(before, 1.0, 0.0).astype(bf16)
    slots = lax.broadcasted_iota(jnp.int32, (MOST, ROWS), 0).astype(f32)
    for load in loads[:2]:
        load.wait()

    def pick(c, _):
        facts = dot_last(chosen, facts_all[c])
        order = dot(facts.astype(bf16), before)
        both = []
        here = pl.ds(pl.multiple_of(c * MOST, MOST), MOST)
        for e in range(2):
            member = facts[e : e + 1]
            onehot = jnp.where(jnp.logical_and(order[e : e + 1] == slots, member > 0.5), 1.0, 0.0)
            gate = facts[2 + e : 3 + e] + facts[4 + e : 5 + e]
            gate_slot[e, here] = jnp.sum(onehot * gate, axis=1, keepdims=True)
            both.append(onehot.astype(bf16))
        both = jnp.concatenate(both, axis=0)
        picks[c] = both
        taken = dot(both, pool[lax.div(c, 2), lax.rem(c, 2), 0]).astype(bf16)
        rows[0, here] = taken[:MOST]
        rows[1, here] = taken[MOST:]
        return 0

    lax.fori_loop(0, N_CTX, pick, 0)
    for n in range(3):
        gather.step(n)
    loads[2].wait()
    for e in range(2):
        for k in range(N_DP):
            for q in range(8):
                wide[e, q * 64 : (q + 1) * 64, k * ROWS : (k + 1) * ROWS] = win[
                    k, e, ROWS:, q * ROWS : (q + 1) * ROWS
                ]
    tile = 256

    def pick_tops(c, _):
        here = pl.ds(pl.multiple_of(c * MOST, MOST), MOST)
        taken = dot(picks[c], pool[lax.div(c, 2), lax.rem(c, 2), 1]).astype(bf16)
        tops[0, here] = taken[:MOST]
        tops[1, here] = taken[MOST:]
        return 0

    def forth(e, t):
        here = pl.ds(t * tile, tile)
        both = dot(rows[e, here], win[:, e, :ROWS].reshape(D, 2 * FF))
        gate_part, up_part = both[:, :FF], both[:, FF:]
        sigmoid = 1.0 / (1.0 + jnp.exp(-gate_part))
        silu = gate_part * sigmoid
        middle = (silu * up_part).astype(bf16)
        hidden[e, here] = middle
        d_mid[e, here, :FF] = (up_part * (sigmoid * (1.0 + gate_part * (1.0 - sigmoid)))).astype(bf16)
        d_mid[e, here, FF:] = silu.astype(bf16)
        result[e, here] = dot(middle, wide[e]).astype(bf16)

    def backward(e, t):
        here = pl.ds(t * tile, tile)
        top = tops[e, here].astype(f32)
        dg_slot[e, here] = jnp.sum(top * result[e, here].astype(f32), axis=1, keepdims=True)
        d_result = (top * gate_slot[e, here]).astype(bf16)
        tops[e, here] = d_result
        d_middle = dot_last(d_result, wide[e])
        d_mid[e, here, :FF] = (d_middle * d_mid[e, here, :FF].astype(f32)).astype(bf16)
        d_mid[e, here, FF:] = (d_middle * d_mid[e, here, FF:].astype(f32)).astype(bf16)
        weight = win[:, e, :ROWS].reshape(D, 2 * FF)
        result[e, here] = dot_last(d_mid[e, here], weight).astype(bf16)

    def combined(c, width, staged, out, sem, with_gates):
        here = pl.ds(pl.multiple_of(c * MOST, MOST), MOST)
        both = picks[c]
        slot = lax.rem(c, 2)

        @pl.when(c >= 2)
        def _():
            pltpu.make_async_copy(staged.at[slot], out.at[c], sem.at[slot]).wait()

        found = [result[0, here], result[1, here]]
        if not with_gates:
            found = [(found[e].astype(f32) * gate_slot[e, here]).astype(bf16) for e in range(2)]
        found = jnp.concatenate(found, axis=0)
        staged[slot, :, :D] = dot_first(both, found).astype(bf16)
        if with_gates:
            lines = [
                jnp.sum(
                    both[e * MOST : (e + 1) * MOST].astype(f32) * dg_slot[e, here], axis=0, keepdims=True
                )
                for e in range(2)
            ]
            high = [v.astype(bf16).astype(f32) for v in lines]
            rest = [v - h for v, h in zip(lines, high)]
            lines = jnp.concatenate(high + rest + [jnp.zeros((4, ROWS), f32)], axis=0).astype(bf16)
            staged[slot, :, D:] = dot_first(lines, back).astype(bf16)
        pltpu.make_async_copy(staged.at[slot], out.at[c], sem.at[slot]).start()

    def combine(staged, out, sem, with_gates):
        def one(c, _):
            combined(c, D, staged, out, sem, with_gates)
            return 0

        lax.fori_loop(0, N_CTX, one, 0)
        for slot in range(2):
            pltpu.make_async_copy(staged.at[slot], out.at[slot], sem.at[slot]).wait()

    def chips(ref):
        return lambda chip, core: ref.at[chip * 2 + core]

    for e in range(2):
        for t in range(3):
            forth(e, t)
            gather.step(3 + 3 * e + t)
    combine(stage, out_parts, out_sem, False)
    first = RowScatter(place, chips(out_parts), *scatters[:10])
    second = RowScatter(place, chips(d_parts), *scatters[10:20])
    for n in range(8):
        first.start(n)
    gather.finish()
    lax.fori_loop(0, N_CTX, pick_tops, 0)
    plan = [(), (0, 1), (), (2, 3), (), (4, 5)]
    for e in range(2):
        for t in range(3):
            backward(e, t)
            for n in plan[3 * e + t]:
                first.step(n)
    combine(d_stage, d_parts, d_sem, True)
    for n in range(8):
        second.start(n)
    first.step(6)
    out_ref[...] = first.step(7)

    def weights(e, k):
        here = pl.ds(k * 256, 256)
        total = dot_first(rows[e, :, here], d_mid[e]).astype(bf16)
        pool[2 * k, e, 0] = total[:ROWS]
        pool[2 * k + 1, e, 0] = total[ROWS:]
        total = dot_first(hidden[e], tops[e, :, here]).astype(bf16)
        for q in range(8):
            pool[2 * k, e, 1, :64, q * ROWS : (q + 1) * ROWS] = total[q * 64 : (q + 1) * 64, :ROWS]
            pool[2 * k + 1, e, 1, :64, q * ROWS : (q + 1) * ROWS] = total[q * 64 : (q + 1) * 64, ROWS:]

    plan = [(), (0, 1), (), (2, 3), (), (4, 5), (), ()]
    for e in range(2):
        for k in range(4):
            weights(e, k)
            for n in plan[4 * e + k]:
                second.step(n)
    saves = [
        pltpu.make_async_copy(pool.at[:, :, 0], g_ref.at[:, :, :ROWS], g_sem.at[0]),
        pltpu.make_async_copy(pool.at[:, :, 1, :64], g_ref.at[:, :, ROWS:], g_sem.at[1]),
    ]
    for save in saves:
        save.start()
    second.step(6)
    d_ref[...] = second.step(7)
    for save in saves:
        save.wait()
    first.finish()
    second.finish()


def experts(hid, facts, cot, weights, number):
    slots = N_CTX * MOST
    v = lambda *shape: pltpu.VMEM(shape, bf16)
    column = pltpu.VMEM((2, slots, 1), f32)
    blocks = (8, 2, ROWS, D)
    return pl.pallas_call(
        experts_kernel,
        out_shape=(
            jax.ShapeDtypeStruct((ROWS, D), f32),
            jax.ShapeDtypeStruct((ROWS, D + EXTRA), f32),
            jax.ShapeDtypeStruct(weights.shape, bf16),
            jax.ShapeDtypeStruct((N_CTX, ROWS, D), bf16),
            jax.ShapeDtypeStruct((N_CTX, ROWS, D + EXTRA), bf16),
        ),
        in_specs=[ANY] * 4,
        out_specs=(VMEM, VMEM, ANY, ANY, ANY),
        scratch_shapes=[
            v(8, 2, 2, ROWS, D),
            v(N_CTX, ROWS, EXTRA),
            v(*weights.shape),
            v(2, FF, D),
            v(N_CTX, 2 * MOST, ROWS),
            column,
            column,
            v(2, slots, D),
            v(2, slots, D),
            v(2, slots, D),
            v(2, slots, FF),
            v(2, slots, 2 * FF),
            v(2, ROWS, D),
            v(2, ROWS, D + EXTRA),
            DMA((3,)),
            DMA((2,)),
            DMA((2,)),
            DMA((2,)),
        ]
        + RowScatter.scratch(ROWS, D)
        + RowScatter.scratch(ROWS, D + EXTRA)
        + RowGather.scratch,
        compiler_params=pltpu.CompilerParams(
            collective_id=number, has_side_effects=True, vmem_limit_bytes=61 * 2**20
        ),
        cost_estimate=pl.CostEstimate(flops=15 * 10**9, bytes_accessed=30 * 2**20, transcendentals=2**20),
        name="experts_both_ways",
    )(hid.reshape(blocks), facts, cot, weights)


def swap_halves(u):
    lane = lax.broadcasted_iota(jnp.int32, u.shape, 1)
    return jnp.where(lax.rem(lane, 64) < 32, pltpu.roll(u, 96, 1), pltpu.roll(u, 32, 1))


def attend_kernel(
    src, order, raw_ref, cos_ref, sin_ref, o_ref, padded, q_ref, k_ref, v_ref, lse_ref, out_nat
):
    core = lax.axis_index("core")
    for b in range(SEQ // BLOCK):
        rows = pl.ds(pl.multiple_of(src[b] * BLOCK, BLOCK), BLOCK)
        here = pl.ds(b * BLOCK, BLOCK)
        qk = raw_ref[rows, 0:128]
        qk = qk * cos_ref[here, :] + swap_halves(qk) * sin_ref[here, :]
        q_ref[here, :] = (qk[:, 0:64]).astype(bf16)
        k_ref[here, :] = (qk[:, 64:128]).astype(bf16)
        v_ref[here, :] = raw_ref[rows, 128:192].astype(bf16)
    step = 256
    for i in range(SEQ // step):
        length = (i + 1) * step
        here = pl.ds(i * step, step)
        scores = dot_last(q_ref[here, :], k_ref[0:length, :]) * 0.125
        row = i * step + lax.broadcasted_iota(jnp.int32, (step, length), 0)
        column = lax.broadcasted_iota(jnp.int32, (step, length), 1)
        scores = jnp.where(column <= row, scores, -1e30)
        top = jnp.max(scores, axis=1, keepdims=True)
        weights = jnp.exp(scores - top)
        total = jnp.sum(weights, axis=1, keepdims=True)
        lse_ref[here, :] = top + jnp.log(total)
        probs = (weights * (1.0 / total)).astype(bf16)
        out_nat[here, :] = dot(probs, v_ref[0:length, :])
    for b in range(SEQ // BLOCK):
        rows = pl.ds(pl.multiple_of(order[b] * BLOCK, BLOCK), BLOCK)
        here = pl.ds(b * BLOCK, BLOCK)
        out = out_nat[rows, :].astype(bf16)
        o_ref[here, :] = out
        empty = jnp.zeros_like(out)
        padded[here, :] = jnp.where(
            core == 0, jnp.concatenate([out, empty], axis=1), jnp.concatenate([empty, out], axis=1)
        )


def attend(src, order, raw, cosine, sine):
    head = jax.ShapeDtypeStruct((SEQ, HEAD_DIM), bf16)
    return pl.pallas_call(
        attend_kernel,
        out_shape=(
            head,
            jax.ShapeDtypeStruct((SEQ, 128), bf16),
            head,
            head,
            head,
            jax.ShapeDtypeStruct((SEQ, 1), f32),
        ),
        in_specs=[SMEM, SMEM, VMEM, VMEM, VMEM],
        out_specs=(VMEM,) * 6,
        scratch_shapes=[pltpu.VMEM((SEQ, HEAD_DIM), f32)],
        compiler_params=pltpu.CompilerParams(vmem_limit_bytes=48 * 2**20),
        cost_estimate=pl.CostEstimate(flops=10**9, bytes_accessed=6 * 2**20, transcendentals=2**21),
        name="attention_forward",
    )(src, order, raw, cosine, sine)


def heads_kernel(padded, att_out, mine, other, merged, msem, xsend, xrecv, *sems):
    place = my_place()
    core = place[4]
    pl.semaphore_wait(greet(chip_neighbours(place)), 4)
    half = SEQ // 2
    swap = remote(
        padded.at[pl.ds(pl.multiple_of((1 - core) * half, half), half)], other, xsend, xrecv,
        sibling_of(place),
    )
    swap.start()
    own = pltpu.make_async_copy(padded.at[pl.ds(pl.multiple_of(core * half, half), half)], mine, msem)
    own.start()
    own.wait()
    swap.wait_recv()
    merged[...] = mine[...] + other[...]

    def view(p):
        chip = p[2] * 4 + p[3]
        return att_out.at[
            pl.ds(pl.multiple_of(p[4] * half, half), half), pl.ds(pl.multiple_of(chip * 128, 128), 128)
        ]

    heads = RowGather(place, merged, view, half // 2, *sems)
    heads.start()
    heads.pass_on()
    heads.finish()
    swap.wait_send()


def gather_heads(padded, number):
    return pl.pallas_call(
        heads_kernel,
        out_shape=jax.ShapeDtypeStruct((SEQ, D), bf16),
        in_specs=[ANY],
        out_specs=ANY,
        scratch_shapes=[pltpu.VMEM((SEQ // 2, 128), bf16)] * 3 + [DMA] * 3 + RowGather.scratch,
        compiler_params=pltpu.CompilerParams(collective_id=number, has_side_effects=True),
        name="gather_heads",
    )(padded)


def attend_back_kernel(
    src, order, q_ref, k_ref, v_ref, lse_ref, do_ref, cos_ref, sin_ref, out_ref, do_nat, acc, done
):
    for b in range(SEQ // BLOCK):
        rows = pl.ds(pl.multiple_of(src[b] * BLOCK, BLOCK), BLOCK)
        do_nat[pl.ds(b * BLOCK, BLOCK), :] = do_ref[rows, :]
    acc[...] = jnp.zeros_like(acc)
    step = 256
    for i in range(SEQ // step):
        length = (i + 1) * step
        here = pl.ds(i * step, step)
        query, d_out = q_ref[here, :], do_nat[here, :].astype(bf16)
        keys = k_ref[0:length, :]
        scores = dot_last(query, keys) * 0.125
        row = i * step + lax.broadcasted_iota(jnp.int32, (step, length), 0)
        column = lax.broadcasted_iota(jnp.int32, (step, length), 1)
        probs = jnp.where(column <= row, jnp.exp(scores - lse_ref[here, :]), 0.0)
        d_probs = dot_last(d_out, v_ref[0:length, :])
        delta = jnp.sum(probs * d_probs, axis=1, keepdims=True)
        d_scores = (probs * (d_probs - delta)).astype(bf16)
        acc[here, 0:64] = dot(d_scores, keys) * 0.125
        acc[0:length, 64:128] += dot_first(d_scores, query) * 0.125
        acc[0:length, 128:192] += dot_first(probs.astype(bf16), d_out)
    for b in range(SEQ // BLOCK):
        here = pl.ds(b * BLOCK, BLOCK)
        qk = acc[here, 0:128]
        qk = qk * cos_ref[here, :] - swap_halves(qk) * sin_ref[here, :]
        done[here, 0:128] = qk
        done[here, 128:256] = acc[here, 128:256]
    for b in range(SEQ // BLOCK):
        rows = pl.ds(pl.multiple_of(order[b] * BLOCK, BLOCK), BLOCK)
        out_ref[pl.ds(b * BLOCK, BLOCK), :] = done[rows, :].astype(bf16)


def attend_back(src, order, q, k, v, lse, d_out, cosine, sine):
    return pl.pallas_call(
        attend_back_kernel,
        out_shape=jax.ShapeDtypeStruct((SEQ, 256), bf16),
        in_specs=[SMEM, SMEM] + [VMEM] * 7,
        out_specs=VMEM,
        scratch_shapes=[
            pltpu.VMEM((SEQ, HEAD_DIM), f32),
            pltpu.VMEM((SEQ, 256), f32),
            pltpu.VMEM((SEQ, 256), f32),
        ],
        compiler_params=pltpu.CompilerParams(vmem_limit_bytes=56 * 2**20),
        cost_estimate=pl.CostEstimate(flops=3 * 10**9, bytes_accessed=6 * 2**20, transcendentals=2**21),
        name="attention_backward",
    )(src, order, q, k, v, lse, d_out, cosine, sine)


def rotary_tables():
    inverse = 10000.0 ** (-np.arange(32, dtype=np.float64) * 2.0 / HEAD_DIM)
    angles = np.arange(SEQ, dtype=np.float64)[:, None] * inverse[None, :]
    cosine, sine = np.cos(angles), np.sin(angles)
    return (
        np.tile(cosine, (1, 4)).astype(np.float32),
        np.concatenate([-sine, sine, -sine, sine], axis=1).astype(np.float32),
    )


def normalize(inputs, gain_values):
    scale_rows = lax.rsqrt(jnp.mean(inputs * inputs, axis=-1, keepdims=True) + epsilon)
    normed = inputs * scale_rows
    return (scale_rows, normed, (normed * gain_values.astype(f32)).astype(bf16))


def norm_backward(grad_in, normed, scale_rows, gain_values):
    grad_normed = grad_in * gain_values.astype(f32)
    inner = jnp.mean(grad_normed * normed, axis=-1, keepdims=True)
    return (scale_rows * (grad_normed - normed * inner), jnp.sum(grad_in * normed, axis=0))


def halves(value):
    high = lax.reduce_precision(value, 8, 7)
    return high.astype(bf16), (value - high).astype(bf16)


def local(
    tokens,
    cotangent,
    block_order,
    routes,
    norm_one,
    w_query,
    w_key,
    w_value,
    w_out,
    norm_two,
    w_router,
    expert_in,
    expert_out,
):
    ctx = lax.axis_index(CTX)
    cosine, sine = (jnp.asarray(t) for t in rotary_tables())
    order = jnp.stack([block_order, 2 * N_CTX - 1 - block_order], axis=1).reshape(-1)
    spots = jnp.arange(2 * N_CTX, dtype=jnp.int32)
    src = jnp.sum(jnp.where(order[None, :] == spots[:, None], spots[None, :], 0), axis=1)

    by_head = lambda w, heads: jnp.moveaxis(w.reshape(8, heads, HEAD_DIM), 1, 0)
    query_part = by_head(w_query, HEADS)
    key_part = jnp.repeat(by_head(w_key, KV_HEADS), 2, axis=0)
    value_part = jnp.repeat(by_head(w_value, KV_HEADS), 2, axis=0)
    small = jnp.concatenate(
        [w_router, norm_one[:, None], norm_two[:, None], jnp.zeros((8, 30), bf16)], axis=1
    )
    small = jnp.broadcast_to(small[None], (N_CTX, 8, 64))
    packed = jnp.concatenate(
        [
            jnp.concatenate([query_part, key_part], axis=2),
            jnp.concatenate([value_part, small], axis=2),
        ],
        axis=1,
    )
    names = jnp.arange(EXPERTS, dtype=jnp.int32)
    member = jnp.any(routes[:, :, None] == names[None, None, :], axis=1).astype(bf16)
    member = jnp.pad(member.reshape(8, 512), ((0, 24), (0, 0)))
    tokens_all, packed_all, out_all = entry(tokens, packed, w_out.reshape(16, 512), member, 0)
    down_packed = expert_out.reshape(2, 8, 64, ROWS).swapaxes(1, 2).reshape(2, 64, D)
    expert_all = lax.all_gather(jnp.concatenate([expert_in, down_packed], axis=1), DP, axis=0)
    low = packed_all[:, :, 8:, :].reshape(D, 128)
    weight = jnp.concatenate(
        [packed_all[:, :, :8, :].reshape(D, 128), low[:, :64], jnp.zeros((D, 64), bf16)], axis=1
    )
    router_weight, gain_one, gain_two = low[:, 64:96], low[:, 96], low[:, 97]
    out_weight = out_all[:, :128].reshape(N_CTX, N_DP, 8, D).swapaxes(0, 1).reshape(D, D)
    head_weight = lax.dynamic_slice_in_dim(out_weight, ctx * HEAD_DIM, HEAD_DIM, axis=0)
    member = out_all[:, 128:136].reshape(SEQ, EXPERTS)

    tokens_float = tokens.astype(f32)
    scale_one, normed_one, _ = normalize(tokens_float, gain_one)
    _, _, hidden_one = normalize(tokens_all.reshape(SEQ, D).astype(f32), gain_one)
    raw = dot(hidden_one, weight)
    attended, padded, query, key, value, lse = attend(src, order, raw, cosine, sine)
    attended_all = gather_heads(padded, 1)
    residual_all = tokens_all.reshape(SEQ, D).astype(f32) + dot(attended_all, out_weight)
    own = lambda v: lax.dynamic_slice_in_dim(v, ctx * ROWS, ROWS, axis=0)

    _, _, hidden_all = normalize(residual_all, gain_two)
    logits = dot(hidden_all, router_weight)
    inside = member > 0.5
    picked = jnp.where(inside, logits, -1e30)
    shifted = jnp.where(inside, jnp.exp(picked - jnp.max(picked, axis=1, keepdims=True)), 0.0)
    gates_all = shifted / jnp.sum(shifted, axis=1, keepdims=True)
    high, rest = halves(gates_all)
    facts = jnp.concatenate([high, rest, member, jnp.zeros((SEQ, EXTRA - 96), bf16)], axis=1)
    residual = own(residual_all)
    scale_two, normed_two, _ = normalize(residual, gain_two)
    gates = own(gates_all)

    out_sum, d_sum, grad_experts, _, _ = experts(
        hidden_all, facts.reshape(N_CTX, ROWS, EXTRA), cotangent, expert_all, 3
    )
    output = residual + out_sum
    grad_experts = lax.psum_scatter(grad_experts, DP, scatter_dimension=0).astype(f32)
    grad_in = grad_experts[:, :ROWS]
    grad_down = grad_experts[:, ROWS:].reshape(2, 64, 8, ROWS).swapaxes(1, 2).reshape(2, FF, ROWS)

    grad_top = cotangent.astype(f32)
    d_gates = d_sum[:, D : D + 32] + d_sum[:, D + 32 : D + 64]
    d_picked = gates * (d_gates - jnp.sum(gates * d_gates, axis=1, keepdims=True))
    d_logits = d_picked.astype(bf16)
    d_hidden_two = d_sum[:, :D] + dot_last(d_logits, router_weight)
    d_norm_two, grad_gain_two = norm_backward(d_hidden_two, normed_two, scale_two, gain_two)
    d_residual = grad_top + d_norm_two
    sent = jnp.concatenate(
        [d_residual.astype(bf16), d_logits, jnp.zeros((ROWS, EXTRA - 32), bf16)], axis=1
    )
    all_three = gather_ctx(sent, 5).reshape(SEQ, D + EXTRA)
    d_branch = all_three[:, :D]
    d_logits_all = all_three[:, D : D + 32]

    d_attended = dot_last(d_branch, head_weight).astype(bf16).astype(f32)
    d_raw = attend_back(src, order, query, key, value, lse, d_attended, cosine, sine)
    d_one = dot_last(d_raw, weight).astype(bf16).reshape(N_CTX, ROWS, D)
    d_hidden_one = scatter_ctx(d_one, 6)
    d_norm_one, grad_gain_one = norm_backward(d_hidden_one, normed_one, scale_one, gain_one)
    input_grad = d_residual + d_norm_one

    grad_out_weight = dot_first(attended, d_branch)
    own_columns = lax.dynamic_slice_in_dim(hidden_all, ctx * 64, 64, axis=1)
    grad_router = dot_first(own_columns, d_logits_all)
    second = jnp.concatenate(
        [grad_out_weight, grad_router, jnp.zeros((64, EXTRA - 32), f32)], axis=1
    ).reshape(8, 8, D + EXTRA)
    grad_heads = dot_first(hidden_one, d_raw)
    first = jnp.concatenate(
        [
            grad_heads[:, :192],
            grad_gain_one[:, None],
            grad_gain_two[:, None],
            jnp.zeros((D, 62), f32),
        ],
        axis=1,
    ).astype(bf16)
    a, b = grads_out(first.reshape(N_DP, ROWS, 256), second, 7)
    b = jnp.sum(b, axis=0)
    side = lambda v: jnp.moveaxis(v, 0, 1).reshape(8, -1)
    pairs = a.reshape(KV_HEADS, 2, 8, 256).sum(axis=1)
    gains = jnp.sum(a[:, :, 192:194], axis=0)
    return (
        output,
        input_grad,
        gains[:, 0],
        side(a[:, :, 0:64]),
        side(pairs[:, :, 64:128]),
        side(pairs[:, :, 128:192]),
        b[:, :D],
        gains[:, 1],
        b[:, D : D + 32],
        grad_in,
        grad_down,
    )


def solution(mesh):
    split = Mesh(mesh.devices.reshape(2, 4, 2, 4, 2), AXES)
    rows = P(AXES, None)
    line = P(AXES)
    return jax.shard_map(
        local,
        mesh=split,
        in_specs=(
            rows,
            rows,
            P(),
            rows,
            line,
            rows,
            rows,
            rows,
            rows,
            line,
            rows,
            P(CTX, DP, None),
            P(CTX, None, DP),
        ),
        out_specs=(
            rows,
            rows,
            line,
            rows,
            rows,
            rows,
            rows,
            line,
            rows,
            P(CTX, DP, None),
            P(CTX, None, DP),
        ),
        check_vma=False,
    )
```

```python
import functools
import math

import jax
import jax.numpy as jnp
import numpy as np
from jax import lax
from jax.experimental import pallas as pl
from jax.experimental.pallas import tpu as pltpu
from jax.sharding import Mesh
from jax.sharding import PartitionSpec as P

D = 1024
HEADS = 16
KV_HEADS = 8
HEAD_DIM = 64
EXPERTS = 32
FF = 512
TOP = 8
MOST = 48
ROWS = 128
SEQ = 2048
BLOCK = 64
AXES = ("ylo", "z", "yhi", "x", "core")
DP = ("ylo", "z")
CTX = ("yhi", "x", "core")
N_DP = 8
N_CTX = 16
EXTRA = 128
MESH_ID = pl.DeviceIdType.MESH
ANY = pl.BlockSpec(memory_space=pl.ANY)
VMEM = pl.BlockSpec(memory_space=pltpu.VMEM)
SMEM = pl.BlockSpec(memory_space=pltpu.SMEM)
DMA = pltpu.SemaphoreType.DMA
bf16 = jnp.bfloat16
f32 = jnp.float32
epsilon = 1e-06


def dot(a, b):
    return jnp.dot(a, b, preferred_element_type=f32)


def dot_last(a, b):
    return lax.dot_general(a, b, (((1,), (1,)), ((), ())), preferred_element_type=f32)


def dot_first(a, b):
    return lax.dot_general(a, b, (((0,), (0,)), ((), ())), preferred_element_type=f32)


def my_place():
    return tuple(lax.axis_index(a) for a in AXES)


def device_at(dp, ctx):
    return (
        lax.div(dp, 4),
        lax.rem(dp, 4),
        lax.div(ctx, 8),
        lax.rem(lax.div(ctx, 2), 4),
        lax.rem(ctx, 2),
    )


def beside(place, dy, dx):
    ylo, z, yhi, x, core = place
    return (ylo, z, lax.rem(yhi + dy, 2), lax.rem(x + dx, 4), core)


def ctx_of(place):
    return place[2] * 8 + place[3] * 2 + place[4]


def dp_of(place):
    return place[0] * 4 + place[1]


def sibling_of(place):
    return place[:4] + (1 - place[4],)


def remote(src, dst, send, recv, device):
    return pltpu.make_async_remote_copy(
        src_ref=src, dst_ref=dst, send_sem=send, recv_sem=recv, device_id=device, device_id_type=MESH_ID
    )


def greet(devices):
    barrier = pltpu.get_barrier_semaphore()
    for device in devices:
        pl.semaphore_signal(barrier, inc=1, device_id=device, device_id_type=MESH_ID)
    return barrier


class RowGather:
    scratch = [DMA, DMA((9,)), DMA((9,)), DMA((10,)), DMA((10,))]
    links = [(1, 0), (0, 1), (0, 3), (0, 1), (0, 3), (0, 1), (0, 3), (0, 1), (0, 3)]
    held = [(0, 0), (0, 0), (0, 0), (1, 0), (1, 0), (0, 3), (0, 1), (1, 3), (1, 1)]
    parts = [None, None, None, None, None, 0, 1, 0, 1]
    after = {0: (3, 4), 1: (5,), 2: (6,), 3: (7,), 4: (8,)}

    def __init__(self, place, x_ref, view, half, local, send, recv, fsend, frecv):
        sibling = sibling_of(place)

        def piece(dy, dx, part):
            ref = view(beside(place, dy, dx))
            return ref if part is None else ref.at[pl.ds(part * half, half)]

        self.own = pltpu.make_async_copy(x_ref, view(place), local)
        self.out, self.landed, self.passed = [], [], []
        for n, ((ly, lx), (hy, hx), part) in enumerate(zip(self.links, self.held, self.parts)):
            source = x_ref if n < 3 else piece(hy, hx, part)
            self.out.append(
                remote(source, piece(hy, hx, part), send.at[n], recv.at[n], beside(place, ly, lx))
            )
            here = piece((hy + ly) % 2, (hx + 4 - lx) % 4, part)
            self.landed.append(remote(here, here, send.at[n], recv.at[n], beside(place, ly, lx)))
            self.passed.append(remote(here, here, fsend.at[n], frecv.at[n], sibling))
        self.passed.append(remote(x_ref, view(place), fsend.at[9], frecv.at[9], sibling))
        self.back = []
        for n in range(9):
            (ly, lx), (hy, hx), part = self.links[n], self.held[n], self.parts[n]
            ref = view(sibling_of(beside(place, (hy + ly) % 2, (hx + 4 - lx) % 4)))
            ref = ref if part is None else ref.at[pl.ds(part * half, half)]
            self.back.append(remote(ref, ref, fsend.at[n], frecv.at[n], sibling))
        ref = view(sibling)
        self.back.append(remote(ref, ref, fsend.at[9], frecv.at[9], sibling))

    def start(self):
        for n in range(3):
            self.out[n].start()
        self.passed[9].start()
        self.own.start()

    def step(self, n):
        self.landed[n].wait_recv()
        for m in self.after.get(n, ()):
            self.out[m].start()
        self.passed[n].start()

    def pass_on(self):
        for n in range(9):
            self.step(n)

    def finish(self):
        self.own.wait()
        for n in range(10):
            self.back[n].wait_recv()
        for copy in self.out + self.passed:
            copy.wait_send()


def chip_neighbours(place):
    return [beside(place, 1, 0), beside(place, 0, 1), beside(place, 0, 3), sibling_of(place)]


def gather_kernel(x_ref, out_ref, *sems):
    place = my_place()
    pl.semaphore_wait(greet(chip_neighbours(place)), 4)
    gather = RowGather(place, x_ref, lambda p: out_ref.at[ctx_of(p)], x_ref.shape[0] // 2, *sems)
    gather.start()
    gather.pass_on()
    gather.finish()


def gather_ctx(x, number):
    return pl.pallas_call(
        gather_kernel,
        out_shape=jax.ShapeDtypeStruct((N_CTX,) + x.shape, x.dtype),
        in_specs=[ANY],
        out_specs=ANY,
        scratch_shapes=RowGather.scratch,
        compiler_params=pltpu.CompilerParams(collective_id=number, has_side_effects=True),
        name="gather_rows",
    )(x)


SPREAD = [(1, 2), (0, 2), (1, 1), (1, 3), (0, 1), (0, 3), (1, 0), (0, 0)]


class RowScatter:
    @staticmethod
    def scratch(rows, width):
        return [
            pltpu.VMEM((8, rows, width), bf16),
            pltpu.VMEM((8, rows, width), bf16),
            pltpu.VMEM((4, rows // 2, width), bf16),
            pltpu.VMEM((4, rows, width), bf16),
            pltpu.VMEM((rows, width), bf16),
            DMA((8,)),
            DMA((8,)),
            DMA((8,)),
            DMA((9,)),
            DMA((9,)),
        ]

    def __init__(self, place, part, own, other, halves, wholes, last, own_sem, fsend, frecv, send, recv):
        self.own, self.other, self.halves, self.wholes, self.last = own, other, halves, wholes, last
        core = place[4]
        half = own.shape[1] // 2
        self.half = half
        self.mine, self.cross = [], []
        for n, (dy, dx) in enumerate(SPREAD):
            chip = lax.div(ctx_of(beside(place, dy, dx)), 2)
            self.mine.append(pltpu.make_async_copy(part(chip, core), own.at[n], own_sem.at[n]))
            self.cross.append(
                remote(part(chip, 1 - core), other.at[n], fsend.at[n], frecv.at[n], sibling_of(place))
            )
        right, left = beside(place, 0, 1), beside(place, 0, 3)
        self.out = []
        for n, (source, target, device) in enumerate(
            [
                (own.at[0, pl.ds(0, half)], halves.at[0], right),
                (own.at[0, pl.ds(half, half)], halves.at[1], left),
                (own.at[1, pl.ds(0, half)], halves.at[2], right),
                (own.at[1, pl.ds(half, half)], halves.at[3], left),
                (own.at[2], wholes.at[0], right),
                (own.at[3], wholes.at[1], left),
                (own.at[4], wholes.at[2], right),
                (own.at[5], wholes.at[3], left),
                (own.at[6], last, beside(place, 1, 0)),
            ]
        ):
            self.out.append(remote(source, target, send.at[n], recv.at[n], device))

    def start(self, n):
        self.cross[n].start()
        self.mine[n].start()

    def join(self, n):
        self.mine[n].wait()
        self.cross[n].wait_recv()
        return self.own[n].astype(f32) + self.other[n].astype(f32)

    def step(self, n):
        if n < 2:
            self.own[n] = self.join(n).astype(bf16)
            self.out[2 * n].start()
            self.out[2 * n + 1].start()
        elif n < 6:
            total = self.join(n)
            half = self.half
            side = pl.ds(0 if n % 2 == 0 else half, half)
            self.out[n - 2].wait_recv()
            self.own[n] = total.astype(bf16)
            first = total[:half] if n % 2 == 0 else total[half:]
            self.own[n, side] = (first + self.halves[n - 2].astype(f32)).astype(bf16)
            self.out[n + 2].start()
        elif n == 6:
            total = self.join(6)
            for m in (0, 1):
                self.out[4 + m].wait_recv()
                total = total + self.wholes[m].astype(f32)
            self.own[6] = total.astype(bf16)
            self.out[8].start()
        else:
            total = self.join(7)
            for m in (2, 3):
                self.out[4 + m].wait_recv()
                total = total + self.wholes[m].astype(f32)
            self.out[8].wait_recv()
            return total + self.last[...].astype(f32)

    def finish(self):
        for copy in self.out + self.cross:
            copy.wait_send()


def scatter_kernel(p_ref, out_ref, *scratch):
    place = my_place()
    pl.semaphore_wait(greet(chip_neighbours(place)), 4)
    scatter = RowScatter(place, lambda chip, core: p_ref.at[chip, core], *scratch)
    for n in range(8):
        scatter.start(n)
    for n in range(7):
        scatter.step(n)
    out_ref[...] = scatter.step(7)
    scatter.finish()


def scatter_ctx(parts, number):
    rows, width = parts.shape[-2:]
    parts = parts.reshape(8, 2, rows, width)
    return pl.pallas_call(
        scatter_kernel,
        out_shape=jax.ShapeDtypeStruct((rows, width), f32),
        in_specs=[ANY],
        out_specs=VMEM,
        scratch_shapes=RowScatter.scratch(rows, width),
        compiler_params=pltpu.CompilerParams(
            collective_id=number, has_side_effects=True, vmem_limit_bytes=24 * 2**20
        ),
        name="scatter_rows",
    )(parts)


def entry_kernel(
    x_ref, q_ref, k_ref, v_ref, small_ref, o_ref, routes_ref, x_out, w_out, o_out, m_out,
    w_pack, o_pad, o_other, o_mid, m_pack, *sems,
):
    row_sems, o_sems, m_sems, rest = sems[:5], sems[5:10], sems[10:15], sems[15:]
    wlocal, wsend, wrecv, psend, precv, xsend, xrecv, osend, orecv = rest
    place = my_place()
    core = place[4]
    dp, ctx = dp_of(place), ctx_of(place)
    barrier = greet(
        [device_at(dp, lax.rem(ctx + k, N_CTX)) for k in range(1, N_CTX)]
        + [device_at(lax.rem(dp + k, N_DP), ctx) for k in range(1, N_DP)]
    )
    pl.semaphore_wait(barrier, 22)
    rows = RowGather(place, x_ref, lambda p: x_out.at[ctx_of(p)], x_ref.shape[0] // 2, *row_sems)
    rows.start()

    out = o_ref[...].astype(f32)
    empty = jnp.zeros_like(out)
    out = jnp.where(core == 0, jnp.concatenate([out, empty], 0), jnp.concatenate([empty, out], 0))
    for s in range(2):
        o_pad[s] = out[:, s * 512 : (s + 1) * 512].astype(bf16)
    swap = remote(o_pad.at[1 - core], o_other, xsend, xrecv, sibling_of(place))
    swap.start()
    query, key, value = (r[...].astype(f32) for r in (q_ref, k_ref, v_ref))
    small = small_ref[...].astype(f32)
    for h in range(HEADS):
        at, pair = slice(h * 64, h * 64 + 64), slice(h // 2 * 64, h // 2 * 64 + 64)
        top = jnp.concatenate([query[:, at], key[:, pair]], axis=1)
        low = jnp.concatenate([value[:, pair], small], axis=1)
        w_pack[h] = jnp.concatenate([top, low], axis=0).astype(bf16)
    first, second, third = [], [], []
    for k in range(1, N_CTX):
        to = lax.rem(ctx + k, N_CTX)
        first.append(
            remote(w_pack.at[to], w_out.at[dp, ctx], wsend.at[k], wrecv.at[k], device_at(dp, to))
        )
    for k in range(1, N_DP):
        device = device_at(lax.rem(dp + k, N_DP), ctx)
        third.append(remote(o_mid.at[dp], o_mid.at[dp], osend.at[k], orecv.at[k], device))
        second.append(remote(w_out.at[dp], w_out.at[dp], psend.at[k], precv.at[k], device))
    for copy in first:
        copy.start()
    own = pltpu.make_async_copy(w_pack.at[ctx], w_out.at[dp, ctx], wlocal)
    own.start()
    swap.wait_recv()
    o_mid[dp] = o_pad[core] + o_other[...]
    for copy in third:
        copy.start()
    routes = routes_ref[...]
    lane = lax.broadcasted_iota(jnp.int32, (ROWS, EXTRA), 1) - 64
    member = jnp.zeros((ROWS, EXTRA), f32)
    for k in range(TOP):
        member = jnp.where(lane == routes[:, k : k + 1], 1.0, member)
    m_pack[...] = member.astype(bf16)
    members = RowGather(place, m_pack, lambda p: m_out.at[ctx_of(p)], ROWS // 2, *m_sems)
    members.start()
    own.wait()
    for copy in first:
        copy.wait_recv()
    for copy in second:
        copy.start()
    for copy in third:
        copy.wait_recv()

    def o_view(p):
        return o_out.at[:, p[2] * 4 + p[3], :, pl.ds(pl.multiple_of(p[4] * 512, 512), 512)]

    outs = RowGather(place, o_mid, o_view, 4, *o_sems)
    outs.start()
    for n in range(5):
        rows.step(n)
    for n in range(9):
        members.step(n)
    for n in range(3):
        outs.step(n)
    for n in range(5, 9):
        rows.step(n)
    for n in range(3, 9):
        outs.step(n)
    rows.finish()
    members.finish()
    outs.finish()
    for copy in second:
        copy.wait_recv()
    swap.wait_send()
    for copy in first + second + third:
        copy.wait_send()


def entry(x, query, key, value, small, out, routes, number):
    return pl.pallas_call(
        entry_kernel,
        out_shape=(
            jax.ShapeDtypeStruct((N_CTX,) + x.shape, bf16),
            jax.ShapeDtypeStruct((N_DP, N_CTX, 16, 128), bf16),
            jax.ShapeDtypeStruct((N_DP, 8, 16, D), bf16),
            jax.ShapeDtypeStruct((N_CTX, ROWS, EXTRA), bf16),
        ),
        in_specs=[ANY] + [VMEM] * 6,
        out_specs=(ANY,) * 4,
        scratch_shapes=[
            pltpu.VMEM((N_CTX, 16, 128), bf16),
            pltpu.VMEM((2, 16, 512), bf16),
            pltpu.VMEM((16, 512), bf16),
            pltpu.VMEM((N_DP, 16, 512), bf16),
            pltpu.VMEM((ROWS, EXTRA), bf16),
        ]
        + RowGather.scratch * 3
        + [DMA, DMA((16,)), DMA((16,)), DMA((8,)), DMA((8,)), DMA, DMA, DMA((8,)), DMA((8,))],
        compiler_params=pltpu.CompilerParams(
            collective_id=number, has_side_effects=True, vmem_limit_bytes=16 * 2**20
        ),
        name="entry_gather",
    )(x, query, key, value, small, out, routes)


def grads_kernel(
    a_ref, b_ref, a_out, b_out, landed, part, wlocal, wsend, wrecv, psend, precv, olocal, osend, orecv, plocal
):
    place = my_place()
    dp, ctx = dp_of(place), ctx_of(place)
    barrier = greet(
        [device_at(dp, lax.rem(ctx + k, N_CTX)) for k in range(1, N_CTX)]
        + [device_at(lax.rem(dp + k, N_DP), ctx) for k in range(1, N_DP)]
    )
    o_ctx = 2 * dp + lax.div(ctx, 8)
    o_home = lax.div(ctx, 2)
    to_ctx = 8 * lax.rem(ctx, 2)
    o_self = o_ctx == ctx
    for k in range(8):
        here = jnp.logical_and(o_self, dp == k)

        @pl.when(jnp.logical_not(here))
        def _():
            pl.semaphore_signal(barrier, inc=1, device_id=device_at(k, o_ctx), device_id_type=MESH_ID)

    pl.semaphore_wait(barrier, 30 - jnp.where(o_self, 1, 0))

    first = []
    for k in range(1, N_DP):
        to = lax.rem(dp + k, N_DP)
        first.append(remote(a_ref.at[to], landed.at[k], wsend.at[k], wrecv.at[k], device_at(to, ctx)))
    for copy in first:
        copy.start()
    own = pltpu.make_async_copy(a_ref.at[dp], landed.at[0], wlocal)
    own.start()

    def o_copy(t):
        return remote(
            b_ref.at[t], b_out.at[dp], osend.at[t], orecv.at[dp], device_at(o_home, to_ctx + t)
        )

    o_own = pltpu.make_async_copy(b_ref.at[lax.rem(ctx, 8)], b_out.at[dp], olocal)
    for t in range(8):
        here = jnp.logical_and(o_home == dp, to_ctx + t == ctx)

        @pl.when(here)
        def _():
            o_own.start()

        @pl.when(jnp.logical_not(here))
        def _():
            o_copy(t).start()

    own.wait()
    total = landed[0].astype(f32)
    for copy in first:
        copy.wait_recv()
    for k in range(1, N_DP):
        total = total + landed[k].astype(f32)
    part[...] = total.reshape(part.shape)
    second = []
    for k in range(1, N_CTX):
        to = lax.rem(ctx + k, N_CTX)
        second.append(remote(part.at[to], a_out.at[ctx], psend.at[k], precv.at[k], device_at(dp, to)))
    for copy in second:
        copy.start()
    mine = pltpu.make_async_copy(part.at[ctx], a_out.at[ctx], plocal)
    mine.start()
    mine.wait()
    for copy in second:
        copy.wait_recv()
    for k in range(8):
        here = jnp.logical_and(o_self, dp == k)

        @pl.when(here)
        def _():
            o_own.wait()

        @pl.when(jnp.logical_not(here))
        def _():
            remote(b_ref.at[0], b_out.at[k], osend.at[0], orecv.at[k], device_at(dp, ctx)).wait_recv()

    for t in range(8):
        here = jnp.logical_and(o_home == dp, to_ctx + t == ctx)

        @pl.when(jnp.logical_not(here))
        def _():
            o_copy(t).wait_send()

    for copy in first + second:
        copy.wait_send()


def grads_out(a, b, number):
    width = a.shape[-1]
    return pl.pallas_call(
        grads_kernel,
        out_shape=(
            jax.ShapeDtypeStruct((N_CTX, 8, width), f32),
            jax.ShapeDtypeStruct((N_DP,) + b.shape[1:], f32),
        ),
        in_specs=[ANY] * 2,
        out_specs=(VMEM, VMEM),
        scratch_shapes=[pltpu.VMEM(a.shape, a.dtype), pltpu.VMEM((N_CTX, 8, width), f32)]
        + [DMA, DMA((8,)), DMA((8,)), DMA((16,)), DMA((16,)), DMA, DMA((8,)), DMA((8,)), DMA],
        compiler_params=pltpu.CompilerParams(
            collective_id=number, has_side_effects=True, vmem_limit_bytes=24 * 2**20
        ),
        name="sum_grads",
    )(a, b)


def experts_kernel(
    tok_ref, att_ref, wo_ref, m_ref, router_ref, gain_ref, cot_ref, w_ref,
    out_ref, d_ref, res_ref, gates_ref, g_ref, hid_ref, out_parts, d_parts,
    pool, members, win, wide, picks, gate_slot, dg_slot, rows, tops, result, hidden, d_mid,
    stage, d_stage, tok, in_sem, tok_sem, out_sem, d_sem, g_sem, *scatters,
):
    loads = [
        pltpu.make_async_copy(att_ref, pool.at[:, :, 0], in_sem.at[0]),
        pltpu.make_async_copy(wo_ref, wide, in_sem.at[1]),
        pltpu.make_async_copy(m_ref, members, in_sem.at[2]),
        pltpu.make_async_copy(w_ref, win, in_sem.at[3]),
    ]
    place = my_place()
    ctx = ctx_of(place)
    pl.semaphore_wait(greet(chip_neighbours(place)), 4)
    gather = RowGather(
        place, cot_ref, lambda p: pool.at[p[2] * 4 + p[3], p[4], 1], ROWS // 2, *scatters[20:]
    )
    gather.start()
    pltpu.make_async_copy(tok_ref.at[0], tok.at[0], tok_sem.at[0]).start()
    for load in loads:
        load.start()
    line = lax.broadcasted_iota(jnp.int32, (8, EXTRA), 0)
    lane = lax.broadcasted_iota(jnp.int32, (8, EXTRA), 1)
    chosen = jnp.logical_and(line < 2, lane == 64 + 2 * ctx + line)
    chosen = jnp.where(chosen, 1.0, 0.0).astype(bf16)
    back = jnp.logical_and(line < 4, lane == jnp.where(line < 2, 0, 32) + 2 * ctx + lax.rem(line, 2))
    back = jnp.where(back, 1.0, 0.0).astype(bf16)
    before = lax.broadcasted_iota(jnp.int32, (ROWS, ROWS), 0) < lax.broadcasted_iota(
        jnp.int32, (ROWS, ROWS), 1
    )
    before = jnp.where(before, 1.0, 0.0).astype(bf16)
    slots = lax.broadcasted_iota(jnp.int32, (MOST, ROWS), 0).astype(f32)
    for load in loads[:3]:
        load.wait()

    def pick(chip, _):
        slot = lax.rem(chip, 2)
        pltpu.make_async_copy(tok_ref.at[chip], tok.at[slot], tok_sem.at[slot]).wait()

        @pl.when(chip < 7)
        def _():
            pltpu.make_async_copy(tok_ref.at[chip + 1], tok.at[1 - slot], tok_sem.at[1 - slot]).start()

        att = pool[chip, :, 0].reshape(2 * ROWS, D)
        residual = tok[slot].reshape(2 * ROWS, D).astype(f32)
        residual = residual + dot(att[:, :FF], wide[0]) + dot(att[:, FF:], wide[1])
        scale = lax.rsqrt(jnp.mean(residual * residual, axis=1, keepdims=True) + epsilon)
        hid = (residual * scale * gain_ref[...]).astype(bf16)
        logits = dot(hid, router_ref[...])
        inside = members[pl.ds(chip * 2, 2)].reshape(2 * ROWS, EXTRA).astype(f32)
        logits = jnp.where(inside > 0.5, logits, -1e30)
        weights = jnp.exp(logits - jnp.max(logits, axis=1, keepdims=True))
        weights = jnp.where(inside > 0.5, weights, 0.0)
        gates = weights / jnp.sum(weights, axis=1, keepdims=True)
        high = gates.astype(bf16)
        rest = (gates - high.astype(f32)).astype(bf16)
        for core in range(2):
            c = chip * 2 + core
            part = slice(core * ROWS, (core + 1) * ROWS)
            pool[chip, core, 0] = hid[part]

            @pl.when(c == ctx)
            def _():
                res_ref[...] = residual[part]
                gates_ref[...] = gates[part]

            facts = dot_last(chosen, inside[part].astype(bf16))
            gate_lines = dot_last(chosen, high[part]) + dot_last(chosen, rest[part])
            order = dot(facts.astype(bf16), before)
            both = []
            here = pl.ds(pl.multiple_of(c * MOST, MOST), MOST)
            for e in range(2):
                member = facts[e : e + 1]
                onehot = jnp.where(jnp.logical_and(order[e : e + 1] == slots, member > 0.5), 1.0, 0.0)
                gate_slot[e, here] = jnp.sum(onehot * gate_lines[e : e + 1], axis=1, keepdims=True)
                both.append(onehot.astype(bf16))
            both = jnp.concatenate(both, axis=0)
            picks[c] = both
            taken = dot(both, hid[part]).astype(bf16)
            rows[0, here] = taken[:MOST]
            rows[1, here] = taken[MOST:]
        return 0

    lax.fori_loop(0, 3, pick, 0)
    for n in range(3):
        gather.step(n)
    lax.fori_loop(3, 8, pick, 0)
    keep = pltpu.make_async_copy(pool.at[:, :, 0], hid_ref, in_sem.at[0])
    keep.start()
    for n in range(3, 5):
        gather.step(n)
    loads[3].wait()
    for e in range(2):
        for k in range(N_DP):
            for q in range(8):
                wide[e, q * 64 : (q + 1) * 64, k * ROWS : (k + 1) * ROWS] = win[
                    k, e, ROWS:, q * ROWS : (q + 1) * ROWS
                ]
    tile = 256

    def pick_tops(c, _):
        here = pl.ds(pl.multiple_of(c * MOST, MOST), MOST)
        taken = dot(picks[c], pool[lax.div(c, 2), lax.rem(c, 2), 1]).astype(bf16)
        tops[0, here] = taken[:MOST]
        tops[1, here] = taken[MOST:]
        return 0

    def forth(e, t):
        here = pl.ds(t * tile, tile)
        both = dot(rows[e, here], win[:, e, :ROWS].reshape(D, 2 * FF))
        gate_part, up_part = both[:, :FF], both[:, FF:]
        sigmoid = 1.0 / (1.0 + jnp.exp(-gate_part))
        silu = gate_part * sigmoid
        middle = (silu * up_part).astype(bf16)
        hidden[e, here] = middle
        d_mid[e, here, :FF] = (up_part * (sigmoid * (1.0 + gate_part * (1.0 - sigmoid)))).astype(bf16)
        d_mid[e, here, FF:] = silu.astype(bf16)
        result[e, here] = dot(middle, wide[e]).astype(bf16)

    def backward(e, t):
        here = pl.ds(t * tile, tile)
        top = tops[e, here].astype(f32)
        dg_slot[e, here] = jnp.sum(top * result[e, here].astype(f32), axis=1, keepdims=True)
        d_result = (top * gate_slot[e, here]).astype(bf16)
        tops[e, here] = d_result
        d_middle = dot_last(d_result, wide[e])
        d_mid[e, here, :FF] = (d_middle * d_mid[e, here, :FF].astype(f32)).astype(bf16)
        d_mid[e, here, FF:] = (d_middle * d_mid[e, here, FF:].astype(f32)).astype(bf16)
        weight = win[:, e, :ROWS].reshape(D, 2 * FF)
        result[e, here] = dot_last(d_mid[e, here], weight).astype(bf16)

    def combined(c, width, staged, out, sem, with_gates):
        here = pl.ds(pl.multiple_of(c * MOST, MOST), MOST)
        both = picks[c]
        slot = lax.rem(c, 2)

        @pl.when(c >= 2)
        def _():
            pltpu.make_async_copy(staged.at[slot], out.at[c], sem.at[slot]).wait()

        found = [result[0, here], result[1, here]]
        if not with_gates:
            found = [(found[e].astype(f32) * gate_slot[e, here]).astype(bf16) for e in range(2)]
        found = jnp.concatenate(found, axis=0)
        staged[slot, :, :D] = dot_first(both, found).astype(bf16)
        if with_gates:
            lines = [
                jnp.sum(
                    both[e * MOST : (e + 1) * MOST].astype(f32) * dg_slot[e, here], axis=0, keepdims=True
                )
                for e in range(2)
            ]
            high = [v.astype(bf16).astype(f32) for v in lines]
            rest = [v - h for v, h in zip(lines, high)]
            lines = jnp.concatenate(high + rest + [jnp.zeros((4, ROWS), f32)], axis=0).astype(bf16)
            staged[slot, :, D:] = dot_first(lines, back).astype(bf16)
        pltpu.make_async_copy(staged.at[slot], out.at[c], sem.at[slot]).start()

    def combine(staged, out, sem, with_gates):
        def one(c, _):
            combined(c, D, staged, out, sem, with_gates)
            return 0

        lax.fori_loop(0, N_CTX, one, 0)
        for slot in range(2):
            pltpu.make_async_copy(staged.at[slot], out.at[slot], sem.at[slot]).wait()

    def chips(ref):
        return lambda chip, core: ref.at[chip * 2 + core]

    for e in range(2):
        for t in range(3):
            forth(e, t)
            if e == 0 and t < 2:
                gather.step(5 + 2 * t)
                gather.step(6 + 2 * t)
    combine(stage, out_parts, out_sem, False)
    first = RowScatter(place, chips(out_parts), *scatters[:10])
    second = RowScatter(place, chips(d_parts), *scatters[10:20])
    for n in range(8):
        first.start(n)
    gather.finish()
    first.step(0)
    first.step(1)
    lax.fori_loop(0, N_CTX, pick_tops, 0)
    plan = [(), (), (2, 3), (4, 5), (), ()]
    for e in range(2):
        for t in range(3):
            backward(e, t)
            for n in plan[3 * e + t]:
                first.step(n)
    combine(d_stage, d_parts, d_sem, True)
    for n in range(8):
        second.start(n)
    first.step(6)
    second.step(0)
    second.step(1)
    keep.wait()

    def weights(e, k):
        here = pl.ds(k * 256, 256)
        total = dot_first(rows[e, :, here], d_mid[e]).astype(bf16)
        pool[2 * k, e, 0] = total[:ROWS]
        pool[2 * k + 1, e, 0] = total[ROWS:]
        total = dot_first(hidden[e], tops[e, :, here]).astype(bf16)
        for q in range(8):
            pool[2 * k, e, 1, :64, q * ROWS : (q + 1) * ROWS] = total[q * 64 : (q + 1) * 64, :ROWS]
            pool[2 * k + 1, e, 1, :64, q * ROWS : (q + 1) * ROWS] = total[q * 64 : (q + 1) * 64, ROWS:]

    plan = [(), (), (), (), (2, 3), (), (4, 5), ()]
    for e in range(2):
        for k in range(4):
            weights(e, k)
            for n in plan[4 * e + k]:
                second.step(n)
    saves = [
        pltpu.make_async_copy(pool.at[:, :, 0], g_ref.at[:, :, :ROWS], g_sem.at[0]),
        pltpu.make_async_copy(pool.at[:, :, 1, :64], g_ref.at[:, :, ROWS:], g_sem.at[1]),
    ]
    for save in saves:
        save.start()
    second.step(6)
    out_ref[...] = first.step(7)
    d_ref[...] = second.step(7)
    for save in saves:
        save.wait()
    first.finish()
    second.finish()


def experts(tok, att, wo, members, router, gain, cot, weights, number):
    slots = N_CTX * MOST
    v = lambda *shape: pltpu.VMEM(shape, bf16)
    column = pltpu.VMEM((2, slots, 1), f32)
    blocks = (8, 2, ROWS, D)
    return pl.pallas_call(
        experts_kernel,
        out_shape=(
            jax.ShapeDtypeStruct((ROWS, D), f32),
            jax.ShapeDtypeStruct((ROWS, D + EXTRA), f32),
            jax.ShapeDtypeStruct((ROWS, D), f32),
            jax.ShapeDtypeStruct((ROWS, EXTRA), f32),
            jax.ShapeDtypeStruct(weights.shape, bf16),
            jax.ShapeDtypeStruct(blocks, bf16),
            jax.ShapeDtypeStruct((N_CTX, ROWS, D), bf16),
            jax.ShapeDtypeStruct((N_CTX, ROWS, D + EXTRA), bf16),
        ),
        in_specs=[ANY] * 4 + [VMEM] * 2 + [ANY] * 2,
        out_specs=(VMEM,) * 4 + (ANY,) * 4,
        scratch_shapes=[
            v(8, 2, 2, ROWS, D),
            v(N_CTX, ROWS, EXTRA),
            v(*weights.shape),
            v(2, FF, D),
            v(N_CTX, 2 * MOST, ROWS),
            column,
            column,
            v(2, slots, D),
            v(2, slots, D),
            v(2, slots, D),
            v(2, slots, FF),
            v(2, slots, 2 * FF),
            v(2, ROWS, D),
            v(2, ROWS, D + EXTRA),
            v(2, 2, ROWS, D),
            DMA((4,)),
            DMA((2,)),
            DMA((2,)),
            DMA((2,)),
            DMA((2,)),
        ]
        + RowScatter.scratch(ROWS, D)
        + RowScatter.scratch(ROWS, D + EXTRA)
        + RowGather.scratch,
        compiler_params=pltpu.CompilerParams(
            collective_id=number, has_side_effects=True, vmem_limit_bytes=61 * 2**20
        ),
        cost_estimate=pl.CostEstimate(flops=15 * 10**9, bytes_accessed=30 * 2**20, transcendentals=2**20),
        name="experts_both_ways",
    )(tok.reshape(blocks), att.reshape(blocks), wo.reshape(2, FF, D), members, router, gain, cot, weights)


def swap_halves(u):
    lane = lax.broadcasted_iota(jnp.int32, u.shape, 1)
    return jnp.where(lax.rem(lane, 64) < 32, pltpu.roll(u, 96, 1), pltpu.roll(u, 32, 1))


def attend_kernel(
    src, order, raw_ref, cos_ref, sin_ref, o_ref, padded, q_ref, k_ref, v_ref, lse_ref, out_nat
):
    core = lax.axis_index("core")
    for b in range(SEQ // BLOCK):
        rows = pl.ds(pl.multiple_of(src[b] * BLOCK, BLOCK), BLOCK)
        here = pl.ds(b * BLOCK, BLOCK)
        qk = raw_ref[rows, 0:128]
        qk = qk * cos_ref[here, :] + swap_halves(qk) * sin_ref[here, :]
        q_ref[here, :] = (qk[:, 0:64]).astype(bf16)
        k_ref[here, :] = (qk[:, 64:128]).astype(bf16)
        v_ref[here, :] = raw_ref[rows, 128:192].astype(bf16)
    step = 256
    for i in range(SEQ // step):
        length = (i + 1) * step
        here = pl.ds(i * step, step)
        scores = dot_last(q_ref[here, :], k_ref[0:length, :]) * 0.125
        row = i * step + lax.broadcasted_iota(jnp.int32, (step, length), 0)
        column = lax.broadcasted_iota(jnp.int32, (step, length), 1)
        scores = jnp.where(column <= row, scores, -1e30)
        top = jnp.max(scores, axis=1, keepdims=True)
        weights = jnp.exp(scores - top)
        total = jnp.sum(weights, axis=1, keepdims=True)
        lse_ref[here, :] = top + jnp.log(total)
        probs = (weights * (1.0 / total)).astype(bf16)
        out_nat[here, :] = dot(probs, v_ref[0:length, :])
    for b in range(SEQ // BLOCK):
        rows = pl.ds(pl.multiple_of(order[b] * BLOCK, BLOCK), BLOCK)
        here = pl.ds(b * BLOCK, BLOCK)
        out = out_nat[rows, :].astype(bf16)
        o_ref[here, :] = out
        empty = jnp.zeros_like(out)
        padded[here, :] = jnp.where(
            core == 0, jnp.concatenate([out, empty], axis=1), jnp.concatenate([empty, out], axis=1)
        )


def attend(src, order, raw, cosine, sine):
    head = jax.ShapeDtypeStruct((SEQ, HEAD_DIM), bf16)
    return pl.pallas_call(
        attend_kernel,
        out_shape=(
            head,
            jax.ShapeDtypeStruct((SEQ, 128), bf16),
            head,
            head,
            head,
            jax.ShapeDtypeStruct((SEQ, 1), f32),
        ),
        in_specs=[SMEM, SMEM, VMEM, VMEM, VMEM],
        out_specs=(VMEM,) * 6,
        scratch_shapes=[pltpu.VMEM((SEQ, HEAD_DIM), f32)],
        compiler_params=pltpu.CompilerParams(vmem_limit_bytes=48 * 2**20),
        cost_estimate=pl.CostEstimate(flops=10**9, bytes_accessed=6 * 2**20, transcendentals=2**21),
        name="attention_forward",
    )(src, order, raw, cosine, sine)


def heads_kernel(padded, att_out, mine, other, merged, msem, xsend, xrecv, *sems):
    place = my_place()
    core = place[4]
    pl.semaphore_wait(greet(chip_neighbours(place)), 4)
    half = SEQ // 2
    swap = remote(
        padded.at[pl.ds(pl.multiple_of((1 - core) * half, half), half)], other, xsend, xrecv,
        sibling_of(place),
    )
    swap.start()
    own = pltpu.make_async_copy(padded.at[pl.ds(pl.multiple_of(core * half, half), half)], mine, msem)
    own.start()
    own.wait()
    swap.wait_recv()
    merged[...] = mine[...] + other[...]

    def view(p):
        chip = p[2] * 4 + p[3]
        return att_out.at[
            pl.ds(pl.multiple_of(p[4] * half, half), half), pl.ds(pl.multiple_of(chip * 128, 128), 128)
        ]

    heads = RowGather(place, merged, view, half // 2, *sems)
    heads.start()
    heads.pass_on()
    heads.finish()
    swap.wait_send()


def gather_heads(padded, number):
    return pl.pallas_call(
        heads_kernel,
        out_shape=jax.ShapeDtypeStruct((SEQ, D), bf16),
        in_specs=[ANY],
        out_specs=ANY,
        scratch_shapes=[pltpu.VMEM((SEQ // 2, 128), bf16)] * 3 + [DMA] * 3 + RowGather.scratch,
        compiler_params=pltpu.CompilerParams(collective_id=number, has_side_effects=True),
        name="gather_heads",
    )(padded)


def attend_back_kernel(
    src, order, q_ref, k_ref, v_ref, lse_ref, do_ref, cos_ref, sin_ref, out_ref, do_nat, acc, done
):
    for b in range(SEQ // BLOCK):
        rows = pl.ds(pl.multiple_of(src[b] * BLOCK, BLOCK), BLOCK)
        do_nat[pl.ds(b * BLOCK, BLOCK), :] = do_ref[rows, :]
    acc[...] = jnp.zeros_like(acc)
    step = 256
    for i in range(SEQ // step):
        length = (i + 1) * step
        here = pl.ds(i * step, step)
        query, d_out = q_ref[here, :], do_nat[here, :].astype(bf16)
        keys = k_ref[0:length, :]
        scores = dot_last(query, keys) * 0.125
        row = i * step + lax.broadcasted_iota(jnp.int32, (step, length), 0)
        column = lax.broadcasted_iota(jnp.int32, (step, length), 1)
        probs = jnp.where(column <= row, jnp.exp(scores - lse_ref[here, :]), 0.0)
        d_probs = dot_last(d_out, v_ref[0:length, :])
        delta = jnp.sum(probs * d_probs, axis=1, keepdims=True)
        d_scores = (probs * (d_probs - delta)).astype(bf16)
        acc[here, 0:64] = dot(d_scores, keys) * 0.125
        acc[0:length, 64:128] += dot_first(d_scores, query) * 0.125
        acc[0:length, 128:192] += dot_first(probs.astype(bf16), d_out)
    for b in range(SEQ // BLOCK):
        here = pl.ds(b * BLOCK, BLOCK)
        qk = acc[here, 0:128]
        qk = qk * cos_ref[here, :] - swap_halves(qk) * sin_ref[here, :]
        done[here, 0:128] = qk
        done[here, 128:256] = acc[here, 128:256]
    for b in range(SEQ // BLOCK):
        rows = pl.ds(pl.multiple_of(order[b] * BLOCK, BLOCK), BLOCK)
        out_ref[pl.ds(b * BLOCK, BLOCK), :] = done[rows, :].astype(bf16)


def attend_back(src, order, q, k, v, lse, d_out, cosine, sine):
    return pl.pallas_call(
        attend_back_kernel,
        out_shape=jax.ShapeDtypeStruct((SEQ, 256), bf16),
        in_specs=[SMEM, SMEM] + [VMEM] * 7,
        out_specs=VMEM,
        scratch_shapes=[
            pltpu.VMEM((SEQ, HEAD_DIM), f32),
            pltpu.VMEM((SEQ, 256), f32),
            pltpu.VMEM((SEQ, 256), f32),
        ],
        compiler_params=pltpu.CompilerParams(vmem_limit_bytes=56 * 2**20),
        cost_estimate=pl.CostEstimate(flops=3 * 10**9, bytes_accessed=6 * 2**20, transcendentals=2**21),
        name="attention_backward",
    )(src, order, q, k, v, lse, d_out, cosine, sine)


def rotary_tables():
    inverse = 10000.0 ** (-np.arange(32, dtype=np.float64) * 2.0 / HEAD_DIM)
    angles = np.arange(SEQ, dtype=np.float64)[:, None] * inverse[None, :]
    cosine, sine = np.cos(angles), np.sin(angles)
    return (
        np.tile(cosine, (1, 4)).astype(np.float32),
        np.concatenate([-sine, sine, -sine, sine], axis=1).astype(np.float32),
    )


def normalize(inputs, gain_values):
    scale_rows = lax.rsqrt(jnp.mean(inputs * inputs, axis=-1, keepdims=True) + epsilon)
    normed = inputs * scale_rows
    return (scale_rows, normed, (normed * gain_values.astype(f32)).astype(bf16))


def norm_backward(grad_in, normed, scale_rows, gain_values):
    grad_normed = grad_in * gain_values.astype(f32)
    inner = jnp.mean(grad_normed * normed, axis=-1, keepdims=True)
    return (scale_rows * (grad_normed - normed * inner), jnp.sum(grad_in * normed, axis=0))


def halves(value):
    high = lax.reduce_precision(value, 8, 7)
    return high.astype(bf16), (value - high).astype(bf16)


def local(
    tokens,
    cotangent,
    block_order,
    routes,
    norm_one,
    w_query,
    w_key,
    w_value,
    w_out,
    norm_two,
    w_router,
    expert_in,
    expert_out,
):
    ctx = lax.axis_index(CTX)
    cosine, sine = (jnp.asarray(t) for t in rotary_tables())
    order = jnp.stack([block_order, 2 * N_CTX - 1 - block_order], axis=1).reshape(-1)
    spots = jnp.arange(2 * N_CTX, dtype=jnp.int32)
    src = jnp.sum(jnp.where(order[None, :] == spots[:, None], spots[None, :], 0), axis=1)

    small = jnp.concatenate(
        [w_router, norm_one[:, None], norm_two[:, None], jnp.zeros((8, 30), bf16)], axis=1
    )
    tokens_all, packed_all, out_all, members = entry(
        tokens, w_query, w_key, w_value, small, w_out, routes, 0
    )
    down_packed = expert_out.reshape(2, 8, 64, ROWS).swapaxes(1, 2).reshape(2, 64, D)
    expert_all = lax.all_gather(jnp.concatenate([expert_in, down_packed], axis=1), DP, axis=0)
    low = packed_all[:, :, 8:, :].reshape(D, 128)
    weight = jnp.concatenate(
        [packed_all[:, :, :8, :].reshape(D, 128), low[:, :64], jnp.zeros((D, 64), bf16)], axis=1
    )
    router_weight, gain_one, gain_two = low[:, 64:96], low[:, 96], low[:, 97]
    out_weight = out_all.reshape(D, D)
    head_weight = lax.dynamic_slice_in_dim(out_weight, ctx * HEAD_DIM, HEAD_DIM, axis=0)

    tokens_float = tokens.astype(f32)
    scale_one, normed_one, _ = normalize(tokens_float, gain_one)
    _, _, hidden_one = normalize(tokens_all.reshape(SEQ, D).astype(f32), gain_one)
    raw = dot(hidden_one, weight)
    attended, padded, query, key, value, lse = attend(src, order, raw, cosine, sine)
    attended_all = gather_heads(padded, 1)

    router_wide = jnp.pad(router_weight, ((0, 0), (64, 32)))
    out_sum, d_sum, residual, gates, grad_experts, hidden_all, _, _ = experts(
        tokens_all,
        attended_all,
        out_weight,
        members,
        router_wide,
        gain_two.astype(f32)[None, :],
        cotangent,
        expert_all,
        3,
    )
    hidden_all = hidden_all.reshape(SEQ, D)
    gates = gates[:, 64:96]
    scale_two, normed_two, _ = normalize(residual, gain_two)
    output = residual + out_sum
    grad_experts = lax.psum_scatter(grad_experts, DP, scatter_dimension=0).astype(f32)
    grad_in = grad_experts[:, :ROWS]
    grad_down = grad_experts[:, ROWS:].reshape(2, 64, 8, ROWS).swapaxes(1, 2).reshape(2, FF, ROWS)

    grad_top = cotangent.astype(f32)
    d_gates = d_sum[:, D : D + 32] + d_sum[:, D + 32 : D + 64]
    d_picked = gates * (d_gates - jnp.sum(gates * d_gates, axis=1, keepdims=True))
    d_logits = d_picked.astype(bf16)
    d_hidden_two = d_sum[:, :D] + dot_last(d_logits, router_weight)
    d_norm_two, grad_gain_two = norm_backward(d_hidden_two, normed_two, scale_two, gain_two)
    d_residual = grad_top + d_norm_two
    sent = jnp.concatenate(
        [d_residual.astype(bf16), d_logits, jnp.zeros((ROWS, EXTRA - 32), bf16)], axis=1
    )
    all_three = gather_ctx(sent, 5).reshape(SEQ, D + EXTRA)
    d_branch = all_three[:, :D]
    d_logits_all = all_three[:, D : D + 32]

    d_attended = dot_last(d_branch, head_weight).astype(bf16).astype(f32)
    d_raw = attend_back(src, order, query, key, value, lse, d_attended, cosine, sine)
    d_one = dot_last(d_raw, weight).astype(bf16).reshape(N_CTX, ROWS, D)
    d_hidden_one = scatter_ctx(d_one, 6)
    d_norm_one, grad_gain_one = norm_backward(d_hidden_one, normed_one, scale_one, gain_one)
    input_grad = d_residual + d_norm_one

    grad_out_weight = dot_first(attended, d_branch)
    own_columns = lax.dynamic_slice_in_dim(hidden_all, ctx * 64, 64, axis=1)
    grad_router = dot_first(own_columns, d_logits_all)
    second = jnp.concatenate(
        [grad_out_weight, grad_router, jnp.zeros((64, EXTRA - 32), f32)], axis=1
    ).reshape(8, 8, D + EXTRA)
    grad_heads = dot_first(hidden_one, d_raw)
    first = jnp.concatenate(
        [
            grad_heads[:, :192],
            grad_gain_one[:, None],
            grad_gain_two[:, None],
            jnp.zeros((D, 62), f32),
        ],
        axis=1,
    ).astype(bf16)
    a, b = grads_out(first.reshape(N_DP, ROWS, 256), second, 7)
    b = jnp.sum(b, axis=0)
    side = lambda v: jnp.moveaxis(v, 0, 1).reshape(8, -1)
    pairs = a.reshape(KV_HEADS, 2, 8, 256).sum(axis=1)
    gains = jnp.sum(a[:, :, 192:194], axis=0)
    return (
        output,
        input_grad,
        gains[:, 0],
        side(a[:, :, 0:64]),
        side(pairs[:, :, 64:128]),
        side(pairs[:, :, 128:192]),
        b[:, :D],
        gains[:, 1],
        b[:, D : D + 32],
        grad_in,
        grad_down,
    )


def solution(mesh):
    split = Mesh(mesh.devices.reshape(2, 4, 2, 4, 2), AXES)
    rows = P(AXES, None)
    line = P(AXES)
    return jax.shard_map(
        local,
        mesh=split,
        in_specs=(
            rows,
            rows,
            P(),
            rows,
            line,
            rows,
            rows,
            rows,
            rows,
            line,
            rows,
            P(CTX, DP, None),
            P(CTX, None, DP),
        ),
        out_specs=(
            rows,
            rows,
            line,
            rows,
            rows,
            rows,
            rows,
            line,
            rows,
            P(CTX, DP, None),
            P(CTX, None, DP),
        ),
        check_vma=False,
    )
```

```python
import functools
import math

import jax
import jax.numpy as jnp
import numpy as np
from jax import lax
from jax.experimental import pallas as pl
from jax.experimental.pallas import tpu as pltpu
from jax.sharding import Mesh
from jax.sharding import PartitionSpec as P

D = 1024
HEADS = 16
KV_HEADS = 8
HEAD_DIM = 64
EXPERTS = 32
FF = 512
TOP = 8
MOST = 48
ROWS = 128
SEQ = 2048
BLOCK = 64
AXES = ("ylo", "z", "yhi", "x", "core")
DP = ("ylo", "z")
CTX = ("yhi", "x", "core")
N_DP = 8
N_CTX = 16
EXTRA = 128
MESH_ID = pl.DeviceIdType.MESH
ANY = pl.BlockSpec(memory_space=pl.ANY)
VMEM = pl.BlockSpec(memory_space=pltpu.VMEM)
SMEM = pl.BlockSpec(memory_space=pltpu.SMEM)
DMA = pltpu.SemaphoreType.DMA
bf16 = jnp.bfloat16
f32 = jnp.float32
epsilon = 1e-06


def dot(a, b):
    return jnp.dot(a, b, preferred_element_type=f32)


def dot_last(a, b):
    return lax.dot_general(a, b, (((1,), (1,)), ((), ())), preferred_element_type=f32)


def dot_first(a, b):
    return lax.dot_general(a, b, (((0,), (0,)), ((), ())), preferred_element_type=f32)


def my_place():
    return tuple(lax.axis_index(a) for a in AXES)


def device_at(dp, ctx):
    return (
        lax.div(dp, 4),
        lax.rem(dp, 4),
        lax.div(ctx, 8),
        lax.rem(lax.div(ctx, 2), 4),
        lax.rem(ctx, 2),
    )


def beside(place, dy, dx):
    ylo, z, yhi, x, core = place
    return (ylo, z, lax.rem(yhi + dy, 2), lax.rem(x + dx, 4), core)


def ctx_of(place):
    return place[2] * 8 + place[3] * 2 + place[4]


def dp_of(place):
    return place[0] * 4 + place[1]


def sibling_of(place):
    return place[:4] + (1 - place[4],)


def remote(src, dst, send, recv, device):
    return pltpu.make_async_remote_copy(
        src_ref=src, dst_ref=dst, send_sem=send, recv_sem=recv, device_id=device, device_id_type=MESH_ID
    )


def greet(devices):
    barrier = pltpu.get_barrier_semaphore()
    for device in devices:
        pl.semaphore_signal(barrier, inc=1, device_id=device, device_id_type=MESH_ID)
    return barrier


class RowGather:
    scratch = [DMA, DMA((9,)), DMA((9,)), DMA((10,)), DMA((10,))]
    links = [(1, 0), (0, 1), (0, 3), (0, 1), (0, 3), (0, 1), (0, 3), (0, 1), (0, 3)]
    held = [(0, 0), (0, 0), (0, 0), (1, 0), (1, 0), (0, 3), (0, 1), (1, 3), (1, 1)]
    parts = [None, None, None, None, None, 0, 1, 0, 1]
    after = {0: (3, 4), 1: (5,), 2: (6,), 3: (7,), 4: (8,)}

    def __init__(self, place, x_ref, view, half, local, send, recv, fsend, frecv):
        sibling = sibling_of(place)

        def piece(dy, dx, part):
            ref = view(beside(place, dy, dx))
            return ref if part is None else ref.at[pl.ds(part * half, half)]

        self.own = pltpu.make_async_copy(x_ref, view(place), local)
        self.out, self.landed, self.passed = [], [], []
        for n, ((ly, lx), (hy, hx), part) in enumerate(zip(self.links, self.held, self.parts)):
            source = x_ref if n < 3 else piece(hy, hx, part)
            self.out.append(
                remote(source, piece(hy, hx, part), send.at[n], recv.at[n], beside(place, ly, lx))
            )
            here = piece((hy + ly) % 2, (hx + 4 - lx) % 4, part)
            self.landed.append(remote(here, here, send.at[n], recv.at[n], beside(place, ly, lx)))
            self.passed.append(remote(here, here, fsend.at[n], frecv.at[n], sibling))
        self.passed.append(remote(x_ref, view(place), fsend.at[9], frecv.at[9], sibling))
        self.back = []
        for n in range(9):
            (ly, lx), (hy, hx), part = self.links[n], self.held[n], self.parts[n]
            ref = view(sibling_of(beside(place, (hy + ly) % 2, (hx + 4 - lx) % 4)))
            ref = ref if part is None else ref.at[pl.ds(part * half, half)]
            self.back.append(remote(ref, ref, fsend.at[n], frecv.at[n], sibling))
        ref = view(sibling)
        self.back.append(remote(ref, ref, fsend.at[9], frecv.at[9], sibling))

    def start(self):
        for n in range(3):
            self.out[n].start()
        self.passed[9].start()
        self.own.start()

    def step(self, n):
        self.landed[n].wait_recv()
        for m in self.after.get(n, ()):
            self.out[m].start()
        self.passed[n].start()

    def pass_on(self):
        for n in range(9):
            self.step(n)

    def finish(self):
        self.own.wait()
        for n in range(10):
            self.back[n].wait_recv()
        for copy in self.out + self.passed:
            copy.wait_send()


def chip_neighbours(place):
    return [beside(place, 1, 0), beside(place, 0, 1), beside(place, 0, 3), sibling_of(place)]


SPREAD = [(1, 2), (0, 2), (1, 1), (1, 3), (0, 1), (0, 3), (1, 0), (0, 0)]


class RowScatter:
    @staticmethod
    def scratch(rows, width):
        return [
            pltpu.VMEM((8, rows, width), bf16),
            pltpu.VMEM((8, rows, width), bf16),
            pltpu.VMEM((4, rows // 2, width), bf16),
            pltpu.VMEM((4, rows, width), bf16),
            pltpu.VMEM((rows, width), bf16),
            DMA((8,)),
            DMA((8,)),
            DMA((8,)),
            DMA((9,)),
            DMA((9,)),
        ]

    def __init__(self, place, part, own, other, halves, wholes, last, own_sem, fsend, frecv, send, recv):
        self.own, self.other, self.halves, self.wholes, self.last = own, other, halves, wholes, last
        core = place[4]
        half = own.shape[1] // 2
        self.half = half
        self.mine, self.cross = [], []
        for n, (dy, dx) in enumerate(SPREAD):
            chip = lax.div(ctx_of(beside(place, dy, dx)), 2)
            self.mine.append(pltpu.make_async_copy(part(chip, core), own.at[n], own_sem.at[n]))
            self.cross.append(
                remote(part(chip, 1 - core), other.at[n], fsend.at[n], frecv.at[n], sibling_of(place))
            )
        right, left = beside(place, 0, 1), beside(place, 0, 3)
        self.out = []
        for n, (source, target, device) in enumerate(
            [
                (own.at[0, pl.ds(0, half)], halves.at[0], right),
                (own.at[0, pl.ds(half, half)], halves.at[1], left),
                (own.at[1, pl.ds(0, half)], halves.at[2], right),
                (own.at[1, pl.ds(half, half)], halves.at[3], left),
                (own.at[2], wholes.at[0], right),
                (own.at[3], wholes.at[1], left),
                (own.at[4], wholes.at[2], right),
                (own.at[5], wholes.at[3], left),
                (own.at[6], last, beside(place, 1, 0)),
            ]
        ):
            self.out.append(remote(source, target, send.at[n], recv.at[n], device))

    def start(self, n):
        self.cross[n].start()
        self.mine[n].start()

    def join(self, n):
        self.mine[n].wait()
        self.cross[n].wait_recv()
        return self.own[n].astype(f32) + self.other[n].astype(f32)

    def step(self, n):
        if n < 2:
            self.own[n] = self.join(n).astype(bf16)
            self.out[2 * n].start()
            self.out[2 * n + 1].start()
        elif n < 6:
            total = self.join(n)
            half = self.half
            side = pl.ds(0 if n % 2 == 0 else half, half)
            self.out[n - 2].wait_recv()
            self.own[n] = total.astype(bf16)
            first = total[:half] if n % 2 == 0 else total[half:]
            self.own[n, side] = (first + self.halves[n - 2].astype(f32)).astype(bf16)
            self.out[n + 2].start()
        elif n == 6:
            total = self.join(6)
            for m in (0, 1):
                self.out[4 + m].wait_recv()
                total = total + self.wholes[m].astype(f32)
            self.own[6] = total.astype(bf16)
            self.out[8].start()
        else:
            total = self.join(7)
            for m in (2, 3):
                self.out[4 + m].wait_recv()
                total = total + self.wholes[m].astype(f32)
            self.out[8].wait_recv()
            return total + self.last[...].astype(f32)

    def finish(self):
        for copy in self.out + self.cross:
            copy.wait_send()


def entry_kernel(
    x_ref, q_ref, k_ref, v_ref, small_ref, o_ref, routes_ref, x_out, w_out, o_out, m_out,
    w_pack, o_pad, o_other, o_mid, m_pack, *sems,
):
    row_sems, o_sems, m_sems, rest = sems[:5], sems[5:10], sems[10:15], sems[15:]
    wlocal, wsend, wrecv, psend, precv, xsend, xrecv, osend, orecv = rest
    place = my_place()
    core = place[4]
    dp, ctx = dp_of(place), ctx_of(place)
    barrier = greet(
        [device_at(dp, lax.rem(ctx + k, N_CTX)) for k in range(1, N_CTX)]
        + [device_at(lax.rem(dp + k, N_DP), ctx) for k in range(1, N_DP)]
    )
    pl.semaphore_wait(barrier, 22)
    rows = RowGather(place, x_ref, lambda p: x_out.at[ctx_of(p)], x_ref.shape[0] // 2, *row_sems)
    rows.start()

    out = o_ref[...].astype(f32)
    empty = jnp.zeros_like(out)
    out = jnp.where(core == 0, jnp.concatenate([out, empty], 0), jnp.concatenate([empty, out], 0))
    for s in range(2):
        o_pad[s] = out[:, s * 512 : (s + 1) * 512].astype(bf16)
    swap = remote(o_pad.at[1 - core], o_other, xsend, xrecv, sibling_of(place))
    swap.start()
    query, key, value = (r[...].astype(f32) for r in (q_ref, k_ref, v_ref))
    small = small_ref[...].astype(f32)
    for h in range(HEADS):
        at, pair = slice(h * 64, h * 64 + 64), slice(h // 2 * 64, h // 2 * 64 + 64)
        top = jnp.concatenate([query[:, at], key[:, pair]], axis=1)
        low = jnp.concatenate([value[:, pair], small], axis=1)
        w_pack[h] = jnp.concatenate([top, low], axis=0).astype(bf16)
    first, second, third = [], [], []
    for k in range(1, N_CTX):
        to = lax.rem(ctx + k, N_CTX)
        first.append(
            remote(w_pack.at[to], w_out.at[dp, ctx], wsend.at[k], wrecv.at[k], device_at(dp, to))
        )
    for k in range(1, N_DP):
        device = device_at(lax.rem(dp + k, N_DP), ctx)
        third.append(remote(o_mid.at[dp], o_mid.at[dp], osend.at[k], orecv.at[k], device))
        second.append(remote(w_out.at[dp], w_out.at[dp], psend.at[k], precv.at[k], device))
    for copy in first:
        copy.start()
    own = pltpu.make_async_copy(w_pack.at[ctx], w_out.at[dp, ctx], wlocal)
    own.start()
    swap.wait_recv()
    o_mid[dp] = o_pad[core] + o_other[...]
    for copy in third:
        copy.start()
    routes = routes_ref[...]
    lane = lax.broadcasted_iota(jnp.int32, (ROWS, EXTRA), 1) - 64
    member = jnp.zeros((ROWS, EXTRA), f32)
    for k in range(TOP):
        member = jnp.where(lane == routes[:, k : k + 1], 1.0, member)
    m_pack[...] = member.astype(bf16)
    members = RowGather(place, m_pack, lambda p: m_out.at[ctx_of(p)], ROWS // 2, *m_sems)
    members.start()
    own.wait()
    for copy in first:
        copy.wait_recv()
    for copy in second:
        copy.start()
    for copy in third:
        copy.wait_recv()

    def o_view(p):
        return o_out.at[:, p[2] * 4 + p[3], :, pl.ds(pl.multiple_of(p[4] * 512, 512), 512)]

    outs = RowGather(place, o_mid, o_view, 4, *o_sems)
    outs.start()
    for n in range(5):
        rows.step(n)
    for n in range(9):
        members.step(n)
    for n in range(3):
        outs.step(n)
    for n in range(5, 9):
        rows.step(n)
    for n in range(3, 9):
        outs.step(n)
    rows.finish()
    members.finish()
    outs.finish()
    for copy in second:
        copy.wait_recv()
    swap.wait_send()
    for copy in first + second + third:
        copy.wait_send()


def entry(x, query, key, value, small, out, routes, number):
    return pl.pallas_call(
        entry_kernel,
        out_shape=(
            jax.ShapeDtypeStruct((N_CTX,) + x.shape, bf16),
            jax.ShapeDtypeStruct((N_DP, N_CTX, 16, 128), bf16),
            jax.ShapeDtypeStruct((N_DP, 8, 16, D), bf16),
            jax.ShapeDtypeStruct((N_CTX, ROWS, EXTRA), bf16),
        ),
        in_specs=[ANY] + [VMEM] * 6,
        out_specs=(ANY,) * 4,
        scratch_shapes=[
            pltpu.VMEM((N_CTX, 16, 128), bf16),
            pltpu.VMEM((2, 16, 512), bf16),
            pltpu.VMEM((16, 512), bf16),
            pltpu.VMEM((N_DP, 16, 512), bf16),
            pltpu.VMEM((ROWS, EXTRA), bf16),
        ]
        + RowGather.scratch * 3
        + [DMA, DMA((16,)), DMA((16,)), DMA((8,)), DMA((8,)), DMA, DMA, DMA((8,)), DMA((8,))],
        compiler_params=pltpu.CompilerParams(
            collective_id=number, has_side_effects=True, vmem_limit_bytes=16 * 2**20
        ),
        name="entry_gather",
    )(x, query, key, value, small, out, routes)


def last_kernel(
    d_raw, weight, side, d_branch, d_logits, hidden_ref, att_ref, hid_ref, one_ref, a_out, w_out,
    hidden, att, hid, parts, w_parts, a_pack, landed, part, w_sum, w_landed, w_mine,
    in_sem, wlocal, wsend, wrecv, psend, precv, plocal, osend, orecv, olocal, xsend, xrecv, *scatters,
):
    place = my_place()
    core = place[4]
    dp, ctx = dp_of(place), ctx_of(place)
    barrier = greet(
        [device_at(dp, lax.rem(ctx + k, N_CTX)) for k in range(1, N_CTX)]
        + [device_at(lax.rem(dp + k, N_DP), ctx) for k in range(1, N_DP)]
    )
    loads = [
        pltpu.make_async_copy(att_ref.at[lax.div(ctx, 2), core], att, in_sem.at[0]),
        pltpu.make_async_copy(hid_ref.at[lax.div(ctx, 2), core], hid, in_sem.at[1]),
        pltpu.make_async_copy(hidden_ref, hidden, in_sem.at[2]),
    ]
    for load in loads:
        load.start()

    def back(c, _):
        here = pl.ds(pl.multiple_of(c * ROWS, ROWS), ROWS)
        parts[lax.div(c, 2), lax.rem(c, 2)] = dot_last(d_raw[here, :], weight[...]).astype(bf16)
        return 0

    lax.fori_loop(0, N_CTX, back, 0)
    pl.semaphore_wait(barrier, 22)
    rows = RowScatter(place, lambda chip, c: parts.at[chip, c], *scatters[:10])
    outs = RowScatter(place, lambda chip, c: w_parts.at[chip, c], *scatters[10:])
    for n in range(8):
        rows.start(n)
    for load in loads:
        load.wait()

    def heads(k, _):
        here = pl.ds(pl.multiple_of(k * ROWS, ROWS), ROWS)
        grad = dot_first(hidden[:, here], d_raw[...])
        gain = jnp.sum(grad * weight[here, :].astype(f32), axis=1, keepdims=True)
        lane = lax.broadcasted_iota(jnp.int32, (ROWS, 128), 1)
        extra = side[here, :]
        high = grad[:, 128:] + dot_first(hid[:, here], d_logits[...])
        high = jnp.where(lane == 64, gain * extra[:, 0:1], jnp.where(lane == 65, extra[:, 1:2], high))
        a_pack[k, :, :128] = grad[:, :128].astype(bf16)
        a_pack[k, :, 128:] = high.astype(bf16)
        return 0

    lax.fori_loop(0, N_DP, heads, 0)
    first, second, third = [], [], []
    for k in range(1, N_DP):
        to = lax.rem(dp + k, N_DP)
        first.append(remote(a_pack.at[to], landed.at[k], wsend.at[k], wrecv.at[k], device_at(to, ctx)))
        third.append(
            remote(
                w_sum.at[pl.ds(pl.multiple_of(to * 16, 16), 16)],
                w_landed.at[k],
                osend.at[k],
                orecv.at[k],
                device_at(to, ctx),
            )
        )
    for copy in first:
        copy.start()
    own = pltpu.make_async_copy(a_pack.at[dp], landed.at[0], wlocal)
    own.start()
    rows.step(0)
    rows.step(1)

    def products(k, _):
        here = pl.ds(pl.multiple_of(k * ROWS, ROWS), ROWS)
        total = dot_first(att[:, here], d_branch[...]).astype(bf16)
        to = pl.ds(pl.multiple_of(k * 16, 16), 16)
        for g in range(8):
            for c in range(2):
                w_parts[g, c, to, :] = total[g * 16 : (g + 1) * 16, c * 512 : (c + 1) * 512]
        return 0

    lax.fori_loop(0, N_DP, products, 0)
    for n in range(8):
        outs.start(n)
    for n in range(2, 6):
        rows.step(n)
    outs.step(0)
    outs.step(1)
    own.wait()
    for copy in first:
        copy.wait_recv()
    total = landed[0].astype(f32)
    for k in range(1, N_DP):
        total = total + landed[k].astype(f32)
    part[...] = total.reshape(part.shape)
    for k in range(1, N_CTX):
        to = lax.rem(ctx + k, N_CTX)
        second.append(remote(part.at[to], a_out.at[ctx], psend.at[k], precv.at[k], device_at(dp, to)))
    for copy in second:
        copy.start()
    mine = pltpu.make_async_copy(part.at[ctx], a_out.at[ctx], plocal)
    mine.start()
    rows.step(6)
    for n in range(2, 6):
        outs.step(n)
    one_ref[...] = rows.step(7)
    outs.step(6)
    w_sum[...] = outs.step(7)
    for copy in third:
        copy.start()
    own = pltpu.make_async_copy(w_sum.at[pl.ds(pl.multiple_of(dp * 16, 16), 16)], w_landed.at[0], olocal)
    own.start()
    own.wait()
    for copy in third:
        copy.wait_recv()
    total = w_landed[0]
    for k in range(1, N_DP):
        total = total + w_landed[k]
    w_mine[...] = total.reshape(2, 8, 512)
    swap = remote(w_mine.at[1 - core], w_out.at[core], xsend, xrecv, sibling_of(place))
    swap.start()
    keep = pltpu.make_async_copy(w_mine.at[core], w_out.at[core], in_sem.at[0])
    swap_in = remote(w_mine.at[1 - core], w_out.at[1 - core], xsend, xrecv, sibling_of(place))
    swap_in.wait_recv()
    swap.wait_send()
    keep.start()
    keep.wait()
    mine.wait()
    for copy in second:
        copy.wait_recv()
    rows.finish()
    outs.finish()
    for copy in first + second + third:
        copy.wait_send()


def last(d_raw, weight, side, d_branch, d_logits, hidden, att, hid, number):
    v = lambda *shape: pltpu.VMEM(shape, bf16)
    return pl.pallas_call(
        last_kernel,
        out_shape=(
            jax.ShapeDtypeStruct((ROWS, D), f32),
            jax.ShapeDtypeStruct((N_CTX, 8, 256), f32),
            jax.ShapeDtypeStruct((2, 8, 512), f32),
        ),
        in_specs=[VMEM] * 5 + [ANY] * 3,
        out_specs=(VMEM,) * 3,
        scratch_shapes=[
            v(SEQ, D),
            v(ROWS, D),
            v(ROWS, D),
            v(8, 2, ROWS, D),
            v(8, 2, ROWS, 512),
            v(N_DP, ROWS, 256),
            v(N_DP, ROWS, 256),
            pltpu.VMEM((N_CTX, 8, 256), f32),
            pltpu.VMEM((ROWS, 512), f32),
            pltpu.VMEM((N_DP, 16, 512), f32),
            pltpu.VMEM((2, 8, 512), f32),
            DMA((3,)),
            DMA,
            DMA((8,)),
            DMA((8,)),
            DMA((16,)),
            DMA((16,)),
            DMA,
            DMA((8,)),
            DMA((8,)),
            DMA,
            DMA,
            DMA,
        ]
        + RowScatter.scratch(ROWS, D)
        + RowScatter.scratch(ROWS, 512),
        compiler_params=pltpu.CompilerParams(
            collective_id=number, has_side_effects=True, vmem_limit_bytes=48 * 2**20
        ),
        name="last_sums",
    )(d_raw, weight, side, d_branch, d_logits, hidden, att, hid)


def experts_kernel(
    tok_ref, att_ref, wo_ref, m_ref, router_ref, gain_ref, cot_ref, w_ref,
    out_ref, res_ref, d_res_ref, d_branch_ref, d_logits_ref, gain_grad_ref,
    g_ref, hid_ref, heads_ref, out_parts, d_parts,
    pool, members, win, wide, picks, gate_slot, dg_slot, rows, tops, result, hidden, d_mid,
    stage, d_stage, tok, gates_ref, d_heads, in_sem, tok_sem, out_sem, d_sem, g_sem, hsend, hrecv, *scatters,
):
    loads = [
        pltpu.make_async_copy(att_ref, pool.at[:, :, 0], in_sem.at[0]),
        pltpu.make_async_copy(wo_ref, wide, in_sem.at[1]),
        pltpu.make_async_copy(m_ref, members, in_sem.at[2]),
        pltpu.make_async_copy(w_ref, win, in_sem.at[3]),
    ]
    place = my_place()
    ctx = ctx_of(place)
    dp = dp_of(place)
    pl.semaphore_wait(greet([device_at(dp, lax.rem(ctx + k, N_CTX)) for k in range(1, N_CTX)]), 15)
    gather = RowGather(
        place, cot_ref, lambda p: pool.at[p[2] * 4 + p[3], p[4], 1], ROWS // 2, *scatters[20:]
    )
    gather.start()
    pltpu.make_async_copy(tok_ref.at[0], tok.at[0], tok_sem.at[0]).start()
    for load in loads:
        load.start()
    line = lax.broadcasted_iota(jnp.int32, (8, EXTRA), 0)
    lane = lax.broadcasted_iota(jnp.int32, (8, EXTRA), 1)
    chosen = jnp.logical_and(line < 2, lane == 64 + 2 * ctx + line)
    chosen = jnp.where(chosen, 1.0, 0.0).astype(bf16)
    back = jnp.logical_and(line < 4, lane == jnp.where(line < 2, 0, 32) + 2 * ctx + lax.rem(line, 2))
    back = jnp.where(back, 1.0, 0.0).astype(bf16)
    before = lax.broadcasted_iota(jnp.int32, (ROWS, ROWS), 0) < lax.broadcasted_iota(
        jnp.int32, (ROWS, ROWS), 1
    )
    before = jnp.where(before, 1.0, 0.0).astype(bf16)
    slots = lax.broadcasted_iota(jnp.int32, (MOST, ROWS), 0).astype(f32)
    for load in loads[:3]:
        load.wait()

    def pick(chip, _):
        slot = lax.rem(chip, 2)
        pltpu.make_async_copy(tok_ref.at[chip], tok.at[slot], tok_sem.at[slot]).wait()

        @pl.when(chip < 7)
        def _():
            pltpu.make_async_copy(tok_ref.at[chip + 1], tok.at[1 - slot], tok_sem.at[1 - slot]).start()

        att = pool[chip, :, 0].reshape(2 * ROWS, D)
        residual = tok[slot].reshape(2 * ROWS, D).astype(f32)
        residual = residual + dot(att[:, :FF], wide[0]) + dot(att[:, FF:], wide[1])
        scale = lax.rsqrt(jnp.mean(residual * residual, axis=1, keepdims=True) + epsilon)
        hid = (residual * scale * gain_ref[...]).astype(bf16)
        logits = dot(hid, router_ref[...])
        inside = members[pl.ds(chip * 2, 2)].reshape(2 * ROWS, EXTRA).astype(f32)
        logits = jnp.where(inside > 0.5, logits, -1e30)
        weights = jnp.exp(logits - jnp.max(logits, axis=1, keepdims=True))
        weights = jnp.where(inside > 0.5, weights, 0.0)
        gates = weights / jnp.sum(weights, axis=1, keepdims=True)
        high = gates.astype(bf16)
        rest = (gates - high.astype(f32)).astype(bf16)
        for core in range(2):
            c = chip * 2 + core
            part = slice(core * ROWS, (core + 1) * ROWS)
            pool[chip, core, 0] = hid[part]

            @pl.when(c == ctx)
            def _():
                res_ref[...] = residual[part]
                gates_ref[...] = gates[part]

            facts = dot_last(chosen, inside[part].astype(bf16))
            gate_lines = dot_last(chosen, high[part]) + dot_last(chosen, rest[part])
            order = dot(facts.astype(bf16), before)
            both = []
            here = pl.ds(pl.multiple_of(c * MOST, MOST), MOST)
            for e in range(2):
                member = facts[e : e + 1]
                onehot = jnp.where(jnp.logical_and(order[e : e + 1] == slots, member > 0.5), 1.0, 0.0)
                gate_slot[e, here] = jnp.sum(onehot * gate_lines[e : e + 1], axis=1, keepdims=True)
                both.append(onehot.astype(bf16))
            both = jnp.concatenate(both, axis=0)
            picks[c] = both
            taken = dot(both, hid[part]).astype(bf16)
            rows[0, here] = taken[:MOST]
            rows[1, here] = taken[MOST:]
        return 0

    lax.fori_loop(0, 3, pick, 0)
    for n in range(3):
        gather.step(n)
    lax.fori_loop(3, 8, pick, 0)
    keep = pltpu.make_async_copy(pool.at[:, :, 0], hid_ref, in_sem.at[0])
    keep.start()
    for n in range(3, 5):
        gather.step(n)
    loads[3].wait()
    for e in range(2):
        for k in range(N_DP):
            for q in range(8):
                wide[e, q * 64 : (q + 1) * 64, k * ROWS : (k + 1) * ROWS] = win[
                    k, e, ROWS:, q * ROWS : (q + 1) * ROWS
                ]
    tile = 256

    def pick_tops(c, _):
        here = pl.ds(pl.multiple_of(c * MOST, MOST), MOST)
        taken = dot(picks[c], pool[lax.div(c, 2), lax.rem(c, 2), 1]).astype(bf16)
        tops[0, here] = taken[:MOST]
        tops[1, here] = taken[MOST:]
        return 0

    def forth(e, t):
        here = pl.ds(t * tile, tile)
        both = dot(rows[e, here], win[:, e, :ROWS].reshape(D, 2 * FF))
        gate_part, up_part = both[:, :FF], both[:, FF:]
        sigmoid = 1.0 / (1.0 + jnp.exp(-gate_part))
        silu = gate_part * sigmoid
        middle = (silu * up_part).astype(bf16)
        hidden[e, here] = middle
        d_mid[e, here, :FF] = (up_part * (sigmoid * (1.0 + gate_part * (1.0 - sigmoid)))).astype(bf16)
        d_mid[e, here, FF:] = silu.astype(bf16)
        result[e, here] = dot(middle, wide[e]).astype(bf16)

    def backward(e, t):
        here = pl.ds(t * tile, tile)
        top = tops[e, here].astype(f32)
        dg_slot[e, here] = jnp.sum(top * result[e, here].astype(f32), axis=1, keepdims=True)
        d_result = (top * gate_slot[e, here]).astype(bf16)
        tops[e, here] = d_result
        d_middle = dot_last(d_result, wide[e])
        d_mid[e, here, :FF] = (d_middle * d_mid[e, here, :FF].astype(f32)).astype(bf16)
        d_mid[e, here, FF:] = (d_middle * d_mid[e, here, FF:].astype(f32)).astype(bf16)
        weight = win[:, e, :ROWS].reshape(D, 2 * FF)
        result[e, here] = dot_last(d_mid[e, here], weight).astype(bf16)

    def combined(c, width, staged, out, sem, with_gates):
        here = pl.ds(pl.multiple_of(c * MOST, MOST), MOST)
        both = picks[c]
        slot = lax.rem(c, 2)

        @pl.when(c >= 2)
        def _():
            pltpu.make_async_copy(staged.at[slot], out.at[c], sem.at[slot]).wait()

        found = [result[0, here], result[1, here]]
        if not with_gates:
            found = [(found[e].astype(f32) * gate_slot[e, here]).astype(bf16) for e in range(2)]
        found = jnp.concatenate(found, axis=0)
        staged[slot, :, :D] = dot_first(both, found).astype(bf16)
        if with_gates:
            lines = [
                jnp.sum(
                    both[e * MOST : (e + 1) * MOST].astype(f32) * dg_slot[e, here], axis=0, keepdims=True
                )
                for e in range(2)
            ]
            high = [v.astype(bf16).astype(f32) for v in lines]
            rest = [v - h for v, h in zip(lines, high)]
            lines = jnp.concatenate(high + rest + [jnp.zeros((4, ROWS), f32)], axis=0).astype(bf16)
            staged[slot, :, D:] = dot_first(lines, back).astype(bf16)
        pltpu.make_async_copy(staged.at[slot], out.at[c], sem.at[slot]).start()

    def combine(staged, out, sem, with_gates):
        def one(c, _):
            combined(c, D, staged, out, sem, with_gates)
            return 0

        lax.fori_loop(0, N_CTX, one, 0)
        for slot in range(2):
            pltpu.make_async_copy(staged.at[slot], out.at[slot], sem.at[slot]).wait()

    def chips(ref):
        return lambda chip, core: ref.at[chip * 2 + core]

    for e in range(2):
        for t in range(3):
            forth(e, t)
            if e == 0 and t < 2:
                gather.step(5 + 2 * t)
                gather.step(6 + 2 * t)
    combine(stage, out_parts, out_sem, False)
    first = RowScatter(place, chips(out_parts), *scatters[:10])
    second = RowScatter(place, chips(d_parts), *scatters[10:20])
    for n in range(8):
        first.start(n)
    gather.finish()
    first.step(0)
    first.step(1)
    lax.fori_loop(0, N_CTX, pick_tops, 0)
    plan = [(), (), (2, 3), (4, 5), (), ()]
    for e in range(2):
        for t in range(3):
            backward(e, t)
            for n in plan[3 * e + t]:
                first.step(n)
    combine(d_stage, d_parts, d_sem, True)
    for n in range(8):
        second.start(n)
    first.step(6)
    second.step(0)
    second.step(1)
    keep.wait()

    def weights(e, k):
        here = pl.ds(k * 256, 256)
        total = dot_first(rows[e, :, here], d_mid[e]).astype(bf16)
        pool[2 * k, e, 0] = total[:ROWS]
        pool[2 * k + 1, e, 0] = total[ROWS:]
        total = dot_first(hidden[e], tops[e, :, here]).astype(bf16)
        for q in range(8):
            pool[2 * k, e, 1, :64, q * ROWS : (q + 1) * ROWS] = total[q * 64 : (q + 1) * 64, :ROWS]
            pool[2 * k + 1, e, 1, :64, q * ROWS : (q + 1) * ROWS] = total[q * 64 : (q + 1) * 64, ROWS:]

    plan = [(), (), (), (), (2, 3), (), (4, 5), ()]
    for e in range(2):
        for k in range(4):
            weights(e, k)
            for n in plan[4 * e + k]:
                second.step(n)
    saves = [
        pltpu.make_async_copy(pool.at[:, :, 0], g_ref.at[:, :, :ROWS], g_sem.at[0]),
        pltpu.make_async_copy(pool.at[:, :, 1, :64], g_ref.at[:, :, ROWS:], g_sem.at[1]),
    ]
    for save in saves:
        save.start()
    reload = [
        pltpu.make_async_copy(wo_ref, wide, in_sem.at[1]),
        pltpu.make_async_copy(cot_ref, tok.at[0, 0], in_sem.at[2]),
    ]
    for load in reload:
        load.start()
    second.step(6)
    out_ref[...] = first.step(7)
    for load in reload:
        load.wait()
    total = second.step(7)
    gates = gates_ref[...]
    d_gates = pltpu.roll(total[:, D:], 64, 1) + pltpu.roll(total[:, D:], 32, 1)
    d_picked = gates * (d_gates - jnp.sum(gates * d_gates, axis=1, keepdims=True))
    d_logits = d_picked.astype(bf16)
    d_logits_ref[...] = pltpu.roll(d_picked, 2, 1).astype(bf16)
    d_hid = total[:, :D] + dot_last(d_logits, router_ref[...])
    residual = res_ref[...]
    scale = lax.rsqrt(jnp.mean(residual * residual, axis=1, keepdims=True) + epsilon)
    normed = residual * scale
    gain_grad_ref[...] = jnp.sum(d_hid * normed, axis=0, keepdims=True)
    d_normed = d_hid * gain_ref[...]
    inner = jnp.mean(d_normed * normed, axis=1, keepdims=True)
    d_res = tok[0, 0].astype(f32) + scale * (d_normed - normed * inner)
    d_res_ref[...] = d_res
    d_branch = d_res.astype(bf16)
    d_branch_ref[...] = d_branch
    for s in range(2):
        d_att = dot_last(d_branch, wide[s]).astype(bf16)
        for g in range(4):
            d_heads[4 * s + g] = d_att[:, g * 128 : (g + 1) * 128]
    copies = []
    for k in range(1, N_CTX):
        to = lax.rem(ctx + k, N_CTX)
        copies.append(
            remote(
                d_heads.at[lax.div(to, 2)], heads_ref.at[ctx], hsend.at[k], hrecv.at[k], device_at(dp, to)
            )
        )
    for copy in copies:
        copy.start()
    own = pltpu.make_async_copy(d_heads.at[lax.div(ctx, 2)], heads_ref.at[ctx], in_sem.at[3])
    own.start()
    for save in saves:
        save.wait()
    own.wait()
    for copy in copies:
        copy.wait_recv()
    for copy in copies:
        copy.wait_send()
    first.finish()
    second.finish()


def experts(tok, att, wo, members, router, gain, cot, weights, number):
    slots = N_CTX * MOST
    v = lambda *shape: pltpu.VMEM(shape, bf16)
    column = pltpu.VMEM((2, slots, 1), f32)
    blocks = (8, 2, ROWS, D)
    return pl.pallas_call(
        experts_kernel,
        out_shape=(
            jax.ShapeDtypeStruct((ROWS, D), f32),
            jax.ShapeDtypeStruct((ROWS, D), f32),
            jax.ShapeDtypeStruct((ROWS, D), f32),
            jax.ShapeDtypeStruct((ROWS, D), bf16),
            jax.ShapeDtypeStruct((ROWS, EXTRA), bf16),
            jax.ShapeDtypeStruct((1, D), f32),
            jax.ShapeDtypeStruct(weights.shape, bf16),
            jax.ShapeDtypeStruct(blocks, bf16),
            jax.ShapeDtypeStruct((N_CTX, ROWS, 128), bf16),
            jax.ShapeDtypeStruct((N_CTX, ROWS, D), bf16),
            jax.ShapeDtypeStruct((N_CTX, ROWS, D + EXTRA), bf16),
        ),
        in_specs=[ANY] * 4 + [VMEM] * 2 + [ANY] * 2,
        out_specs=(VMEM,) * 6 + (ANY,) * 5,
        scratch_shapes=[
            v(8, 2, 2, ROWS, D),
            v(N_CTX, ROWS, EXTRA),
            v(*weights.shape),
            v(2, FF, D),
            v(N_CTX, 2 * MOST, ROWS),
            column,
            column,
            v(2, slots, D),
            v(2, slots, D),
            v(2, slots, D),
            v(2, slots, FF),
            v(2, slots, 2 * FF),
            v(2, ROWS, D),
            v(2, ROWS, D + EXTRA),
            v(2, 2, ROWS, D),
            pltpu.VMEM((ROWS, EXTRA), f32),
            v(8, ROWS, 128),
            DMA((4,)),
            DMA((2,)),
            DMA((2,)),
            DMA((2,)),
            DMA((2,)),
            DMA((16,)),
            DMA((16,)),
        ]
        + RowScatter.scratch(ROWS, D)
        + RowScatter.scratch(ROWS, D + EXTRA)
        + RowGather.scratch,
        compiler_params=pltpu.CompilerParams(
            collective_id=number, has_side_effects=True, vmem_limit_bytes=61 * 2**20
        ),
        cost_estimate=pl.CostEstimate(flops=15 * 10**9, bytes_accessed=30 * 2**20, transcendentals=2**20),
        name="experts_both_ways",
    )(tok.reshape(blocks), att.reshape(blocks), wo.reshape(2, FF, D), members, router, gain, cot, weights)


def swap_halves(u):
    lane = lax.broadcasted_iota(jnp.int32, u.shape, 1)
    return jnp.where(lax.rem(lane, 64) < 32, pltpu.roll(u, 96, 1), pltpu.roll(u, 32, 1))


def attend_kernel(
    src, order, raw_ref, cos_ref, sin_ref, o_ref, padded, q_ref, k_ref, v_ref, lse_ref, out_nat
):
    core = lax.axis_index("core")
    for b in range(SEQ // BLOCK):
        rows = pl.ds(pl.multiple_of(src[b] * BLOCK, BLOCK), BLOCK)
        here = pl.ds(b * BLOCK, BLOCK)
        qk = raw_ref[rows, 0:128]
        qk = qk * cos_ref[here, :] + swap_halves(qk) * sin_ref[here, :]
        q_ref[here, :] = (qk[:, 0:64]).astype(bf16)
        k_ref[here, :] = (qk[:, 64:128]).astype(bf16)
        v_ref[here, :] = raw_ref[rows, 128:192].astype(bf16)
    step = 256
    for i in range(SEQ // step):
        length = (i + 1) * step
        here = pl.ds(i * step, step)
        scores = dot_last(q_ref[here, :], k_ref[0:length, :]) * 0.125
        row = i * step + lax.broadcasted_iota(jnp.int32, (step, length), 0)
        column = lax.broadcasted_iota(jnp.int32, (step, length), 1)
        scores = jnp.where(column <= row, scores, -1e30)
        top = jnp.max(scores, axis=1, keepdims=True)
        weights = jnp.exp(scores - top)
        total = jnp.sum(weights, axis=1, keepdims=True)
        lse_ref[here, :] = top + jnp.log(total)
        probs = (weights * (1.0 / total)).astype(bf16)
        out_nat[here, :] = dot(probs, v_ref[0:length, :])
    for b in range(SEQ // BLOCK):
        rows = pl.ds(pl.multiple_of(order[b] * BLOCK, BLOCK), BLOCK)
        here = pl.ds(b * BLOCK, BLOCK)
        out = out_nat[rows, :].astype(bf16)
        o_ref[here, :] = out
        empty = jnp.zeros_like(out)
        padded[here, :] = jnp.where(
            core == 0, jnp.concatenate([out, empty], axis=1), jnp.concatenate([empty, out], axis=1)
        )


def attend(src, order, raw, cosine, sine):
    head = jax.ShapeDtypeStruct((SEQ, HEAD_DIM), bf16)
    return pl.pallas_call(
        attend_kernel,
        out_shape=(
            head,
            jax.ShapeDtypeStruct((SEQ, 128), bf16),
            head,
            head,
            head,
            jax.ShapeDtypeStruct((SEQ, 1), f32),
        ),
        in_specs=[SMEM, SMEM, VMEM, VMEM, VMEM],
        out_specs=(VMEM,) * 6,
        scratch_shapes=[pltpu.VMEM((SEQ, HEAD_DIM), f32)],
        compiler_params=pltpu.CompilerParams(vmem_limit_bytes=48 * 2**20),
        cost_estimate=pl.CostEstimate(flops=10**9, bytes_accessed=6 * 2**20, transcendentals=2**21),
        name="attention_forward",
    )(src, order, raw, cosine, sine)


def heads_kernel(padded, att_out, mine, other, merged, msem, xsend, xrecv, *sems):
    place = my_place()
    core = place[4]
    pl.semaphore_wait(greet(chip_neighbours(place)), 4)
    half = SEQ // 2
    swap = remote(
        padded.at[pl.ds(pl.multiple_of((1 - core) * half, half), half)], other, xsend, xrecv,
        sibling_of(place),
    )
    swap.start()
    own = pltpu.make_async_copy(padded.at[pl.ds(pl.multiple_of(core * half, half), half)], mine, msem)
    own.start()
    own.wait()
    swap.wait_recv()
    merged[...] = mine[...] + other[...]

    def view(p):
        chip = p[2] * 4 + p[3]
        return att_out.at[
            pl.ds(pl.multiple_of(p[4] * half, half), half), pl.ds(pl.multiple_of(chip * 128, 128), 128)
        ]

    heads = RowGather(place, merged, view, half // 2, *sems)
    heads.start()
    heads.pass_on()
    heads.finish()
    swap.wait_send()


def gather_heads(padded, number):
    return pl.pallas_call(
        heads_kernel,
        out_shape=jax.ShapeDtypeStruct((SEQ, D), bf16),
        in_specs=[ANY],
        out_specs=ANY,
        scratch_shapes=[pltpu.VMEM((SEQ // 2, 128), bf16)] * 3 + [DMA] * 3 + RowGather.scratch,
        compiler_params=pltpu.CompilerParams(collective_id=number, has_side_effects=True),
        name="gather_heads",
    )(padded)


def attend_back_kernel(
    src, order, q_ref, k_ref, v_ref, lse_ref, do_ref, cos_ref, sin_ref, out_ref, do_nat, acc, done
):
    core = lax.axis_index("core")
    for b in range(SEQ // BLOCK):
        rows = pl.ds(pl.multiple_of(src[b] * BLOCK, BLOCK), BLOCK)
        pair = do_ref[rows, :].astype(f32)
        do_nat[pl.ds(b * BLOCK, BLOCK), :] = jnp.where(core == 0, pair[:, :64], pair[:, 64:])
    acc[...] = jnp.zeros_like(acc)
    step = 256
    for i in range(SEQ // step):
        length = (i + 1) * step
        here = pl.ds(i * step, step)
        query, d_out = q_ref[here, :], do_nat[here, :].astype(bf16)
        keys = k_ref[0:length, :]
        scores = dot_last(query, keys) * 0.125
        row = i * step + lax.broadcasted_iota(jnp.int32, (step, length), 0)
        column = lax.broadcasted_iota(jnp.int32, (step, length), 1)
        probs = jnp.where(column <= row, jnp.exp(scores - lse_ref[here, :]), 0.0)
        d_probs = dot_last(d_out, v_ref[0:length, :])
        delta = jnp.sum(probs * d_probs, axis=1, keepdims=True)
        d_scores = (probs * (d_probs - delta)).astype(bf16)
        acc[here, 0:64] = dot(d_scores, keys) * 0.125
        acc[0:length, 64:128] += dot_first(d_scores, query) * 0.125
        acc[0:length, 128:192] += dot_first(probs.astype(bf16), d_out)
    for b in range(SEQ // BLOCK):
        here = pl.ds(b * BLOCK, BLOCK)
        qk = acc[here, 0:128]
        qk = qk * cos_ref[here, :] - swap_halves(qk) * sin_ref[here, :]
        done[here, 0:128] = qk
        done[here, 128:256] = acc[here, 128:256]
    for b in range(SEQ // BLOCK):
        rows = pl.ds(pl.multiple_of(order[b] * BLOCK, BLOCK), BLOCK)
        out_ref[pl.ds(b * BLOCK, BLOCK), :] = done[rows, :].astype(bf16)


def attend_back(src, order, q, k, v, lse, d_out, cosine, sine):
    return pl.pallas_call(
        attend_back_kernel,
        out_shape=jax.ShapeDtypeStruct((SEQ, 256), bf16),
        in_specs=[SMEM, SMEM] + [VMEM] * 7,
        out_specs=VMEM,
        scratch_shapes=[
            pltpu.VMEM((SEQ, HEAD_DIM), f32),
            pltpu.VMEM((SEQ, 256), f32),
            pltpu.VMEM((SEQ, 256), f32),
        ],
        compiler_params=pltpu.CompilerParams(vmem_limit_bytes=56 * 2**20),
        cost_estimate=pl.CostEstimate(flops=3 * 10**9, bytes_accessed=6 * 2**20, transcendentals=2**21),
        name="attention_backward",
    )(src, order, q, k, v, lse, d_out, cosine, sine)


def rotary_tables():
    inverse = 10000.0 ** (-np.arange(32, dtype=np.float64) * 2.0 / HEAD_DIM)
    angles = np.arange(SEQ, dtype=np.float64)[:, None] * inverse[None, :]
    cosine, sine = np.cos(angles), np.sin(angles)
    return (
        np.tile(cosine, (1, 4)).astype(np.float32),
        np.concatenate([-sine, sine, -sine, sine], axis=1).astype(np.float32),
    )


def normalize(inputs, gain_values):
    scale_rows = lax.rsqrt(jnp.mean(inputs * inputs, axis=-1, keepdims=True) + epsilon)
    normed = inputs * scale_rows
    return (scale_rows, normed, (normed * gain_values.astype(f32)).astype(bf16))


def norm_backward(grad_in, normed, scale_rows, gain_values):
    grad_normed = grad_in * gain_values.astype(f32)
    inner = jnp.mean(grad_normed * normed, axis=-1, keepdims=True)
    return (scale_rows * (grad_normed - normed * inner), jnp.sum(grad_in * normed, axis=0))


def halves(value):
    high = lax.reduce_precision(value, 8, 7)
    return high.astype(bf16), (value - high).astype(bf16)


def local(
    tokens,
    cotangent,
    block_order,
    routes,
    norm_one,
    w_query,
    w_key,
    w_value,
    w_out,
    norm_two,
    w_router,
    expert_in,
    expert_out,
):
    ctx = lax.axis_index(CTX)
    cosine, sine = (jnp.asarray(t) for t in rotary_tables())
    order = jnp.stack([block_order, 2 * N_CTX - 1 - block_order], axis=1).reshape(-1)
    spots = jnp.arange(2 * N_CTX, dtype=jnp.int32)
    src = jnp.sum(jnp.where(order[None, :] == spots[:, None], spots[None, :], 0), axis=1)

    small = jnp.concatenate(
        [w_router, norm_one[:, None], norm_two[:, None], jnp.zeros((8, 30), bf16)], axis=1
    )
    tokens_all, packed_all, out_all, members = entry(
        tokens, w_query, w_key, w_value, small, w_out, routes, 0
    )
    down_packed = expert_out.reshape(2, 8, 64, ROWS).swapaxes(1, 2).reshape(2, 64, D)
    expert_all = lax.all_gather(jnp.concatenate([expert_in, down_packed], axis=1), DP, axis=0)
    low = packed_all[:, :, 8:, :].reshape(D, 128)
    weight = jnp.concatenate(
        [packed_all[:, :, :8, :].reshape(D, 128), low[:, :64], jnp.zeros((D, 64), bf16)], axis=1
    )
    router_weight, gain_one, gain_two = low[:, 64:96], low[:, 96], low[:, 97]
    out_weight = out_all.reshape(D, D)
    head_weight = lax.dynamic_slice_in_dim(out_weight, ctx * HEAD_DIM, HEAD_DIM, axis=0)

    tokens_float = tokens.astype(f32)
    scale_one, normed_one, _ = normalize(tokens_float, gain_one)
    _, _, hidden_one = normalize(tokens_all.reshape(SEQ, D).astype(f32), gain_one)
    raw = dot(hidden_one, weight)
    attended, padded, query, key, value, lse = attend(src, order, raw, cosine, sine)
    attended_all = gather_heads(padded, 1)

    router_wide = jnp.pad(router_weight, ((0, 0), (64, 32)))
    (
        out_sum,
        residual,
        d_residual,
        d_branch,
        d_logits,
        grad_gain_two,
        grad_experts,
        hidden_two,
        d_heads,
        _,
        _,
    ) = experts(
        tokens_all,
        attended_all,
        out_weight,
        members,
        router_wide,
        gain_two.astype(f32)[None, :],
        cotangent,
        expert_all,
        3,
    )
    output = residual + out_sum
    grad_experts = lax.psum_scatter(grad_experts, DP, scatter_dimension=0).astype(f32)
    grad_in = grad_experts[:, :ROWS]
    grad_down = grad_experts[:, ROWS:].reshape(2, 64, 8, ROWS).swapaxes(1, 2).reshape(2, FF, ROWS)

    d_raw = attend_back(src, order, query, key, value, lse, d_heads.reshape(SEQ, 128), cosine, sine)
    side = jnp.stack([1.0 / gain_one.astype(f32), grad_gain_two[0]], axis=1)
    side = jnp.pad(side, ((0, 0), (0, 126)))
    blocks = (8, 2, ROWS, D)
    d_hidden_one, a, b = last(
        d_raw,
        weight,
        side,
        d_branch,
        d_logits,
        hidden_one,
        attended_all.reshape(blocks),
        hidden_two,
        5,
    )
    d_norm_one, _ = norm_backward(d_hidden_one, normed_one, scale_one, gain_one)
    input_grad = d_residual + d_norm_one

    side_by_side = lambda v: jnp.moveaxis(v, 0, 1).reshape(8, -1)
    pairs = a.reshape(KV_HEADS, 2, 8, 256).sum(axis=1)
    common = jnp.sum(a[:, :, 192:], axis=0)
    return (
        output,
        input_grad,
        common[:, 0],
        side_by_side(a[:, :, 0:64]),
        side_by_side(pairs[:, :, 64:128]),
        side_by_side(pairs[:, :, 128:192]),
        side_by_side(b),
        common[:, 1],
        common[:, 2:34],
        grad_in,
        grad_down,
    )


def solution(mesh):
    split = Mesh(mesh.devices.reshape(2, 4, 2, 4, 2), AXES)
    rows = P(AXES, None)
    line = P(AXES)
    return jax.shard_map(
        local,
        mesh=split,
        in_specs=(
            rows,
            rows,
            P(),
            rows,
            line,
            rows,
            rows,
            rows,
            rows,
            line,
            rows,
            P(CTX, DP, None),
            P(CTX, None, DP),
        ),
        out_specs=(
            rows,
            rows,
            line,
            rows,
            rows,
            rows,
            rows,
            line,
            rows,
            P(CTX, DP, None),
            P(CTX, None, DP),
        ),
        check_vma=False,
    )
```

```python
import functools
import math

import jax
import jax.numpy as jnp
import numpy as np
from jax import lax
from jax.experimental import pallas as pl
from jax.experimental.pallas import tpu as pltpu
from jax.sharding import Mesh
from jax.sharding import PartitionSpec as P

D = 1024
HEADS = 16
KV_HEADS = 8
HEAD_DIM = 64
EXPERTS = 32
FF = 512
TOP = 8
MOST = 48
ROWS = 128
SEQ = 2048
BLOCK = 64
AXES = ("ylo", "z", "yhi", "x", "core")
DP = ("ylo", "z")
CTX = ("yhi", "x", "core")
N_DP = 8
N_CTX = 16
EXTRA = 128
MESH_ID = pl.DeviceIdType.MESH
ANY = pl.BlockSpec(memory_space=pl.ANY)
VMEM = pl.BlockSpec(memory_space=pltpu.VMEM)
SMEM = pl.BlockSpec(memory_space=pltpu.SMEM)
DMA = pltpu.SemaphoreType.DMA
bf16 = jnp.bfloat16
f32 = jnp.float32
epsilon = 1e-06


def dot(a, b):
    return jnp.dot(a, b, preferred_element_type=f32)


def dot_last(a, b):
    return lax.dot_general(a, b, (((1,), (1,)), ((), ())), preferred_element_type=f32)


def dot_first(a, b):
    return lax.dot_general(a, b, (((0,), (0,)), ((), ())), preferred_element_type=f32)


def my_place():
    return tuple(lax.axis_index(a) for a in AXES)


def device_at(dp, ctx):
    return (
        lax.div(dp, 4),
        lax.rem(dp, 4),
        lax.div(ctx, 8),
        lax.rem(lax.div(ctx, 2), 4),
        lax.rem(ctx, 2),
    )


def beside(place, dy, dx):
    ylo, z, yhi, x, core = place
    return (ylo, z, lax.rem(yhi + dy, 2), lax.rem(x + dx, 4), core)


def ctx_of(place):
    return place[2] * 8 + place[3] * 2 + place[4]


def dp_of(place):
    return place[0] * 4 + place[1]


def sibling_of(place):
    return place[:4] + (1 - place[4],)


def remote(src, dst, send, recv, device):
    return pltpu.make_async_remote_copy(
        src_ref=src, dst_ref=dst, send_sem=send, recv_sem=recv, device_id=device, device_id_type=MESH_ID
    )


def greet(devices):
    barrier = pltpu.get_barrier_semaphore()
    for device in devices:
        pl.semaphore_signal(barrier, inc=1, device_id=device, device_id_type=MESH_ID)
    return barrier


class RowGather:
    scratch = [DMA, DMA((9,)), DMA((9,)), DMA((10,)), DMA((10,))]
    links = [(1, 0), (0, 1), (0, 3), (0, 1), (0, 3), (0, 1), (0, 3), (0, 1), (0, 3)]
    held = [(0, 0), (0, 0), (0, 0), (1, 0), (1, 0), (0, 3), (0, 1), (1, 3), (1, 1)]
    parts = [None, None, None, None, None, 0, 1, 0, 1]
    after = {0: (3, 4), 1: (5,), 2: (6,), 3: (7,), 4: (8,)}

    def __init__(self, place, x_ref, view, half, local, send, recv, fsend, frecv):
        sibling = sibling_of(place)

        def piece(dy, dx, part):
            ref = view(beside(place, dy, dx))
            return ref if part is None else ref.at[pl.ds(part * half, half)]

        self.own = pltpu.make_async_copy(x_ref, view(place), local)
        self.out, self.landed, self.passed = [], [], []
        for n, ((ly, lx), (hy, hx), part) in enumerate(zip(self.links, self.held, self.parts)):
            source = x_ref if n < 3 else piece(hy, hx, part)
            self.out.append(
                remote(source, piece(hy, hx, part), send.at[n], recv.at[n], beside(place, ly, lx))
            )
            here = piece((hy + ly) % 2, (hx + 4 - lx) % 4, part)
            self.landed.append(remote(here, here, send.at[n], recv.at[n], beside(place, ly, lx)))
            self.passed.append(remote(here, here, fsend.at[n], frecv.at[n], sibling))
        self.passed.append(remote(x_ref, view(place), fsend.at[9], frecv.at[9], sibling))
        self.back = []
        for n in range(9):
            (ly, lx), (hy, hx), part = self.links[n], self.held[n], self.parts[n]
            ref = view(sibling_of(beside(place, (hy + ly) % 2, (hx + 4 - lx) % 4)))
            ref = ref if part is None else ref.at[pl.ds(part * half, half)]
            self.back.append(remote(ref, ref, fsend.at[n], frecv.at[n], sibling))
        ref = view(sibling)
        self.back.append(remote(ref, ref, fsend.at[9], frecv.at[9], sibling))

    def start(self):
        for n in range(3):
            self.out[n].start()
        self.passed[9].start()
        self.own.start()

    def step(self, n):
        self.landed[n].wait_recv()
        for m in self.after.get(n, ()):
            self.out[m].start()
        self.passed[n].start()

    def pass_on(self):
        for n in range(9):
            self.step(n)

    def finish(self):
        self.own.wait()
        for n in range(10):
            self.back[n].wait_recv()
        for copy in self.out + self.passed:
            copy.wait_send()


def chip_neighbours(place):
    return [beside(place, 1, 0), beside(place, 0, 1), beside(place, 0, 3), sibling_of(place)]


SPREAD = [(1, 2), (0, 2), (1, 1), (1, 3), (0, 1), (0, 3), (1, 0), (0, 0)]


class RowScatter:
    @staticmethod
    def scratch(rows, width):
        return [
            pltpu.VMEM((8, rows, width), bf16),
            pltpu.VMEM((8, rows, width), bf16),
            pltpu.VMEM((4, rows // 2, width), bf16),
            pltpu.VMEM((4, rows, width), bf16),
            pltpu.VMEM((rows, width), bf16),
            DMA((8,)),
            DMA((8,)),
            DMA((8,)),
            DMA((9,)),
            DMA((9,)),
        ]

    def __init__(self, place, part, own, other, halves, wholes, last, own_sem, fsend, frecv, send, recv):
        self.own, self.other, self.halves, self.wholes, self.last = own, other, halves, wholes, last
        core = place[4]
        half = own.shape[1] // 2
        self.half = half
        self.mine, self.cross = [], []
        for n, (dy, dx) in enumerate(SPREAD):
            chip = lax.div(ctx_of(beside(place, dy, dx)), 2)
            self.mine.append(pltpu.make_async_copy(part(chip, core), own.at[n], own_sem.at[n]))
            self.cross.append(
                remote(part(chip, 1 - core), other.at[n], fsend.at[n], frecv.at[n], sibling_of(place))
            )
        right, left = beside(place, 0, 1), beside(place, 0, 3)
        self.out = []
        for n, (source, target, device) in enumerate(
            [
                (own.at[0, pl.ds(0, half)], halves.at[0], right),
                (own.at[0, pl.ds(half, half)], halves.at[1], left),
                (own.at[1, pl.ds(0, half)], halves.at[2], right),
                (own.at[1, pl.ds(half, half)], halves.at[3], left),
                (own.at[2], wholes.at[0], right),
                (own.at[3], wholes.at[1], left),
                (own.at[4], wholes.at[2], right),
                (own.at[5], wholes.at[3], left),
                (own.at[6], last, beside(place, 1, 0)),
            ]
        ):
            self.out.append(remote(source, target, send.at[n], recv.at[n], device))

    def start(self, n):
        self.cross[n].start()
        self.mine[n].start()

    def release(self):
        for n in range(8):
            self.cross[n].wait_send()

    def join(self, n):
        self.mine[n].wait()
        self.cross[n].wait_recv()
        return self.own[n].astype(f32) + self.other[n].astype(f32)

    def step(self, n):
        if n < 2:
            self.own[n] = self.join(n).astype(bf16)
            self.out[2 * n].start()
            self.out[2 * n + 1].start()
        elif n < 6:
            total = self.join(n)
            half = self.half
            side = pl.ds(0 if n % 2 == 0 else half, half)
            self.out[n - 2].wait_recv()
            self.own[n] = total.astype(bf16)
            first = total[:half] if n % 2 == 0 else total[half:]
            self.own[n, side] = (first + self.halves[n - 2].astype(f32)).astype(bf16)
            self.out[n + 2].start()
        elif n == 6:
            total = self.join(6)
            for m in (0, 1):
                self.out[4 + m].wait_recv()
                total = total + self.wholes[m].astype(f32)
            self.own[6] = total.astype(bf16)
            self.out[8].start()
        else:
            total = self.join(7)
            for m in (2, 3):
                self.out[4 + m].wait_recv()
                total = total + self.wholes[m].astype(f32)
            self.out[8].wait_recv()
            return total + self.last[...].astype(f32)

    def finish(self):
        for copy in self.out:
            copy.wait_send()


def entry_kernel(
    x_ref, q_ref, k_ref, v_ref, small_ref, o_ref, routes_ref, x_out, w_out, o_out, m_out,
    w_pack, o_pad, o_other, o_mid, m_pack, *sems,
):
    row_sems, o_sems, m_sems, rest = sems[:5], sems[5:10], sems[10:15], sems[15:]
    wlocal, wsend, wrecv, psend, precv, xsend, xrecv, osend, orecv = rest
    place = my_place()
    core = place[4]
    dp, ctx = dp_of(place), ctx_of(place)
    barrier = greet(
        [device_at(dp, lax.rem(ctx + k, N_CTX)) for k in range(1, N_CTX)]
        + [device_at(lax.rem(dp + k, N_DP), ctx) for k in range(1, N_DP)]
    )
    pl.semaphore_wait(barrier, 22)
    rows = RowGather(place, x_ref, lambda p: x_out.at[ctx_of(p)], x_ref.shape[0] // 2, *row_sems)
    rows.start()

    out = o_ref[...].astype(f32)
    empty = jnp.zeros_like(out)
    out = jnp.where(core == 0, jnp.concatenate([out, empty], 0), jnp.concatenate([empty, out], 0))
    for s in range(2):
        o_pad[s] = out[:, s * 512 : (s + 1) * 512].astype(bf16)
    swap = remote(o_pad.at[1 - core], o_other, xsend, xrecv, sibling_of(place))
    swap.start()
    query, key, value = (r[...].astype(f32) for r in (q_ref, k_ref, v_ref))
    small = small_ref[...].astype(f32)
    for h in range(HEADS):
        at, pair = slice(h * 64, h * 64 + 64), slice(h // 2 * 64, h // 2 * 64 + 64)
        top = jnp.concatenate([query[:, at], key[:, pair]], axis=1)
        low = jnp.concatenate([value[:, pair], small], axis=1)
        w_pack[h] = jnp.concatenate([top, low], axis=0).astype(bf16)
    first, second, third = [], [], []
    for k in range(1, N_CTX):
        to = lax.rem(ctx + k, N_CTX)
        first.append(
            remote(w_pack.at[to], w_out.at[dp, ctx], wsend.at[k], wrecv.at[k], device_at(dp, to))
        )
    for k in range(1, N_DP):
        device = device_at(lax.rem(dp + k, N_DP), ctx)
        third.append(remote(o_mid.at[dp], o_mid.at[dp], osend.at[k], orecv.at[k], device))
        second.append(remote(w_out.at[dp], w_out.at[dp], psend.at[k], precv.at[k], device))
    for copy in first:
        copy.start()
    own = pltpu.make_async_copy(w_pack.at[ctx], w_out.at[dp, ctx], wlocal)
    own.start()
    swap.wait_recv()
    o_mid[dp] = o_pad[core] + o_other[...]
    for copy in third:
        copy.start()
    routes = routes_ref[...]
    lane = lax.broadcasted_iota(jnp.int32, (ROWS, EXTRA), 1) - 64
    member = jnp.zeros((ROWS, EXTRA), f32)
    for k in range(TOP):
        member = jnp.where(lane == routes[:, k : k + 1], 1.0, member)
    m_pack[...] = member.astype(bf16)
    members = RowGather(place, m_pack, lambda p: m_out.at[ctx_of(p)], ROWS // 2, *m_sems)
    members.start()
    own.wait()
    for copy in first:
        copy.wait_recv()
    for copy in second:
        copy.start()
    for copy in third:
        copy.wait_recv()

    def o_view(p):
        return o_out.at[:, p[2] * 4 + p[3], :, pl.ds(pl.multiple_of(p[4] * 512, 512), 512)]

    outs = RowGather(place, o_mid, o_view, 4, *o_sems)
    outs.start()
    for n in range(5):
        rows.step(n)
    for n in range(9):
        members.step(n)
    for n in range(3):
        outs.step(n)
    for n in range(5, 9):
        rows.step(n)
    for n in range(3, 9):
        outs.step(n)
    rows.finish()
    members.finish()
    outs.finish()
    for copy in second:
        copy.wait_recv()
    swap.wait_send()
    for copy in first + second + third:
        copy.wait_send()


def entry(x, query, key, value, small, out, routes, number):
    return pl.pallas_call(
        entry_kernel,
        out_shape=(
            jax.ShapeDtypeStruct((N_CTX,) + x.shape, bf16),
            jax.ShapeDtypeStruct((N_DP, N_CTX, 16, 128), bf16),
            jax.ShapeDtypeStruct((N_DP, 8, 16, D), bf16),
            jax.ShapeDtypeStruct((N_CTX, ROWS, EXTRA), bf16),
        ),
        in_specs=[ANY] + [VMEM] * 6,
        out_specs=(ANY,) * 4,
        scratch_shapes=[
            pltpu.VMEM((N_CTX, 16, 128), bf16),
            pltpu.VMEM((2, 16, 512), bf16),
            pltpu.VMEM((16, 512), bf16),
            pltpu.VMEM((N_DP, 16, 512), bf16),
            pltpu.VMEM((ROWS, EXTRA), bf16),
        ]
        + RowGather.scratch * 3
        + [DMA, DMA((16,)), DMA((16,)), DMA((8,)), DMA((8,)), DMA, DMA, DMA((8,)), DMA((8,))],
        compiler_params=pltpu.CompilerParams(
            collective_id=number, has_side_effects=True, vmem_limit_bytes=16 * 2**20
        ),
        name="entry_gather",
    )(x, query, key, value, small, out, routes)


def last_kernel(
    d_raw, weight, side, d_branch, d_logits, hidden_ref, att_ref, hid_ref, one_ref, a_out, w_out,
    hidden, att, hid, parts, w_parts, a_pack, landed, part, w_sum, w_landed, w_mine,
    in_sem, wlocal, wsend, wrecv, psend, precv, plocal, osend, orecv, olocal, xsend, xrecv, *scatters,
):
    place = my_place()
    core = place[4]
    dp, ctx = dp_of(place), ctx_of(place)
    barrier = greet(
        [device_at(dp, lax.rem(ctx + k, N_CTX)) for k in range(1, N_CTX)]
        + [device_at(lax.rem(dp + k, N_DP), ctx) for k in range(1, N_DP)]
    )
    loads = [
        pltpu.make_async_copy(att_ref.at[lax.div(ctx, 2), core], att, in_sem.at[0]),
        pltpu.make_async_copy(hid_ref, hid, in_sem.at[1]),
        pltpu.make_async_copy(hidden_ref, hidden, in_sem.at[2]),
    ]
    for load in loads:
        load.start()

    def back(c, _):
        here = pl.ds(pl.multiple_of(c * ROWS, ROWS), ROWS)
        parts[lax.div(c, 2), lax.rem(c, 2)] = dot_last(d_raw[here, :], weight[...]).astype(bf16)
        return 0

    lax.fori_loop(0, N_CTX, back, 0)
    pl.semaphore_wait(barrier, 22)
    rows = RowScatter(place, lambda chip, c: parts.at[chip, c], *scatters[:10])
    outs = RowScatter(place, lambda chip, c: w_parts.at[chip, c], *scatters[10:])
    for n in range(8):
        rows.start(n)
    for load in loads:
        load.wait()

    def heads(k, _):
        here = pl.ds(pl.multiple_of(k * ROWS, ROWS), ROWS)
        grad = dot_first(hidden[:, here], d_raw[...])
        gain = jnp.sum(grad * weight[here, :].astype(f32), axis=1, keepdims=True)
        lane = lax.broadcasted_iota(jnp.int32, (ROWS, 128), 1)
        extra = side[here, :]
        high = grad[:, 128:] + dot_first(hid[:, here], d_logits[...])
        high = jnp.where(lane == 64, gain * extra[:, 0:1], jnp.where(lane == 65, extra[:, 1:2], high))
        a_pack[k, :, :128] = grad[:, :128].astype(bf16)
        a_pack[k, :, 128:] = high.astype(bf16)
        return 0

    lax.fori_loop(0, N_DP, heads, 0)
    first, second, third = [], [], []
    for k in range(1, N_DP):
        to = lax.rem(dp + k, N_DP)
        first.append(remote(a_pack.at[to], landed.at[k], wsend.at[k], wrecv.at[k], device_at(to, ctx)))
        third.append(
            remote(
                w_sum.at[pl.ds(pl.multiple_of(to * 16, 16), 16)],
                w_landed.at[k],
                osend.at[k],
                orecv.at[k],
                device_at(to, ctx),
            )
        )
    for copy in first:
        copy.start()
    own = pltpu.make_async_copy(a_pack.at[dp], landed.at[0], wlocal)
    own.start()
    rows.step(0)
    rows.step(1)

    def products(k, _):
        here = pl.ds(pl.multiple_of(k * ROWS, ROWS), ROWS)
        total = dot_first(att[:, here], d_branch[...]).astype(bf16)
        to = pl.ds(pl.multiple_of(k * 16, 16), 16)
        for g in range(8):
            for c in range(2):
                w_parts[g, c, to, :] = total[g * 16 : (g + 1) * 16, c * 512 : (c + 1) * 512]
        return 0

    lax.fori_loop(0, N_DP, products, 0)
    for n in range(8):
        outs.start(n)
    for n in range(2, 6):
        rows.step(n)
    outs.step(0)
    outs.step(1)
    own.wait()
    for copy in first:
        copy.wait_recv()
    total = landed[0].astype(f32)
    for k in range(1, N_DP):
        total = total + landed[k].astype(f32)
    part[...] = total.reshape(part.shape)
    for k in range(1, N_CTX):
        to = lax.rem(ctx + k, N_CTX)
        second.append(remote(part.at[to], a_out.at[ctx], psend.at[k], precv.at[k], device_at(dp, to)))
    for copy in second:
        copy.start()
    mine = pltpu.make_async_copy(part.at[ctx], a_out.at[ctx], plocal)
    mine.start()
    rows.step(6)
    for n in range(2, 6):
        outs.step(n)
    one_ref[...] = rows.step(7)
    outs.step(6)
    w_sum[...] = outs.step(7)
    for copy in third:
        copy.start()
    own = pltpu.make_async_copy(w_sum.at[pl.ds(pl.multiple_of(dp * 16, 16), 16)], w_landed.at[0], olocal)
    own.start()
    own.wait()
    for copy in third:
        copy.wait_recv()
    total = w_landed[0]
    for k in range(1, N_DP):
        total = total + w_landed[k]
    w_mine[...] = total.reshape(2, 8, 512)
    swap = remote(w_mine.at[1 - core], w_out.at[core], xsend, xrecv, sibling_of(place))
    swap.start()
    keep = pltpu.make_async_copy(w_mine.at[core], w_out.at[core], in_sem.at[0])
    swap_in = remote(w_mine.at[1 - core], w_out.at[1 - core], xsend, xrecv, sibling_of(place))
    swap_in.wait_recv()
    swap.wait_send()
    keep.start()
    keep.wait()
    mine.wait()
    for copy in second:
        copy.wait_recv()
    rows.release()
    outs.release()
    rows.finish()
    outs.finish()
    for copy in first + second + third:
        copy.wait_send()


def last(d_raw, weight, side, d_branch, d_logits, hidden, att, hid, number):
    v = lambda *shape: pltpu.VMEM(shape, bf16)
    return pl.pallas_call(
        last_kernel,
        out_shape=(
            jax.ShapeDtypeStruct((ROWS, D), f32),
            jax.ShapeDtypeStruct((N_CTX, 8, 256), f32),
            jax.ShapeDtypeStruct((2, 8, 512), f32),
        ),
        in_specs=[VMEM] * 5 + [ANY] * 3,
        out_specs=(VMEM,) * 3,
        scratch_shapes=[
            v(SEQ, D),
            v(ROWS, D),
            v(ROWS, D),
            v(8, 2, ROWS, D),
            v(8, 2, ROWS, 512),
            v(N_DP, ROWS, 256),
            v(N_DP, ROWS, 256),
            pltpu.VMEM((N_CTX, 8, 256), f32),
            pltpu.VMEM((ROWS, 512), f32),
            pltpu.VMEM((N_DP, 16, 512), f32),
            pltpu.VMEM((2, 8, 512), f32),
            DMA((3,)),
            DMA,
            DMA((8,)),
            DMA((8,)),
            DMA((16,)),
            DMA((16,)),
            DMA,
            DMA((8,)),
            DMA((8,)),
            DMA,
            DMA,
            DMA,
        ]
        + RowScatter.scratch(ROWS, D)
        + RowScatter.scratch(ROWS, 512),
        compiler_params=pltpu.CompilerParams(
            collective_id=number, has_side_effects=True, vmem_limit_bytes=48 * 2**20
        ),
        name="last_sums",
    )(d_raw, weight, side, d_branch, d_logits, hidden, att, hid)


def experts_kernel(
    tok_ref, att_ref, wo_ref, m_ref, router_ref, gain_ref, cot_ref, w_ref,
    out_ref, res_ref, d_res_ref, d_branch_ref, d_logits_ref, hid_ref, gain_grad_ref, g_ref, heads_ref,
    pool, members, win, wide, picks, facts_all, gates_all, logits_all, gate_slot, dg_slot,
    rows, tops, result, hidden, d_mid, own_rows, d_heads,
    in_sem, tok_sem, hsend, hrecv, *scatters,
):
    body = pl.ds(0, D)
    loads = [
        pltpu.make_async_copy(wo_ref, wide, in_sem.at[0]),
        pltpu.make_async_copy(m_ref, members, in_sem.at[1]),
        pltpu.make_async_copy(w_ref, win, in_sem.at[2]),
    ]
    place = my_place()
    core = place[4]
    dp, ctx = dp_of(place), ctx_of(place)
    chip = lax.div(ctx, 2)

    def tokens_of(i):
        return result.at[i // 3, pl.ds(i % 3 * 256, 256)] if i < 6 else tops.at[0, pl.ds((i - 6) * 256, 256)]

    streams = []
    for i in range(8):
        streams.append(
            (
                pltpu.make_async_copy(tok_ref.at[i], tokens_of(i), tok_sem.at[0, i]),
                pltpu.make_async_copy(att_ref.at[i], pool.at[i, :, 0, :, body], tok_sem.at[1, i]),
            )
        )
    loads[0].start()
    for pair in streams[:2]:
        pair[0].start()
        pair[1].start()
    pl.semaphore_wait(greet([device_at(dp, lax.rem(ctx + k, N_CTX)) for k in range(1, N_CTX)]), 15)
    gather = RowGather(
        place,
        cot_ref,
        lambda p: pool.at[p[2] * 4 + p[3], p[4], 1, :, body],
        ROWS // 2,
        *scatters[20:],
    )
    gather.start()
    for pair in streams[2:]:
        pair[0].start()
        pair[1].start()
    for load in loads[1:]:
        load.start()
    line = lax.broadcasted_iota(jnp.int32, (8, EXTRA), 0)
    lane = lax.broadcasted_iota(jnp.int32, (8, EXTRA), 1)
    chosen = jnp.logical_and(line < 2, lane == 64 + 2 * ctx + line)
    chosen = jnp.where(chosen, 1.0, 0.0).astype(bf16)
    back = jnp.logical_and(line < 4, lane == jnp.where(line < 2, 0, 32) + 2 * ctx + lax.rem(line, 2))
    back = jnp.where(back, 1.0, 0.0).astype(bf16)
    before = lax.broadcasted_iota(jnp.int32, (ROWS, ROWS), 0) < lax.broadcasted_iota(
        jnp.int32, (ROWS, ROWS), 1
    )
    before = jnp.where(before, 1.0, 0.0).astype(bf16)
    slots = lax.broadcasted_iota(jnp.int32, (MOST, ROWS), 0).astype(f32)

    def second_norm(token, att):
        residual = token.astype(f32) + dot(att[:, :FF], wide[0]) + dot(att[:, FF:], wide[1])
        scale = lax.rsqrt(jnp.mean(residual * residual, axis=1, keepdims=True) + epsilon)
        normed = residual * scale
        return residual, scale, normed, (normed * gain_ref[...]).astype(bf16)

    def gates_of(logits, inside):
        logits = jnp.where(inside > 0.5, logits, -1e30)
        weights = jnp.exp(logits - jnp.max(logits, axis=1, keepdims=True))
        weights = jnp.where(inside > 0.5, weights, 0.0)
        return weights / jnp.sum(weights, axis=1, keepdims=True)

    loads[0].wait()
    for i in range(8):
        for copy in streams[i]:
            copy.wait()
        att = pool[i, :, 0, :, :D].reshape(2 * ROWS, D)
        token = (
            result[i // 3, i % 3 * 256 : i % 3 * 256 + 256]
            if i < 6
            else tops[0, (i - 6) * 256 : (i - 5) * 256]
        )
        hid = second_norm(token, att)[3]
        pool[i, :, 0, :, :D] = hid.reshape(2, ROWS, D)
        logits_all[i * 256 : (i + 1) * 256] = dot(hid, router_ref[...])
        if i == 2:
            gather.step(0)
    gather.step(1)
    gather.step(2)
    loads[1].wait()
    for half in range(2):
        inside = members[8 * half : 8 * half + 8].reshape(8 * ROWS, EXTRA)
        gates = gates_of(logits_all[1024 * half : 1024 * (half + 1)], inside.astype(f32))
        high = gates.astype(bf16)
        rest = (gates - high.astype(f32)).astype(bf16)
        facts = dot_last(chosen, inside)
        lines = dot_last(chosen, high) + dot_last(chosen, rest)
        for c in range(8):
            facts_all[8 * half + c] = facts[:, c * ROWS : (c + 1) * ROWS]
            gates_all[8 * half + c] = lines[:, c * ROWS : (c + 1) * ROWS]

    def pick(i, _):
        for k in range(4):
            c = i * 4 + k
            facts, lines = facts_all[c], gates_all[c]
            order = dot(facts.astype(bf16), before)
            here = pl.ds(pl.multiple_of(c * MOST, MOST), MOST)
            both = []
            for e in range(2):
                member = facts[e : e + 1]
                onehot = jnp.where(jnp.logical_and(order[e : e + 1] == slots, member > 0.5), 1.0, 0.0)
                gate_slot[e, here] = jnp.sum(onehot * lines[e : e + 1], axis=1, keepdims=True)
                both.append(onehot.astype(bf16))
            both = jnp.concatenate(both, axis=0)
            picks[c] = both
            taken = dot(both, pool[i * 2 + k // 2, k % 2, 0, :, :D]).astype(bf16)
            rows[0, here] = taken[:MOST]
            rows[1, here] = taken[MOST:]
        return 0

    lax.fori_loop(0, 4, pick, 0)
    for n in range(3, 5):
        gather.step(n)
    loads[2].wait()
    for e in range(2):
        for k in range(N_DP):
            for q in range(8):
                wide[e, q * 64 : (q + 1) * 64, k * ROWS : (k + 1) * ROWS] = win[
                    k, e, ROWS:, q * ROWS : (q + 1) * ROWS
                ]
    tile = 256

    def pick_tops(i, _):
        for k in range(4):
            c = i * 4 + k
            here = pl.ds(pl.multiple_of(c * MOST, MOST), MOST)
            taken = dot(picks[c], pool[i * 2 + k // 2, k % 2, 1, :, :D]).astype(bf16)
            tops[0, here] = taken[:MOST]
            tops[1, here] = taken[MOST:]
        return 0

    def forth(e, t):
        here = pl.ds(t * tile, tile)
        both = dot(rows[e, here], win[:, e, :ROWS].reshape(D, 2 * FF))
        gate_part, up_part = both[:, :FF], both[:, FF:]
        sigmoid = 1.0 / (1.0 + jnp.exp(-gate_part))
        silu = gate_part * sigmoid
        middle = (silu * up_part).astype(bf16)
        hidden[e, here] = middle
        d_mid[e, here, :FF] = (up_part * (sigmoid * (1.0 + gate_part * (1.0 - sigmoid)))).astype(bf16)
        d_mid[e, here, FF:] = silu.astype(bf16)
        result[e, here] = dot(middle, wide[e]).astype(bf16)

    def backward(e, t):
        here = pl.ds(t * tile, tile)
        top = tops[e, here].astype(f32)
        dg_slot[e, here] = jnp.sum(top * result[e, here].astype(f32), axis=1, keepdims=True)
        d_result = (top * gate_slot[e, here]).astype(bf16)
        tops[e, here] = d_result
        d_middle = dot_last(d_result, wide[e])
        d_mid[e, here, :FF] = (d_middle * d_mid[e, here, :FF].astype(f32)).astype(bf16)
        d_mid[e, here, FF:] = (d_middle * d_mid[e, here, FF:].astype(f32)).astype(bf16)
        weight = win[:, e, :ROWS].reshape(D, 2 * FF)
        result[e, here] = dot_last(d_mid[e, here], weight).astype(bf16)

    def combine_out(i, _):
        for k in range(4):
            c = i * 4 + k
            here = pl.ds(pl.multiple_of(c * MOST, MOST), MOST)
            found = [(result[e, here].astype(f32) * gate_slot[e, here]).astype(bf16) for e in range(2)]
            found = jnp.concatenate(found, axis=0)
            pool[i * 2 + k // 2, k % 2, 0, :, :D] = dot_first(picks[c], found).astype(bf16)
        return 0

    def combine_back(i, _):
        for k in range(4):
            c = i * 4 + k
            here = pl.ds(pl.multiple_of(c * MOST, MOST), MOST)
            both = picks[c]
            found = jnp.concatenate([result[0, here], result[1, here]], axis=0)
            pool[i * 2 + k // 2, k % 2, 1, :, :D] = dot_first(both, found).astype(bf16)
            lines = [
                jnp.sum(
                    both[e * MOST : (e + 1) * MOST].astype(f32) * dg_slot[e, here], axis=0, keepdims=True
                )
                for e in range(2)
            ]
            high = [v.astype(bf16).astype(f32) for v in lines]
            rest = [v - h for v, h in zip(lines, high)]
            lines = jnp.concatenate(high + rest + [jnp.zeros((4, ROWS), f32)], axis=0).astype(bf16)
            pool[i * 2 + k // 2, k % 2, 1, :, D:] = dot_first(lines, back).astype(bf16)
        return 0

    for e in range(2):
        for t in range(3):
            forth(e, t)
            if e == 0 and t < 2:
                gather.step(5 + 2 * t)
                gather.step(6 + 2 * t)
    lax.fori_loop(0, 4, combine_out, 0)
    first = RowScatter(place, lambda h, c: pool.at[h, c, 0, :, body], *scatters[:10])
    second = RowScatter(place, lambda h, c: pool.at[h, c, 1], *scatters[10:20])
    for n in range(8):
        first.start(n)
    gather.finish()
    first.step(0)
    first.step(1)
    lax.fori_loop(0, 4, pick_tops, 0)
    plan = [(), (), (2, 3), (4, 5), (), ()]
    for e in range(2):
        for t in range(3):
            backward(e, t)
            for n in plan[3 * e + t]:
                first.step(n)
    lax.fori_loop(0, 4, combine_back, 0)
    for n in range(8):
        second.start(n)
    first.step(6)
    second.step(0)
    second.step(1)
    reload = [
        pltpu.make_async_copy(wo_ref, wide, in_sem.at[0]),
        pltpu.make_async_copy(cot_ref, own_rows.at[0], in_sem.at[1]),
        pltpu.make_async_copy(tok_ref.at[chip, pl.ds(core * ROWS, ROWS)], own_rows.at[1], tok_sem.at[0, 0]),
        pltpu.make_async_copy(att_ref.at[chip, core], own_rows.at[2], tok_sem.at[0, 1]),
    ]

    def weights(e, k):
        here = pl.ds(k * 256, 256)
        total = dot_first(rows[e, :, here], d_mid[e]).astype(bf16)
        win[2 * k, e, :ROWS] = total[:ROWS]
        win[2 * k + 1, e, :ROWS] = total[ROWS:]
        total = dot_first(hidden[e], tops[e, :, here]).astype(bf16)
        for q in range(8):
            win[2 * k, e, ROWS:, q * ROWS : (q + 1) * ROWS] = total[q * 64 : (q + 1) * 64, :ROWS]
            win[2 * k + 1, e, ROWS:, q * ROWS : (q + 1) * ROWS] = total[q * 64 : (q + 1) * 64, ROWS:]

    for copy in reload:
        copy.start()
    plan = [(), (), (), (), (2, 3), (), (4, 5), ()]
    for e in range(2):
        for k in range(4):
            weights(e, k)
            for n in plan[4 * e + k]:
                second.step(n)
    save = pltpu.make_async_copy(win, g_ref, in_sem.at[2])
    save.start()
    for copy in reload:
        copy.wait()
    residual, scale, normed, hid = second_norm(own_rows[1], own_rows[2])
    res_ref[...] = residual
    hid_ref[...] = hid
    gates = gates_of(dot(hid, router_ref[...]), members[ctx].astype(f32))
    second.step(6)
    out_ref[...] = first.step(7)
    total = second.step(7)
    d_gates = pltpu.roll(total[:, D:], 64, 1) + pltpu.roll(total[:, D:], 32, 1)
    d_picked = gates * (d_gates - jnp.sum(gates * d_gates, axis=1, keepdims=True))
    d_logits = d_picked.astype(bf16)
    d_logits_ref[...] = pltpu.roll(d_picked, 2, 1).astype(bf16)
    d_hid = total[:, :D] + dot_last(d_logits, router_ref[...])
    gain_grad_ref[...] = jnp.sum(d_hid * normed, axis=0, keepdims=True)
    d_normed = d_hid * gain_ref[...]
    inner = jnp.mean(d_normed * normed, axis=1, keepdims=True)
    d_res = own_rows[0].astype(f32) + scale * (d_normed - normed * inner)
    d_res_ref[...] = d_res
    d_branch = d_res.astype(bf16)
    d_branch_ref[...] = d_branch
    for s in range(2):
        d_att = dot_last(d_branch, wide[s]).astype(bf16)
        for g in range(4):
            d_heads[4 * s + g] = d_att[:, g * 128 : (g + 1) * 128]
    copies = []
    for k in range(1, N_CTX):
        to = lax.rem(ctx + k, N_CTX)
        copies.append(
            remote(
                d_heads.at[lax.div(to, 2)], heads_ref.at[ctx], hsend.at[k], hrecv.at[k], device_at(dp, to)
            )
        )
    for copy in copies:
        copy.start()
    own = pltpu.make_async_copy(d_heads.at[lax.div(ctx, 2)], heads_ref.at[ctx], in_sem.at[0])
    own.start()
    save.wait()
    own.wait()
    for copy in copies:
        copy.wait_recv()
    for copy in copies:
        copy.wait_send()
    first.release()
    second.release()
    first.finish()
    second.finish()


def experts(tok, att, wo, members, router, gain, cot, weights, number):
    slots = N_CTX * MOST
    v = lambda *shape: pltpu.VMEM(shape, bf16)
    column = pltpu.VMEM((2, slots, 1), f32)
    blocks = (8, 2, ROWS, D)
    return pl.pallas_call(
        experts_kernel,
        out_shape=(
            jax.ShapeDtypeStruct((ROWS, D), f32),
            jax.ShapeDtypeStruct((ROWS, D), f32),
            jax.ShapeDtypeStruct((ROWS, D), f32),
            jax.ShapeDtypeStruct((ROWS, D), bf16),
            jax.ShapeDtypeStruct((ROWS, EXTRA), bf16),
            jax.ShapeDtypeStruct((ROWS, D), bf16),
            jax.ShapeDtypeStruct((1, D), f32),
            jax.ShapeDtypeStruct(weights.shape, bf16),
            jax.ShapeDtypeStruct((N_CTX, ROWS, 128), bf16),
        ),
        in_specs=[ANY] * 4 + [VMEM] * 2 + [ANY] * 2,
        out_specs=(VMEM,) * 7 + (ANY,) * 2,
        scratch_shapes=[
            v(8, 2, 2, ROWS, D + EXTRA),
            v(N_CTX, ROWS, EXTRA),
            v(*weights.shape),
            v(2, FF, D),
            v(N_CTX, 2 * MOST, ROWS),
            pltpu.VMEM((N_CTX, 8, ROWS), f32),
            pltpu.VMEM((N_CTX, 8, ROWS), f32),
            pltpu.VMEM((SEQ, EXTRA), f32),
            column,
            column,
            v(2, slots, D),
            v(2, slots, D),
            v(2, slots, D),
            v(2, slots, FF),
            v(2, slots, 2 * FF),
            v(3, ROWS, D),
            v(8, ROWS, 128),
            DMA((3,)),
            DMA((2, 8)),
            DMA((16,)),
            DMA((16,)),
        ]
        + RowScatter.scratch(ROWS, D)
        + RowScatter.scratch(ROWS, D + EXTRA)
        + RowGather.scratch,
        compiler_params=pltpu.CompilerParams(
            collective_id=number, has_side_effects=True, vmem_limit_bytes=61 * 2**20
        ),
        cost_estimate=pl.CostEstimate(flops=15 * 10**9, bytes_accessed=30 * 2**20, transcendentals=2**20),
        name="experts_both_ways",
    )(tok.reshape(8, 2 * ROWS, D), att.reshape(blocks), wo.reshape(2, FF, D), members, router, gain, cot, weights)


def swap_halves(u):
    lane = lax.broadcasted_iota(jnp.int32, u.shape, 1)
    return jnp.where(lax.rem(lane, 64) < 32, pltpu.roll(u, 96, 1), pltpu.roll(u, 32, 1))


def attend_kernel(
    src, order, raw_ref, cos_ref, sin_ref, o_ref, padded, q_ref, k_ref, v_ref, lse_ref, out_nat
):
    core = lax.axis_index("core")
    for b in range(SEQ // BLOCK):
        rows = pl.ds(pl.multiple_of(src[b] * BLOCK, BLOCK), BLOCK)
        here = pl.ds(b * BLOCK, BLOCK)
        qk = raw_ref[rows, 0:128]
        qk = qk * cos_ref[here, :] + swap_halves(qk) * sin_ref[here, :]
        q_ref[here, :] = (qk[:, 0:64]).astype(bf16)
        k_ref[here, :] = (qk[:, 64:128]).astype(bf16)
        v_ref[here, :] = raw_ref[rows, 128:192].astype(bf16)
    step = 256
    for i in range(SEQ // step):
        length = (i + 1) * step
        here = pl.ds(i * step, step)
        scores = dot_last(q_ref[here, :], k_ref[0:length, :]) * 0.125
        row = i * step + lax.broadcasted_iota(jnp.int32, (step, length), 0)
        column = lax.broadcasted_iota(jnp.int32, (step, length), 1)
        scores = jnp.where(column <= row, scores, -1e30)
        top = jnp.max(scores, axis=1, keepdims=True)
        weights = jnp.exp(scores - top)
        total = jnp.sum(weights, axis=1, keepdims=True)
        lse_ref[here, :] = top + jnp.log(total)
        probs = (weights * (1.0 / total)).astype(bf16)
        out_nat[here, :] = dot(probs, v_ref[0:length, :])
    for b in range(SEQ // BLOCK):
        rows = pl.ds(pl.multiple_of(order[b] * BLOCK, BLOCK), BLOCK)
        here = pl.ds(b * BLOCK, BLOCK)
        out = out_nat[rows, :].astype(bf16)
        o_ref[here, :] = out
        empty = jnp.zeros_like(out)
        padded[here, :] = jnp.where(
            core == 0, jnp.concatenate([out, empty], axis=1), jnp.concatenate([empty, out], axis=1)
        )


def attend(src, order, raw, cosine, sine):
    head = jax.ShapeDtypeStruct((SEQ, HEAD_DIM), bf16)
    return pl.pallas_call(
        attend_kernel,
        out_shape=(
            head,
            jax.ShapeDtypeStruct((SEQ, 128), bf16),
            head,
            head,
            head,
            jax.ShapeDtypeStruct((SEQ, 1), f32),
        ),
        in_specs=[SMEM, SMEM, VMEM, VMEM, VMEM],
        out_specs=(VMEM,) * 6,
        scratch_shapes=[pltpu.VMEM((SEQ, HEAD_DIM), f32)],
        compiler_params=pltpu.CompilerParams(vmem_limit_bytes=48 * 2**20),
        cost_estimate=pl.CostEstimate(flops=10**9, bytes_accessed=6 * 2**20, transcendentals=2**21),
        name="attention_forward",
    )(src, order, raw, cosine, sine)


def heads_kernel(padded, att_out, mine, other, merged, msem, xsend, xrecv, *sems):
    place = my_place()
    core = place[4]
    pl.semaphore_wait(greet(chip_neighbours(place)), 4)
    half = SEQ // 2
    swap = remote(
        padded.at[pl.ds(pl.multiple_of((1 - core) * half, half), half)], other, xsend, xrecv,
        sibling_of(place),
    )
    swap.start()
    own = pltpu.make_async_copy(padded.at[pl.ds(pl.multiple_of(core * half, half), half)], mine, msem)
    own.start()
    own.wait()
    swap.wait_recv()
    merged[...] = mine[...] + other[...]

    def view(p):
        chip = p[2] * 4 + p[3]
        return att_out.at[
            pl.ds(pl.multiple_of(p[4] * half, half), half), pl.ds(pl.multiple_of(chip * 128, 128), 128)
        ]

    heads = RowGather(place, merged, view, half // 2, *sems)
    heads.start()
    heads.pass_on()
    heads.finish()
    swap.wait_send()


def gather_heads(padded, number):
    return pl.pallas_call(
        heads_kernel,
        out_shape=jax.ShapeDtypeStruct((SEQ, D), bf16),
        in_specs=[ANY],
        out_specs=ANY,
        scratch_shapes=[pltpu.VMEM((SEQ // 2, 128), bf16)] * 3 + [DMA] * 3 + RowGather.scratch,
        compiler_params=pltpu.CompilerParams(collective_id=number, has_side_effects=True),
        name="gather_heads",
    )(padded)


def attend_back_kernel(
    src, order, q_ref, k_ref, v_ref, lse_ref, do_ref, cos_ref, sin_ref, out_ref, do_nat, acc, done
):
    core = lax.axis_index("core")
    for b in range(SEQ // BLOCK):
        rows = pl.ds(pl.multiple_of(src[b] * BLOCK, BLOCK), BLOCK)
        pair = do_ref[rows, :].astype(f32)
        do_nat[pl.ds(b * BLOCK, BLOCK), :] = jnp.where(core == 0, pair[:, :64], pair[:, 64:])
    acc[...] = jnp.zeros_like(acc)
    step = 256
    for i in range(SEQ // step):
        length = (i + 1) * step
        here = pl.ds(i * step, step)
        query, d_out = q_ref[here, :], do_nat[here, :].astype(bf16)
        keys = k_ref[0:length, :]
        scores = dot_last(query, keys) * 0.125
        row = i * step + lax.broadcasted_iota(jnp.int32, (step, length), 0)
        column = lax.broadcasted_iota(jnp.int32, (step, length), 1)
        probs = jnp.where(column <= row, jnp.exp(scores - lse_ref[here, :]), 0.0)
        d_probs = dot_last(d_out, v_ref[0:length, :])
        delta = jnp.sum(probs * d_probs, axis=1, keepdims=True)
        d_scores = (probs * (d_probs - delta)).astype(bf16)
        acc[here, 0:64] = dot(d_scores, keys) * 0.125
        acc[0:length, 64:128] += dot_first(d_scores, query) * 0.125
        acc[0:length, 128:192] += dot_first(probs.astype(bf16), d_out)
    for b in range(SEQ // BLOCK):
        here = pl.ds(b * BLOCK, BLOCK)
        qk = acc[here, 0:128]
        qk = qk * cos_ref[here, :] - swap_halves(qk) * sin_ref[here, :]
        done[here, 0:128] = qk
        done[here, 128:256] = acc[here, 128:256]
    for b in range(SEQ // BLOCK):
        rows = pl.ds(pl.multiple_of(order[b] * BLOCK, BLOCK), BLOCK)
        out_ref[pl.ds(b * BLOCK, BLOCK), :] = done[rows, :].astype(bf16)


def attend_back(src, order, q, k, v, lse, d_out, cosine, sine):
    return pl.pallas_call(
        attend_back_kernel,
        out_shape=jax.ShapeDtypeStruct((SEQ, 256), bf16),
        in_specs=[SMEM, SMEM] + [VMEM] * 7,
        out_specs=VMEM,
        scratch_shapes=[
            pltpu.VMEM((SEQ, HEAD_DIM), f32),
            pltpu.VMEM((SEQ, 256), f32),
            pltpu.VMEM((SEQ, 256), f32),
        ],
        compiler_params=pltpu.CompilerParams(vmem_limit_bytes=56 * 2**20),
        cost_estimate=pl.CostEstimate(flops=3 * 10**9, bytes_accessed=6 * 2**20, transcendentals=2**21),
        name="attention_backward",
    )(src, order, q, k, v, lse, d_out, cosine, sine)


def rotary_tables():
    inverse = 10000.0 ** (-np.arange(32, dtype=np.float64) * 2.0 / HEAD_DIM)
    angles = np.arange(SEQ, dtype=np.float64)[:, None] * inverse[None, :]
    cosine, sine = np.cos(angles), np.sin(angles)
    return (
        np.tile(cosine, (1, 4)).astype(np.float32),
        np.concatenate([-sine, sine, -sine, sine], axis=1).astype(np.float32),
    )


def normalize(inputs, gain_values):
    scale_rows = lax.rsqrt(jnp.mean(inputs * inputs, axis=-1, keepdims=True) + epsilon)
    normed = inputs * scale_rows
    return (scale_rows, normed, (normed * gain_values.astype(f32)).astype(bf16))


def norm_backward(grad_in, normed, scale_rows, gain_values):
    grad_normed = grad_in * gain_values.astype(f32)
    inner = jnp.mean(grad_normed * normed, axis=-1, keepdims=True)
    return (scale_rows * (grad_normed - normed * inner), jnp.sum(grad_in * normed, axis=0))


def halves(value):
    high = lax.reduce_precision(value, 8, 7)
    return high.astype(bf16), (value - high).astype(bf16)


def local(
    tokens,
    cotangent,
    block_order,
    routes,
    norm_one,
    w_query,
    w_key,
    w_value,
    w_out,
    norm_two,
    w_router,
    expert_in,
    expert_out,
):
    ctx = lax.axis_index(CTX)
    cosine, sine = (jnp.asarray(t) for t in rotary_tables())
    order = jnp.stack([block_order, 2 * N_CTX - 1 - block_order], axis=1).reshape(-1)
    spots = jnp.arange(2 * N_CTX, dtype=jnp.int32)
    src = jnp.sum(jnp.where(order[None, :] == spots[:, None], spots[None, :], 0), axis=1)

    small = jnp.concatenate(
        [w_router, norm_one[:, None], norm_two[:, None], jnp.zeros((8, 30), bf16)], axis=1
    )
    tokens_all, packed_all, out_all, members = entry(
        tokens, w_query, w_key, w_value, small, w_out, routes, 0
    )
    down_packed = expert_out.reshape(2, 8, 64, ROWS).swapaxes(1, 2).reshape(2, 64, D)
    expert_all = lax.all_gather(jnp.concatenate([expert_in, down_packed], axis=1), DP, axis=0)
    low = packed_all[:, :, 8:, :].reshape(D, 128)
    weight = jnp.concatenate(
        [packed_all[:, :, :8, :].reshape(D, 128), low[:, :64], jnp.zeros((D, 64), bf16)], axis=1
    )
    router_weight, gain_one, gain_two = low[:, 64:96], low[:, 96], low[:, 97]
    out_weight = out_all.reshape(D, D)
    head_weight = lax.dynamic_slice_in_dim(out_weight, ctx * HEAD_DIM, HEAD_DIM, axis=0)

    tokens_float = tokens.astype(f32)
    scale_one, normed_one, _ = normalize(tokens_float, gain_one)
    _, _, hidden_one = normalize(tokens_all.reshape(SEQ, D).astype(f32), gain_one)
    raw = dot(hidden_one, weight)
    attended, padded, query, key, value, lse = attend(src, order, raw, cosine, sine)
    attended_all = gather_heads(padded, 1)

    router_wide = jnp.pad(router_weight, ((0, 0), (64, 32)))
    (
        out_sum,
        residual,
        d_residual,
        d_branch,
        d_logits,
        hidden_two,
        grad_gain_two,
        grad_experts,
        d_heads,
    ) = experts(
        tokens_all,
        attended_all,
        out_weight,
        members,
        router_wide,
        gain_two.astype(f32)[None, :],
        cotangent,
        expert_all,
        3,
    )
    output = residual + out_sum
    grad_experts = lax.psum_scatter(grad_experts, DP, scatter_dimension=0).astype(f32)
    grad_in = grad_experts[:, :ROWS]
    grad_down = grad_experts[:, ROWS:].reshape(2, 64, 8, ROWS).swapaxes(1, 2).reshape(2, FF, ROWS)

    d_raw = attend_back(src, order, query, key, value, lse, d_heads.reshape(SEQ, 128), cosine, sine)
    side = jnp.stack([1.0 / gain_one.astype(f32), grad_gain_two[0]], axis=1)
    side = jnp.pad(side, ((0, 0), (0, 126)))
    blocks = (8, 2, ROWS, D)
    d_hidden_one, a, b = last(
        d_raw,
        weight,
        side,
        d_branch,
        d_logits,
        hidden_one,
        attended_all.reshape(blocks),
        hidden_two,
        5,
    )
    d_norm_one, _ = norm_backward(d_hidden_one, normed_one, scale_one, gain_one)
    input_grad = d_residual + d_norm_one

    side_by_side = lambda v: jnp.moveaxis(v, 0, 1).reshape(8, -1)
    pairs = a.reshape(KV_HEADS, 2, 8, 256).sum(axis=1)
    common = jnp.sum(a[:, :, 192:], axis=0)
    return (
        output,
        input_grad,
        common[:, 0],
        side_by_side(a[:, :, 0:64]),
        side_by_side(pairs[:, :, 64:128]),
        side_by_side(pairs[:, :, 128:192]),
        side_by_side(b),
        common[:, 1],
        common[:, 2:34],
        grad_in,
        grad_down,
    )


def solution(mesh):
    split = Mesh(mesh.devices.reshape(2, 4, 2, 4, 2), AXES)
    rows = P(AXES, None)
    line = P(AXES)
    return jax.shard_map(
        local,
        mesh=split,
        in_specs=(
            rows,
            rows,
            P(),
            rows,
            line,
            rows,
            rows,
            rows,
            rows,
            line,
            rows,
            P(CTX, DP, None),
            P(CTX, None, DP),
        ),
        out_specs=(
            rows,
            rows,
            line,
            rows,
            rows,
            rows,
            rows,
            line,
            rows,
            P(CTX, DP, None),
            P(CTX, None, DP),
        ),
        check_vma=False,
    )
```

```python
import functools
import math

import jax
import jax.numpy as jnp
import numpy as np
from jax import lax
from jax.experimental import pallas as pl
from jax.experimental.pallas import tpu as pltpu
from jax.sharding import Mesh
from jax.sharding import PartitionSpec as P

D = 1024
HEADS = 16
KV_HEADS = 8
HEAD_DIM = 64
EXPERTS = 32
FF = 512
TOP = 8
MOST = 48
ROWS = 128
SEQ = 2048
BLOCK = 64
AXES = ("ylo", "z", "yhi", "x", "core")
DP = ("ylo", "z")
CTX = ("yhi", "x", "core")
N_DP = 8
N_CTX = 16
EXTRA = 128
MESH_ID = pl.DeviceIdType.MESH
ANY = pl.BlockSpec(memory_space=pl.ANY)
VMEM = pl.BlockSpec(memory_space=pltpu.VMEM)
SMEM = pl.BlockSpec(memory_space=pltpu.SMEM)
DMA = pltpu.SemaphoreType.DMA
bf16 = jnp.bfloat16
f32 = jnp.float32
epsilon = 1e-06


def dot(a, b):
    return jnp.dot(a, b, preferred_element_type=f32)


def dot_last(a, b):
    return lax.dot_general(a, b, (((1,), (1,)), ((), ())), preferred_element_type=f32)


def dot_first(a, b):
    return lax.dot_general(a, b, (((0,), (0,)), ((), ())), preferred_element_type=f32)


def my_place():
    return tuple(lax.axis_index(a) for a in AXES)


def device_at(dp, ctx):
    return (
        lax.div(dp, 4),
        lax.rem(dp, 4),
        lax.div(ctx, 8),
        lax.rem(lax.div(ctx, 2), 4),
        lax.rem(ctx, 2),
    )


def beside(place, dy, dx):
    ylo, z, yhi, x, core = place
    return (ylo, z, lax.rem(yhi + dy, 2), lax.rem(x + dx, 4), core)


def ctx_of(place):
    return place[2] * 8 + place[3] * 2 + place[4]


def dp_of(place):
    return place[0] * 4 + place[1]


def sibling_of(place):
    return place[:4] + (1 - place[4],)


def remote(src, dst, send, recv, device):
    return pltpu.make_async_remote_copy(
        src_ref=src, dst_ref=dst, send_sem=send, recv_sem=recv, device_id=device, device_id_type=MESH_ID
    )


def greet(devices):
    barrier = pltpu.get_barrier_semaphore()
    for device in devices:
        pl.semaphore_signal(barrier, inc=1, device_id=device, device_id_type=MESH_ID)
    return barrier


class RowGather:
    scratch = [DMA, DMA((9,)), DMA((9,)), DMA((10,)), DMA((10,))]
    links = [(1, 0), (0, 1), (0, 3), (0, 1), (0, 3), (0, 1), (0, 3), (0, 1), (0, 3)]
    held = [(0, 0), (0, 0), (0, 0), (1, 0), (1, 0), (0, 3), (0, 1), (1, 3), (1, 1)]
    parts = [None, None, None, None, None, 0, 1, 0, 1]
    after = {0: (3, 4), 1: (5,), 2: (6,), 3: (7,), 4: (8,)}

    def __init__(self, place, x_ref, view, half, local, send, recv, fsend, frecv):
        sibling = sibling_of(place)

        def piece(dy, dx, part):
            ref = view(beside(place, dy, dx))
            return ref if part is None else ref.at[pl.ds(part * half, half)]

        self.own = pltpu.make_async_copy(x_ref, view(place), local)
        self.out, self.landed, self.passed = [], [], []
        for n, ((ly, lx), (hy, hx), part) in enumerate(zip(self.links, self.held, self.parts)):
            source = x_ref if n < 3 else piece(hy, hx, part)
            self.out.append(
                remote(source, piece(hy, hx, part), send.at[n], recv.at[n], beside(place, ly, lx))
            )
            here = piece((hy + ly) % 2, (hx + 4 - lx) % 4, part)
            self.landed.append(remote(here, here, send.at[n], recv.at[n], beside(place, ly, lx)))
            self.passed.append(remote(here, here, fsend.at[n], frecv.at[n], sibling))
        self.passed.append(remote(x_ref, view(place), fsend.at[9], frecv.at[9], sibling))
        self.back = []
        for n in range(9):
            (ly, lx), (hy, hx), part = self.links[n], self.held[n], self.parts[n]
            ref = view(sibling_of(beside(place, (hy + ly) % 2, (hx + 4 - lx) % 4)))
            ref = ref if part is None else ref.at[pl.ds(part * half, half)]
            self.back.append(remote(ref, ref, fsend.at[n], frecv.at[n], sibling))
        ref = view(sibling)
        self.back.append(remote(ref, ref, fsend.at[9], frecv.at[9], sibling))

    def start(self):
        for n in range(3):
            self.out[n].start()
        self.passed[9].start()
        self.own.start()

    def step(self, n):
        self.landed[n].wait_recv()
        for m in self.after.get(n, ()):
            self.out[m].start()
        self.passed[n].start()

    def pass_on(self):
        for n in range(9):
            self.step(n)

    def finish(self):
        self.own.wait()
        for n in range(10):
            self.back[n].wait_recv()
        for copy in self.out + self.passed:
            copy.wait_send()


def around(place, dz):
    ylo, z, yhi, x, core = place
    return (ylo, lax.rem(z + dz, 4), yhi, x, core)


class PlaneRing:
    scratch = [DMA, DMA((4,)), DMA((4,))]

    def __init__(self, place, block, out, local, send, recv):
        z, up, down = place[1], around(place, 1), around(place, 3)
        below = out.at[down[1], pl.ds(0, 1)]
        above = out.at[up[1], pl.ds(1, 1)]
        self.own = pltpu.make_async_copy(block, out.at[z], local)
        self.out = [
            remote(block, out.at[z], send.at[0], recv.at[0], up),
            remote(block, out.at[z], send.at[1], recv.at[1], down),
            remote(below, below, send.at[2], recv.at[2], up),
            remote(above, above, send.at[3], recv.at[3], down),
        ]

    def start(self):
        self.out[0].start()
        self.out[1].start()
        self.own.start()

    def step(self, n):
        self.out[n].wait_recv()
        self.out[2 + n].start()

    def finish(self):
        self.own.wait()
        self.out[2].wait_recv()
        self.out[3].wait_recv()
        for copy in self.out:
            copy.wait_send()


def chip_neighbours(place):
    return [beside(place, 1, 0), beside(place, 0, 1), beside(place, 0, 3), sibling_of(place)]


SPREAD = [(1, 2), (0, 2), (1, 1), (1, 3), (0, 1), (0, 3), (1, 0), (0, 0)]


class RowScatter:
    @staticmethod
    def scratch(rows, width):
        return [
            pltpu.VMEM((8, rows, width), bf16),
            pltpu.VMEM((8, rows, width), bf16),
            pltpu.VMEM((4, rows // 2, width), bf16),
            pltpu.VMEM((4, rows, width), bf16),
            pltpu.VMEM((rows, width), bf16),
            DMA((8,)),
            DMA((8,)),
            DMA((8,)),
            DMA((9,)),
            DMA((9,)),
        ]

    def __init__(self, place, part, own, other, halves, wholes, last, own_sem, fsend, frecv, send, recv):
        self.own, self.other, self.halves, self.wholes, self.last = own, other, halves, wholes, last
        core = place[4]
        half = own.shape[1] // 2
        self.half = half
        self.mine, self.cross = [], []
        for n, (dy, dx) in enumerate(SPREAD):
            chip = lax.div(ctx_of(beside(place, dy, dx)), 2)
            self.mine.append(pltpu.make_async_copy(part(chip, core), own.at[n], own_sem.at[n]))
            self.cross.append(
                remote(part(chip, 1 - core), other.at[n], fsend.at[n], frecv.at[n], sibling_of(place))
            )
        right, left = beside(place, 0, 1), beside(place, 0, 3)
        self.out = []
        for n, (source, target, device) in enumerate(
            [
                (own.at[0, pl.ds(0, half)], halves.at[0], right),
                (own.at[0, pl.ds(half, half)], halves.at[1], left),
                (own.at[1, pl.ds(0, half)], halves.at[2], right),
                (own.at[1, pl.ds(half, half)], halves.at[3], left),
                (own.at[2], wholes.at[0], right),
                (own.at[3], wholes.at[1], left),
                (own.at[4], wholes.at[2], right),
                (own.at[5], wholes.at[3], left),
                (own.at[6], last, beside(place, 1, 0)),
            ]
        ):
            self.out.append(remote(source, target, send.at[n], recv.at[n], device))

    def start(self, n):
        self.cross[n].start()
        self.mine[n].start()

    def release(self):
        for n in range(8):
            self.cross[n].wait_send()

    def join(self, n):
        self.mine[n].wait()
        self.cross[n].wait_recv()
        return self.own[n].astype(f32) + self.other[n].astype(f32)

    def step(self, n):
        if n < 2:
            self.own[n] = self.join(n).astype(bf16)
            self.out[2 * n].start()
            self.out[2 * n + 1].start()
        elif n < 6:
            total = self.join(n)
            half = self.half
            side = pl.ds(0 if n % 2 == 0 else half, half)
            self.out[n - 2].wait_recv()
            self.own[n] = total.astype(bf16)
            first = total[:half] if n % 2 == 0 else total[half:]
            self.own[n, side] = (first + self.halves[n - 2].astype(f32)).astype(bf16)
            self.out[n + 2].start()
        elif n == 6:
            total = self.join(6)
            for m in (0, 1):
                self.out[4 + m].wait_recv()
                total = total + self.wholes[m].astype(f32)
            self.own[6] = total.astype(bf16)
            self.out[8].start()
        else:
            total = self.join(7)
            for m in (2, 3):
                self.out[4 + m].wait_recv()
                total = total + self.wholes[m].astype(f32)
            self.out[8].wait_recv()
            return total + self.last[...].astype(f32)

    def finish(self):
        for copy in self.out:
            copy.wait_send()


def entry_kernel(
    x_ref, q_ref, k_ref, v_ref, small_ref, o_ref, routes_ref, ein_ref, eout_ref,
    x_out, w_out, o_out, m_out, ein_own, eout_own, ein_y, eout_y,
    w_pack, o_pad, o_other, o_mid, m_pack, *sems,
):
    row_sems, o_sems, m_sems, rest = sems[:5], sems[5:10], sems[10:15], sems[15:]
    wlocal, wsend, wrecv, psend, precv, xsend, xrecv, osend, orecv, ysend, yrecv = rest[:11]
    place = my_place()
    core = place[4]
    dp, ctx = dp_of(place), ctx_of(place)
    barrier = greet(
        [device_at(dp, lax.rem(ctx + k, N_CTX)) for k in range(1, N_CTX)]
        + [device_at(lax.rem(dp + k, N_DP), ctx) for k in range(1, N_DP)]
    )
    pl.semaphore_wait(barrier, 22)
    rows = RowGather(place, x_ref, lambda p: x_out.at[ctx_of(p)], x_ref.shape[0] // 2, *row_sems)
    rows.start()
    rings = [
        PlaneRing(place, ein_ref, ein_own, *rest[11:14]),
        PlaneRing(place, eout_ref, eout_own, *rest[14:17]),
    ]
    for ring in rings:
        ring.start()
    beyond = (1 - place[0],) + place[1:]
    across = [
        remote(ein_ref, ein_y, ysend.at[0], yrecv.at[0], beyond),
        remote(eout_ref, eout_y, ysend.at[1], yrecv.at[1], beyond),
    ]

    out = o_ref[...].astype(f32)
    empty = jnp.zeros_like(out)
    out = jnp.where(core == 0, jnp.concatenate([out, empty], 0), jnp.concatenate([empty, out], 0))
    for s in range(2):
        o_pad[s] = out[:, s * 512 : (s + 1) * 512].astype(bf16)
    swap = remote(o_pad.at[1 - core], o_other, xsend, xrecv, sibling_of(place))
    swap.start()
    query, key, value = (r[...].astype(f32) for r in (q_ref, k_ref, v_ref))
    small = small_ref[...].astype(f32)
    for h in range(HEADS):
        at, pair = slice(h * 64, h * 64 + 64), slice(h // 2 * 64, h // 2 * 64 + 64)
        top = jnp.concatenate([query[:, at], key[:, pair]], axis=1)
        low = jnp.concatenate([value[:, pair], small], axis=1)
        w_pack[h] = jnp.concatenate([top, low], axis=0).astype(bf16)
    first, second, third = [], [], []
    for k in range(1, N_CTX):
        to = lax.rem(ctx + k, N_CTX)
        first.append(
            remote(w_pack.at[to], w_out.at[dp, ctx], wsend.at[k], wrecv.at[k], device_at(dp, to))
        )
    for k in range(1, N_DP):
        device = device_at(lax.rem(dp + k, N_DP), ctx)
        third.append(remote(o_mid.at[dp], o_mid.at[dp], osend.at[k], orecv.at[k], device))
        second.append(remote(w_out.at[dp], w_out.at[dp], psend.at[k], precv.at[k], device))
    for copy in first:
        copy.start()
    own = pltpu.make_async_copy(w_pack.at[ctx], w_out.at[dp, ctx], wlocal)
    own.start()
    swap.wait_recv()
    o_mid[dp] = o_pad[core] + o_other[...]
    for copy in third:
        copy.start()
    routes = routes_ref[...]
    lane = lax.broadcasted_iota(jnp.int32, (ROWS, EXTRA), 1) - 64
    member = jnp.zeros((ROWS, EXTRA), f32)
    for k in range(TOP):
        member = jnp.where(lane == routes[:, k : k + 1], 1.0, member)
    m_pack[...] = member.astype(bf16)
    members = RowGather(place, m_pack, lambda p: m_out.at[ctx_of(p)], ROWS // 2, *m_sems)
    members.start()
    own.wait()
    for copy in first:
        copy.wait_recv()
    for copy in second:
        copy.start()
    for copy in third:
        copy.wait_recv()

    def o_view(p):
        return o_out.at[:, p[2] * 4 + p[3], :, pl.ds(pl.multiple_of(p[4] * 512, 512), 512)]

    outs = RowGather(place, o_mid, o_view, 4, *o_sems)
    outs.start()
    rows.step(0)
    for copy in across:
        copy.start()
    for n in range(1, 5):
        rows.step(n)
    for n in range(9):
        members.step(n)
    for n in range(3):
        outs.step(n)
    for n in range(2):
        for ring in rings:
            ring.step(n)
    for n in range(5, 9):
        rows.step(n)
    for n in range(3, 9):
        outs.step(n)
    rows.finish()
    members.finish()
    outs.finish()
    for ring in rings:
        ring.finish()
    for copy in across:
        copy.wait()
    for copy in second:
        copy.wait_recv()
    swap.wait_send()
    for copy in first + second + third:
        copy.wait_send()


def entry(x, query, key, value, small, out, routes, ein, eout, number):
    return pl.pallas_call(
        entry_kernel,
        out_shape=(
            jax.ShapeDtypeStruct((N_CTX,) + x.shape, bf16),
            jax.ShapeDtypeStruct((N_DP, N_CTX, 16, 128), bf16),
            jax.ShapeDtypeStruct((N_DP, 8, 16, D), bf16),
            jax.ShapeDtypeStruct((N_CTX, ROWS, EXTRA), bf16),
            jax.ShapeDtypeStruct((4,) + ein.shape, bf16),
            jax.ShapeDtypeStruct((4,) + eout.shape, bf16),
            jax.ShapeDtypeStruct(ein.shape, bf16),
            jax.ShapeDtypeStruct(eout.shape, bf16),
        ),
        in_specs=[ANY] + [VMEM] * 6 + [ANY] * 2,
        out_specs=(ANY,) * 8,
        scratch_shapes=[
            pltpu.VMEM((N_CTX, 16, 128), bf16),
            pltpu.VMEM((2, 16, 512), bf16),
            pltpu.VMEM((16, 512), bf16),
            pltpu.VMEM((N_DP, 16, 512), bf16),
            pltpu.VMEM((ROWS, EXTRA), bf16),
        ]
        + RowGather.scratch * 3
        + [DMA, DMA((16,)), DMA((16,)), DMA((8,)), DMA((8,)), DMA, DMA, DMA((8,)), DMA((8,))]
        + [DMA((2,)), DMA((2,))]
        + PlaneRing.scratch * 2,
        compiler_params=pltpu.CompilerParams(
            collective_id=number, has_side_effects=True, vmem_limit_bytes=16 * 2**20
        ),
        name="entry_gather",
    )(x, query, key, value, small, out, routes, ein, eout)


def last_kernel(
    d_raw, weight, side, d_branch, d_logits, hidden_ref, att_ref, hid_ref, one_ref, a_out, w_out,
    hidden, att, hid, parts, w_parts, a_pack, landed, part, w_sum, w_landed, w_mine,
    in_sem, wlocal, wsend, wrecv, psend, precv, plocal, osend, orecv, olocal, xsend, xrecv, *scatters,
):
    place = my_place()
    core = place[4]
    dp, ctx = dp_of(place), ctx_of(place)
    barrier = greet(
        [device_at(dp, lax.rem(ctx + k, N_CTX)) for k in range(1, N_CTX)]
        + [device_at(lax.rem(dp + k, N_DP), ctx) for k in range(1, N_DP)]
    )
    loads = [
        pltpu.make_async_copy(att_ref.at[lax.div(ctx, 2), core], att, in_sem.at[0]),
        pltpu.make_async_copy(hid_ref, hid, in_sem.at[1]),
        pltpu.make_async_copy(hidden_ref, hidden, in_sem.at[2]),
    ]
    for load in loads:
        load.start()

    def back(c, _):
        here = pl.ds(pl.multiple_of(c * ROWS, ROWS), ROWS)
        parts[lax.div(c, 2), lax.rem(c, 2)] = dot_last(d_raw[here, :], weight[...]).astype(bf16)
        return 0

    lax.fori_loop(0, N_CTX, back, 0)
    pl.semaphore_wait(barrier, 22)
    rows = RowScatter(place, lambda chip, c: parts.at[chip, c], *scatters[:10])
    outs = RowScatter(place, lambda chip, c: w_parts.at[chip, c], *scatters[10:])
    for n in range(8):
        rows.start(n)
    for load in loads:
        load.wait()

    def heads(k, _):
        here = pl.ds(pl.multiple_of(k * ROWS, ROWS), ROWS)
        grad = dot_first(hidden[:, here], d_raw[...])
        gain = jnp.sum(grad * weight[here, :].astype(f32), axis=1, keepdims=True)
        lane = lax.broadcasted_iota(jnp.int32, (ROWS, 128), 1)
        extra = side[here, :]
        high = grad[:, 128:] + dot_first(hid[:, here], d_logits[...])
        high = jnp.where(lane == 64, gain * extra[:, 0:1], jnp.where(lane == 65, extra[:, 1:2], high))
        a_pack[k, :, :128] = grad[:, :128].astype(bf16)
        a_pack[k, :, 128:] = high.astype(bf16)
        return 0

    lax.fori_loop(0, N_DP, heads, 0)
    first, second, third = [], [], []
    for k in range(1, N_DP):
        to = lax.rem(dp + k, N_DP)
        first.append(remote(a_pack.at[to], landed.at[k], wsend.at[k], wrecv.at[k], device_at(to, ctx)))
        third.append(
            remote(
                w_sum.at[pl.ds(pl.multiple_of(to * 16, 16), 16)],
                w_landed.at[k],
                osend.at[k],
                orecv.at[k],
                device_at(to, ctx),
            )
        )
    for copy in first:
        copy.start()
    own = pltpu.make_async_copy(a_pack.at[dp], landed.at[0], wlocal)
    own.start()
    rows.step(0)
    rows.step(1)

    def products(k, _):
        here = pl.ds(pl.multiple_of(k * ROWS, ROWS), ROWS)
        total = dot_first(att[:, here], d_branch[...]).astype(bf16)
        to = pl.ds(pl.multiple_of(k * 16, 16), 16)
        for g in range(8):
            for c in range(2):
                w_parts[g, c, to, :] = total[g * 16 : (g + 1) * 16, c * 512 : (c + 1) * 512]
        return 0

    lax.fori_loop(0, N_DP, products, 0)
    for n in range(8):
        outs.start(n)
    for n in range(2, 6):
        rows.step(n)
    outs.step(0)
    outs.step(1)
    own.wait()
    for copy in first:
        copy.wait_recv()
    total = landed[0].astype(f32)
    for k in range(1, N_DP):
        total = total + landed[k].astype(f32)
    part[...] = total.reshape(part.shape)
    for k in range(1, N_CTX):
        to = lax.rem(ctx + k, N_CTX)
        second.append(remote(part.at[to], a_out.at[ctx], psend.at[k], precv.at[k], device_at(dp, to)))
    for copy in second:
        copy.start()
    mine = pltpu.make_async_copy(part.at[ctx], a_out.at[ctx], plocal)
    mine.start()
    rows.step(6)
    for n in range(2, 6):
        outs.step(n)
    one_ref[...] = rows.step(7)
    outs.step(6)
    w_sum[...] = outs.step(7)
    for copy in third:
        copy.start()
    own = pltpu.make_async_copy(w_sum.at[pl.ds(pl.multiple_of(dp * 16, 16), 16)], w_landed.at[0], olocal)
    own.start()
    own.wait()
    for copy in third:
        copy.wait_recv()
    total = w_landed[0]
    for k in range(1, N_DP):
        total = total + w_landed[k]
    w_mine[...] = total.reshape(2, 8, 512)
    swap = remote(w_mine.at[1 - core], w_out.at[core], xsend, xrecv, sibling_of(place))
    swap.start()
    keep = pltpu.make_async_copy(w_mine.at[core], w_out.at[core], in_sem.at[0])
    swap_in = remote(w_mine.at[1 - core], w_out.at[1 - core], xsend, xrecv, sibling_of(place))
    swap_in.wait_recv()
    swap.wait_send()
    keep.start()
    keep.wait()
    mine.wait()
    for copy in second:
        copy.wait_recv()
    rows.release()
    outs.release()
    rows.finish()
    outs.finish()
    for copy in first + second + third:
        copy.wait_send()


def last(d_raw, weight, side, d_branch, d_logits, hidden, att, hid, number):
    v = lambda *shape: pltpu.VMEM(shape, bf16)
    return pl.pallas_call(
        last_kernel,
        out_shape=(
            jax.ShapeDtypeStruct((ROWS, D), f32),
            jax.ShapeDtypeStruct((N_CTX, 8, 256), f32),
            jax.ShapeDtypeStruct((2, 8, 512), f32),
        ),
        in_specs=[VMEM] * 5 + [ANY] * 3,
        out_specs=(VMEM,) * 3,
        scratch_shapes=[
            v(SEQ, D),
            v(ROWS, D),
            v(ROWS, D),
            v(8, 2, ROWS, D),
            v(8, 2, ROWS, 512),
            v(N_DP, ROWS, 256),
            v(N_DP, ROWS, 256),
            pltpu.VMEM((N_CTX, 8, 256), f32),
            pltpu.VMEM((ROWS, 512), f32),
            pltpu.VMEM((N_DP, 16, 512), f32),
            pltpu.VMEM((2, 8, 512), f32),
            DMA((3,)),
            DMA,
            DMA((8,)),
            DMA((8,)),
            DMA((16,)),
            DMA((16,)),
            DMA,
            DMA((8,)),
            DMA((8,)),
            DMA,
            DMA,
            DMA,
        ]
        + RowScatter.scratch(ROWS, D)
        + RowScatter.scratch(ROWS, 512),
        compiler_params=pltpu.CompilerParams(
            collective_id=number, has_side_effects=True, vmem_limit_bytes=48 * 2**20
        ),
        name="last_sums",
    )(d_raw, weight, side, d_branch, d_logits, hidden, att, hid)


def experts_kernel(
    tok_ref, att_ref, wo_ref, m_ref, router_ref, gain_ref, cot_ref, ein_own, ein_far, eout_own, eout_far,
    out_ref, res_ref, d_res_ref, d_branch_ref, d_logits_ref, hid_ref, gain_grad_ref, g_ref, heads_ref,
    pool, members, win, down, wide, picks, facts_all, gates_all, logits_all, gate_slot, dg_slot,
    rows, tops, result, hidden, d_mid, own_rows, d_heads,
    in_sem, tok_sem, hsend, hrecv, *scatters,
):
    body = pl.ds(0, D)
    loads = [
        pltpu.make_async_copy(wo_ref, wide, in_sem.at[0]),
        pltpu.make_async_copy(m_ref, members, in_sem.at[1]),
    ]
    place = my_place()
    core = place[4]
    near, far = pl.ds(place[0] * 4, 4), pl.ds(4 - place[0] * 4, 4)
    loads += [
        pltpu.make_async_copy(ein_own, win.at[near, :, pl.ds(0, ROWS)], in_sem.at[2]),
        pltpu.make_async_copy(ein_far, win.at[far, :, pl.ds(0, ROWS)], in_sem.at[3]),
        pltpu.make_async_copy(eout_own, down.at[near], in_sem.at[4]),
        pltpu.make_async_copy(eout_far, down.at[far], in_sem.at[5]),
    ]
    dp, ctx = dp_of(place), ctx_of(place)
    chip = lax.div(ctx, 2)

    def tokens_of(i):
        return result.at[i // 3, pl.ds(i % 3 * 256, 256)] if i < 6 else tops.at[0, pl.ds((i - 6) * 256, 256)]

    streams = []
    for i in range(8):
        streams.append(
            (
                pltpu.make_async_copy(tok_ref.at[i], tokens_of(i), tok_sem.at[0, i]),
                pltpu.make_async_copy(att_ref.at[i], pool.at[i, :, 0, :, body], tok_sem.at[1, i]),
            )
        )
    loads[0].start()
    for pair in streams[:2]:
        pair[0].start()
        pair[1].start()
    pl.semaphore_wait(greet([device_at(dp, lax.rem(ctx + k, N_CTX)) for k in range(1, N_CTX)]), 15)
    gather = RowGather(
        place,
        cot_ref,
        lambda p: pool.at[p[2] * 4 + p[3], p[4], 1, :, body],
        ROWS // 2,
        *scatters[20:],
    )
    gather.start()
    for pair in streams[2:]:
        pair[0].start()
        pair[1].start()
    for load in loads[1:]:
        load.start()
    line = lax.broadcasted_iota(jnp.int32, (8, EXTRA), 0)
    lane = lax.broadcasted_iota(jnp.int32, (8, EXTRA), 1)
    chosen = jnp.logical_and(line < 2, lane == 64 + 2 * ctx + line)
    chosen = jnp.where(chosen, 1.0, 0.0).astype(bf16)
    back = jnp.logical_and(line < 4, lane == jnp.where(line < 2, 0, 32) + 2 * ctx + lax.rem(line, 2))
    back = jnp.where(back, 1.0, 0.0).astype(bf16)
    before = lax.broadcasted_iota(jnp.int32, (ROWS, ROWS), 0) < lax.broadcasted_iota(
        jnp.int32, (ROWS, ROWS), 1
    )
    before = jnp.where(before, 1.0, 0.0).astype(bf16)
    slots = lax.broadcasted_iota(jnp.int32, (MOST, ROWS), 0).astype(f32)

    def second_norm(token, att):
        residual = token.astype(f32) + dot(att[:, :FF], wide[0]) + dot(att[:, FF:], wide[1])
        scale = lax.rsqrt(jnp.mean(residual * residual, axis=1, keepdims=True) + epsilon)
        normed = residual * scale
        return residual, scale, normed, (normed * gain_ref[...]).astype(bf16)

    def gates_of(logits, inside):
        logits = jnp.where(inside > 0.5, logits, -1e30)
        weights = jnp.exp(logits - jnp.max(logits, axis=1, keepdims=True))
        weights = jnp.where(inside > 0.5, weights, 0.0)
        return weights / jnp.sum(weights, axis=1, keepdims=True)

    loads[0].wait()
    for i in range(8):
        for copy in streams[i]:
            copy.wait()
        att = pool[i, :, 0, :, :D].reshape(2 * ROWS, D)
        token = (
            result[i // 3, i % 3 * 256 : i % 3 * 256 + 256]
            if i < 6
            else tops[0, (i - 6) * 256 : (i - 5) * 256]
        )
        hid = second_norm(token, att)[3]
        pool[i, :, 0, :, :D] = hid.reshape(2, ROWS, D)
        logits_all[i * 256 : (i + 1) * 256] = dot(hid, router_ref[...])
        if i == 2:
            gather.step(0)
    gather.step(1)
    gather.step(2)
    loads[1].wait()
    for half in range(2):
        inside = members[8 * half : 8 * half + 8].reshape(8 * ROWS, EXTRA)
        gates = gates_of(logits_all[1024 * half : 1024 * (half + 1)], inside.astype(f32))
        high = gates.astype(bf16)
        rest = (gates - high.astype(f32)).astype(bf16)
        facts = dot_last(chosen, inside)
        lines = dot_last(chosen, high) + dot_last(chosen, rest)
        for c in range(8):
            facts_all[8 * half + c] = facts[:, c * ROWS : (c + 1) * ROWS]
            gates_all[8 * half + c] = lines[:, c * ROWS : (c + 1) * ROWS]

    def pick(i, _):
        for k in range(4):
            c = i * 4 + k
            facts, lines = facts_all[c], gates_all[c]
            order = dot(facts.astype(bf16), before)
            here = pl.ds(pl.multiple_of(c * MOST, MOST), MOST)
            both = []
            for e in range(2):
                member = facts[e : e + 1]
                onehot = jnp.where(jnp.logical_and(order[e : e + 1] == slots, member > 0.5), 1.0, 0.0)
                gate_slot[e, here] = jnp.sum(onehot * lines[e : e + 1], axis=1, keepdims=True)
                both.append(onehot.astype(bf16))
            both = jnp.concatenate(both, axis=0)
            picks[c] = both
            taken = dot(both, pool[i * 2 + k // 2, k % 2, 0, :, :D]).astype(bf16)
            rows[0, here] = taken[:MOST]
            rows[1, here] = taken[MOST:]
        return 0

    lax.fori_loop(0, 4, pick, 0)
    for n in range(3, 5):
        gather.step(n)
    for load in loads[2:]:
        load.wait()
    for e in range(2):
        for k in range(N_DP):
            wide[e, :, k * ROWS : (k + 1) * ROWS] = down[k, e]
    tile = 256

    def pick_tops(i, _):
        for k in range(4):
            c = i * 4 + k
            here = pl.ds(pl.multiple_of(c * MOST, MOST), MOST)
            taken = dot(picks[c], pool[i * 2 + k // 2, k % 2, 1, :, :D]).astype(bf16)
            tops[0, here] = taken[:MOST]
            tops[1, here] = taken[MOST:]
        return 0

    def forth(e, t):
        here = pl.ds(t * tile, tile)
        both = dot(rows[e, here], win[:, e, :ROWS].reshape(D, 2 * FF))
        gate_part, up_part = both[:, :FF], both[:, FF:]
        sigmoid = 1.0 / (1.0 + jnp.exp(-gate_part))
        silu = gate_part * sigmoid
        middle = (silu * up_part).astype(bf16)
        hidden[e, here] = middle
        d_mid[e, here, :FF] = (up_part * (sigmoid * (1.0 + gate_part * (1.0 - sigmoid)))).astype(bf16)
        d_mid[e, here, FF:] = silu.astype(bf16)
        result[e, here] = dot(middle, wide[e]).astype(bf16)

    def backward(e, t):
        here = pl.ds(t * tile, tile)
        top = tops[e, here].astype(f32)
        dg_slot[e, here] = jnp.sum(top * result[e, here].astype(f32), axis=1, keepdims=True)
        d_result = (top * gate_slot[e, here]).astype(bf16)
        tops[e, here] = d_result
        d_middle = dot_last(d_result, wide[e])
        d_mid[e, here, :FF] = (d_middle * d_mid[e, here, :FF].astype(f32)).astype(bf16)
        d_mid[e, here, FF:] = (d_middle * d_mid[e, here, FF:].astype(f32)).astype(bf16)
        weight = win[:, e, :ROWS].reshape(D, 2 * FF)
        result[e, here] = dot_last(d_mid[e, here], weight).astype(bf16)

    def combine_out(i, _):
        for k in range(4):
            c = i * 4 + k
            here = pl.ds(pl.multiple_of(c * MOST, MOST), MOST)
            found = [(result[e, here].astype(f32) * gate_slot[e, here]).astype(bf16) for e in range(2)]
            found = jnp.concatenate(found, axis=0)
            pool[i * 2 + k // 2, k % 2, 0, :, :D] = dot_first(picks[c], found).astype(bf16)
        return 0

    def combine_back(i, _):
        for k in range(4):
            c = i * 4 + k
            here = pl.ds(pl.multiple_of(c * MOST, MOST), MOST)
            both = picks[c]
            found = jnp.concatenate([result[0, here], result[1, here]], axis=0)
            pool[i * 2 + k // 2, k % 2, 1, :, :D] = dot_first(both, found).astype(bf16)
            lines = [
                jnp.sum(
                    both[e * MOST : (e + 1) * MOST].astype(f32) * dg_slot[e, here], axis=0, keepdims=True
                )
                for e in range(2)
            ]
            high = [v.astype(bf16).astype(f32) for v in lines]
            rest = [v - h for v, h in zip(lines, high)]
            lines = jnp.concatenate(high + rest + [jnp.zeros((4, ROWS), f32)], axis=0).astype(bf16)
            pool[i * 2 + k // 2, k % 2, 1, :, D:] = dot_first(lines, back).astype(bf16)
        return 0

    for e in range(2):
        for t in range(3):
            forth(e, t)
            if e == 0 and t < 2:
                gather.step(5 + 2 * t)
                gather.step(6 + 2 * t)
    lax.fori_loop(0, 4, combine_out, 0)
    first = RowScatter(place, lambda h, c: pool.at[h, c, 0, :, body], *scatters[:10])
    second = RowScatter(place, lambda h, c: pool.at[h, c, 1], *scatters[10:20])
    for n in range(8):
        first.start(n)
    gather.finish()
    first.step(0)
    first.step(1)
    lax.fori_loop(0, 4, pick_tops, 0)
    plan = [(), (), (2, 3), (4, 5), (), ()]
    for e in range(2):
        for t in range(3):
            backward(e, t)
            for n in plan[3 * e + t]:
                first.step(n)
    lax.fori_loop(0, 4, combine_back, 0)
    for n in range(8):
        second.start(n)
    first.step(6)
    second.step(0)
    second.step(1)
    reload = [
        pltpu.make_async_copy(wo_ref, wide, in_sem.at[0]),
        pltpu.make_async_copy(cot_ref, own_rows.at[0], in_sem.at[1]),
        pltpu.make_async_copy(tok_ref.at[chip, pl.ds(core * ROWS, ROWS)], own_rows.at[1], tok_sem.at[0, 0]),
        pltpu.make_async_copy(att_ref.at[chip, core], own_rows.at[2], tok_sem.at[0, 1]),
    ]

    def weights(e, k):
        here = pl.ds(k * 256, 256)
        total = dot_first(rows[e, :, here], d_mid[e]).astype(bf16)
        win[2 * k, e, :ROWS] = total[:ROWS]
        win[2 * k + 1, e, :ROWS] = total[ROWS:]
        total = dot_first(hidden[e], tops[e, :, here]).astype(bf16)
        for q in range(8):
            win[2 * k, e, ROWS:, q * ROWS : (q + 1) * ROWS] = total[q * 64 : (q + 1) * 64, :ROWS]
            win[2 * k + 1, e, ROWS:, q * ROWS : (q + 1) * ROWS] = total[q * 64 : (q + 1) * 64, ROWS:]

    for copy in reload:
        copy.start()
    plan = [(), (), (), (), (2, 3), (), (4, 5), ()]
    for e in range(2):
        for k in range(4):
            weights(e, k)
            for n in plan[4 * e + k]:
                second.step(n)
    save = pltpu.make_async_copy(win, g_ref, in_sem.at[2])
    save.start()
    for copy in reload:
        copy.wait()
    residual, scale, normed, hid = second_norm(own_rows[1], own_rows[2])
    res_ref[...] = residual
    hid_ref[...] = hid
    gates = gates_of(dot(hid, router_ref[...]), members[ctx].astype(f32))
    second.step(6)
    out_ref[...] = first.step(7)
    total = second.step(7)
    d_gates = pltpu.roll(total[:, D:], 64, 1) + pltpu.roll(total[:, D:], 32, 1)
    d_picked = gates * (d_gates - jnp.sum(gates * d_gates, axis=1, keepdims=True))
    d_logits = d_picked.astype(bf16)
    d_logits_ref[...] = pltpu.roll(d_picked, 2, 1).astype(bf16)
    d_hid = total[:, :D] + dot_last(d_logits, router_ref[...])
    gain_grad_ref[...] = jnp.sum(d_hid * normed, axis=0, keepdims=True)
    d_normed = d_hid * gain_ref[...]
    inner = jnp.mean(d_normed * normed, axis=1, keepdims=True)
    d_res = own_rows[0].astype(f32) + scale * (d_normed - normed * inner)
    d_res_ref[...] = d_res
    d_branch = d_res.astype(bf16)
    d_branch_ref[...] = d_branch
    for s in range(2):
        d_att = dot_last(d_branch, wide[s]).astype(bf16)
        for g in range(4):
            d_heads[4 * s + g] = d_att[:, g * 128 : (g + 1) * 128]
    copies = []
    for k in range(1, N_CTX):
        to = lax.rem(ctx + k, N_CTX)
        copies.append(
            remote(
                d_heads.at[lax.div(to, 2)], heads_ref.at[ctx], hsend.at[k], hrecv.at[k], device_at(dp, to)
            )
        )
    for copy in copies:
        copy.start()
    own = pltpu.make_async_copy(d_heads.at[lax.div(ctx, 2)], heads_ref.at[ctx], in_sem.at[0])
    own.start()
    save.wait()
    own.wait()
    for copy in copies:
        copy.wait_recv()
    for copy in copies:
        copy.wait_send()
    first.release()
    second.release()
    first.finish()
    second.finish()


def experts(tok, att, wo, members, router, gain, cot, weights, number):
    shape = (N_DP, 2, ROWS + 64, D)
    slots = N_CTX * MOST
    v = lambda *shape: pltpu.VMEM(shape, bf16)
    column = pltpu.VMEM((2, slots, 1), f32)
    blocks = (8, 2, ROWS, D)
    return pl.pallas_call(
        experts_kernel,
        out_shape=(
            jax.ShapeDtypeStruct((ROWS, D), f32),
            jax.ShapeDtypeStruct((ROWS, D), f32),
            jax.ShapeDtypeStruct((ROWS, D), f32),
            jax.ShapeDtypeStruct((ROWS, D), bf16),
            jax.ShapeDtypeStruct((ROWS, EXTRA), bf16),
            jax.ShapeDtypeStruct((ROWS, D), bf16),
            jax.ShapeDtypeStruct((1, D), f32),
            jax.ShapeDtypeStruct(shape, bf16),
            jax.ShapeDtypeStruct((N_CTX, ROWS, 128), bf16),
        ),
        in_specs=[ANY] * 4 + [VMEM] * 2 + [ANY] * 5,
        out_specs=(VMEM,) * 7 + (ANY,) * 2,
        scratch_shapes=[
            v(8, 2, 2, ROWS, D + EXTRA),
            v(N_CTX, ROWS, EXTRA),
            v(*shape),
            v(N_DP, 2, FF, ROWS),
            v(2, FF, D),
            v(N_CTX, 2 * MOST, ROWS),
            pltpu.VMEM((N_CTX, 8, ROWS), f32),
            pltpu.VMEM((N_CTX, 8, ROWS), f32),
            pltpu.VMEM((SEQ, EXTRA), f32),
            column,
            column,
            v(2, slots, D),
            v(2, slots, D),
            v(2, slots, D),
            v(2, slots, FF),
            v(2, slots, 2 * FF),
            v(3, ROWS, D),
            v(8, ROWS, 128),
            DMA((6,)),
            DMA((2, 8)),
            DMA((16,)),
            DMA((16,)),
        ]
        + RowScatter.scratch(ROWS, D)
        + RowScatter.scratch(ROWS, D + EXTRA)
        + RowGather.scratch,
        compiler_params=pltpu.CompilerParams(
            collective_id=number, has_side_effects=True, vmem_limit_bytes=61 * 2**20
        ),
        cost_estimate=pl.CostEstimate(flops=15 * 10**9, bytes_accessed=30 * 2**20, transcendentals=2**20),
        name="experts_both_ways",
    )(tok.reshape(8, 2 * ROWS, D), att.reshape(blocks), wo.reshape(2, FF, D), members, router, gain, cot, *weights)


def swap_halves(u):
    lane = lax.broadcasted_iota(jnp.int32, u.shape, 1)
    return jnp.where(lax.rem(lane, 64) < 32, pltpu.roll(u, 96, 1), pltpu.roll(u, 32, 1))


def attend_kernel(
    src, order, raw_ref, cos_ref, sin_ref, o_ref, padded, q_ref, k_ref, v_ref, lse_ref, out_nat
):
    core = lax.axis_index("core")
    for b in range(SEQ // BLOCK):
        rows = pl.ds(pl.multiple_of(src[b] * BLOCK, BLOCK), BLOCK)
        here = pl.ds(b * BLOCK, BLOCK)
        qk = raw_ref[rows, 0:128]
        qk = qk * cos_ref[here, :] + swap_halves(qk) * sin_ref[here, :]
        q_ref[here, :] = (qk[:, 0:64]).astype(bf16)
        k_ref[here, :] = (qk[:, 64:128]).astype(bf16)
        v_ref[here, :] = raw_ref[rows, 128:192].astype(bf16)
    step = 256
    for i in range(SEQ // step):
        length = (i + 1) * step
        here = pl.ds(i * step, step)
        scores = dot_last(q_ref[here, :], k_ref[0:length, :]) * 0.125
        row = i * step + lax.broadcasted_iota(jnp.int32, (step, length), 0)
        column = lax.broadcasted_iota(jnp.int32, (step, length), 1)
        scores = jnp.where(column <= row, scores, -1e30)
        top = jnp.max(scores, axis=1, keepdims=True)
        weights = jnp.exp(scores - top)
        total = jnp.sum(weights, axis=1, keepdims=True)
        lse_ref[here, :] = top + jnp.log(total)
        probs = (weights * (1.0 / total)).astype(bf16)
        out_nat[here, :] = dot(probs, v_ref[0:length, :])
    for b in range(SEQ // BLOCK):
        rows = pl.ds(pl.multiple_of(order[b] * BLOCK, BLOCK), BLOCK)
        here = pl.ds(b * BLOCK, BLOCK)
        out = out_nat[rows, :].astype(bf16)
        o_ref[here, :] = out
        empty = jnp.zeros_like(out)
        padded[here, :] = jnp.where(
            core == 0, jnp.concatenate([out, empty], axis=1), jnp.concatenate([empty, out], axis=1)
        )


def attend(src, order, raw, cosine, sine):
    head = jax.ShapeDtypeStruct((SEQ, HEAD_DIM), bf16)
    return pl.pallas_call(
        attend_kernel,
        out_shape=(
            head,
            jax.ShapeDtypeStruct((SEQ, 128), bf16),
            head,
            head,
            head,
            jax.ShapeDtypeStruct((SEQ, 1), f32),
        ),
        in_specs=[SMEM, SMEM, VMEM, VMEM, VMEM],
        out_specs=(VMEM,) * 6,
        scratch_shapes=[pltpu.VMEM((SEQ, HEAD_DIM), f32)],
        compiler_params=pltpu.CompilerParams(vmem_limit_bytes=48 * 2**20),
        cost_estimate=pl.CostEstimate(flops=10**9, bytes_accessed=6 * 2**20, transcendentals=2**21),
        name="attention_forward",
    )(src, order, raw, cosine, sine)


def heads_kernel(
    padded, ein_ref, eout_ref, att_out, ein_out, eout_out, mine, other, merged, msem, xsend, xrecv, *sems
):
    place = my_place()
    core = place[4]
    pl.semaphore_wait(greet(chip_neighbours(place) + [around(place, 1), around(place, 3)]), 6)
    half = SEQ // 2
    swap = remote(
        padded.at[pl.ds(pl.multiple_of((1 - core) * half, half), half)], other, xsend, xrecv,
        sibling_of(place),
    )
    swap.start()
    own = pltpu.make_async_copy(padded.at[pl.ds(pl.multiple_of(core * half, half), half)], mine, msem)
    own.start()
    own.wait()
    swap.wait_recv()
    merged[...] = mine[...] + other[...]

    def view(p):
        chip = p[2] * 4 + p[3]
        return att_out.at[
            pl.ds(pl.multiple_of(p[4] * half, half), half), pl.ds(pl.multiple_of(chip * 128, 128), 128)
        ]

    heads = RowGather(place, merged, view, half // 2, *sems[:5])
    heads.start()
    rings = [
        PlaneRing(place, ein_ref, ein_out, *sems[5:8]),
        PlaneRing(place, eout_ref, eout_out, *sems[8:11]),
    ]
    for ring in rings:
        ring.start()
    for n in range(5):
        heads.step(n)
    for n in range(2):
        for ring in rings:
            ring.step(n)
    for n in range(5, 9):
        heads.step(n)
    heads.finish()
    for ring in rings:
        ring.finish()
    swap.wait_send()


def gather_heads(padded, ein, eout, number):
    return pl.pallas_call(
        heads_kernel,
        out_shape=(
            jax.ShapeDtypeStruct((SEQ, D), bf16),
            jax.ShapeDtypeStruct((4,) + ein.shape, bf16),
            jax.ShapeDtypeStruct((4,) + eout.shape, bf16),
        ),
        in_specs=[ANY] * 3,
        out_specs=(ANY,) * 3,
        scratch_shapes=[pltpu.VMEM((SEQ // 2, 128), bf16)] * 3
        + [DMA] * 3
        + RowGather.scratch
        + PlaneRing.scratch * 2,
        compiler_params=pltpu.CompilerParams(collective_id=number, has_side_effects=True),
        name="gather_heads",
    )(padded, ein, eout)


def attend_back_kernel(
    src, order, q_ref, k_ref, v_ref, lse_ref, do_ref, cos_ref, sin_ref, out_ref, do_nat, acc, done
):
    core = lax.axis_index("core")
    for b in range(SEQ // BLOCK):
        rows = pl.ds(pl.multiple_of(src[b] * BLOCK, BLOCK), BLOCK)
        pair = do_ref[rows, :].astype(f32)
        do_nat[pl.ds(b * BLOCK, BLOCK), :] = jnp.where(core == 0, pair[:, :64], pair[:, 64:])
    acc[...] = jnp.zeros_like(acc)
    step = 256
    for i in range(SEQ // step):
        length = (i + 1) * step
        here = pl.ds(i * step, step)
        query, d_out = q_ref[here, :], do_nat[here, :].astype(bf16)
        keys = k_ref[0:length, :]
        scores = dot_last(query, keys) * 0.125
        row = i * step + lax.broadcasted_iota(jnp.int32, (step, length), 0)
        column = lax.broadcasted_iota(jnp.int32, (step, length), 1)
        probs = jnp.where(column <= row, jnp.exp(scores - lse_ref[here, :]), 0.0)
        d_probs = dot_last(d_out, v_ref[0:length, :])
        delta = jnp.sum(probs * d_probs, axis=1, keepdims=True)
        d_scores = (probs * (d_probs - delta)).astype(bf16)
        acc[here, 0:64] = dot(d_scores, keys) * 0.125
        acc[0:length, 64:128] += dot_first(d_scores, query) * 0.125
        acc[0:length, 128:192] += dot_first(probs.astype(bf16), d_out)
    for b in range(SEQ // BLOCK):
        here = pl.ds(b * BLOCK, BLOCK)
        qk = acc[here, 0:128]
        qk = qk * cos_ref[here, :] - swap_halves(qk) * sin_ref[here, :]
        done[here, 0:128] = qk
        done[here, 128:256] = acc[here, 128:256]
    for b in range(SEQ // BLOCK):
        rows = pl.ds(pl.multiple_of(order[b] * BLOCK, BLOCK), BLOCK)
        out_ref[pl.ds(b * BLOCK, BLOCK), :] = done[rows, :].astype(bf16)


def attend_back(src, order, q, k, v, lse, d_out, cosine, sine):
    return pl.pallas_call(
        attend_back_kernel,
        out_shape=jax.ShapeDtypeStruct((SEQ, 256), bf16),
        in_specs=[SMEM, SMEM] + [VMEM] * 7,
        out_specs=VMEM,
        scratch_shapes=[
            pltpu.VMEM((SEQ, HEAD_DIM), f32),
            pltpu.VMEM((SEQ, 256), f32),
            pltpu.VMEM((SEQ, 256), f32),
        ],
        compiler_params=pltpu.CompilerParams(vmem_limit_bytes=56 * 2**20),
        cost_estimate=pl.CostEstimate(flops=3 * 10**9, bytes_accessed=6 * 2**20, transcendentals=2**21),
        name="attention_backward",
    )(src, order, q, k, v, lse, d_out, cosine, sine)


def rotary_tables():
    inverse = 10000.0 ** (-np.arange(32, dtype=np.float64) * 2.0 / HEAD_DIM)
    angles = np.arange(SEQ, dtype=np.float64)[:, None] * inverse[None, :]
    cosine, sine = np.cos(angles), np.sin(angles)
    return (
        np.tile(cosine, (1, 4)).astype(np.float32),
        np.concatenate([-sine, sine, -sine, sine], axis=1).astype(np.float32),
    )


def normalize(inputs, gain_values):
    scale_rows = lax.rsqrt(jnp.mean(inputs * inputs, axis=-1, keepdims=True) + epsilon)
    normed = inputs * scale_rows
    return (scale_rows, normed, (normed * gain_values.astype(f32)).astype(bf16))


def norm_backward(grad_in, normed, scale_rows, gain_values):
    grad_normed = grad_in * gain_values.astype(f32)
    inner = jnp.mean(grad_normed * normed, axis=-1, keepdims=True)
    return (scale_rows * (grad_normed - normed * inner), jnp.sum(grad_in * normed, axis=0))


def halves(value):
    high = lax.reduce_precision(value, 8, 7)
    return high.astype(bf16), (value - high).astype(bf16)


def local(
    tokens,
    cotangent,
    block_order,
    routes,
    norm_one,
    w_query,
    w_key,
    w_value,
    w_out,
    norm_two,
    w_router,
    expert_in,
    expert_out,
):
    ctx = lax.axis_index(CTX)
    cosine, sine = (jnp.asarray(t) for t in rotary_tables())
    order = jnp.stack([block_order, 2 * N_CTX - 1 - block_order], axis=1).reshape(-1)
    spots = jnp.arange(2 * N_CTX, dtype=jnp.int32)
    src = jnp.sum(jnp.where(order[None, :] == spots[:, None], spots[None, :], 0), axis=1)

    small = jnp.concatenate(
        [w_router, norm_one[:, None], norm_two[:, None], jnp.zeros((8, 30), bf16)], axis=1
    )
    tokens_all, packed_all, out_all, members, in_own, down_own, in_beyond, down_beyond = entry(
        tokens, w_query, w_key, w_value, small, w_out, routes, expert_in, expert_out, 0
    )
    low = packed_all[:, :, 8:, :].reshape(D, 128)
    weight = jnp.concatenate(
        [packed_all[:, :, :8, :].reshape(D, 128), low[:, :64], jnp.zeros((D, 64), bf16)], axis=1
    )
    router_weight, gain_one, gain_two = low[:, 64:96], low[:, 96], low[:, 97]
    out_weight = out_all.reshape(D, D)
    head_weight = lax.dynamic_slice_in_dim(out_weight, ctx * HEAD_DIM, HEAD_DIM, axis=0)

    tokens_float = tokens.astype(f32)
    scale_one, normed_one, _ = normalize(tokens_float, gain_one)
    _, _, hidden_one = normalize(tokens_all.reshape(SEQ, D).astype(f32), gain_one)
    raw = dot(hidden_one, weight)
    attended, padded, query, key, value, lse = attend(src, order, raw, cosine, sine)
    attended_all, in_far, down_far = gather_heads(padded, in_beyond, down_beyond, 1)

    router_wide = jnp.pad(router_weight, ((0, 0), (64, 32)))
    (
        out_sum,
        residual,
        d_residual,
        d_branch,
        d_logits,
        hidden_two,
        grad_gain_two,
        grad_experts,
        d_heads,
    ) = experts(
        tokens_all,
        attended_all,
        out_weight,
        members,
        router_wide,
        gain_two.astype(f32)[None, :],
        cotangent,
        (in_own, in_far, down_own, down_far),
        3,
    )
    output = residual + out_sum
    grad_experts = lax.psum_scatter(grad_experts, DP, scatter_dimension=0).astype(f32)
    grad_in = grad_experts[:, :ROWS]
    grad_down = grad_experts[:, ROWS:].reshape(2, 64, 8, ROWS).swapaxes(1, 2).reshape(2, FF, ROWS)

    d_raw = attend_back(src, order, query, key, value, lse, d_heads.reshape(SEQ, 128), cosine, sine)
    side = jnp.stack([1.0 / gain_one.astype(f32), grad_gain_two[0]], axis=1)
    side = jnp.pad(side, ((0, 0), (0, 126)))
    blocks = (8, 2, ROWS, D)
    d_hidden_one, a, b = last(
        d_raw,
        weight,
        side,
        d_branch,
        d_logits,
        hidden_one,
        attended_all.reshape(blocks),
        hidden_two,
        5,
    )
    d_norm_one, _ = norm_backward(d_hidden_one, normed_one, scale_one, gain_one)
    input_grad = d_residual + d_norm_one

    side_by_side = lambda v: jnp.moveaxis(v, 0, 1).reshape(8, -1)
    pairs = a.reshape(KV_HEADS, 2, 8, 256).sum(axis=1)
    common = jnp.sum(a[:, :, 192:], axis=0)
    return (
        output,
        input_grad,
        common[:, 0],
        side_by_side(a[:, :, 0:64]),
        side_by_side(pairs[:, :, 64:128]),
        side_by_side(pairs[:, :, 128:192]),
        side_by_side(b),
        common[:, 1],
        common[:, 2:34],
        grad_in,
        grad_down,
    )


def solution(mesh):
    split = Mesh(mesh.devices.reshape(2, 4, 2, 4, 2), AXES)
    rows = P(AXES, None)
    line = P(AXES)
    return jax.shard_map(
        local,
        mesh=split,
        in_specs=(
            rows,
            rows,
            P(),
            rows,
            line,
            rows,
            rows,
            rows,
            rows,
            line,
            rows,
            P(CTX, DP, None),
            P(CTX, None, DP),
        ),
        out_specs=(
            rows,
            rows,
            line,
            rows,
            rows,
            rows,
            rows,
            line,
            rows,
            P(CTX, DP, None),
            P(CTX, None, DP),
        ),
        check_vma=False,
    )
```

```python
import functools
import math

import jax
import jax.numpy as jnp
import numpy as np
from jax import lax
from jax.experimental import pallas as pl
from jax.experimental.pallas import tpu as pltpu
from jax.sharding import Mesh
from jax.sharding import PartitionSpec as P

D = 1024
HEADS = 16
KV_HEADS = 8
HEAD_DIM = 64
EXPERTS = 32
FF = 512
TOP = 8
MOST = 48
ROWS = 128
SEQ = 2048
BLOCK = 64
AXES = ("ylo", "z", "yhi", "x", "core")
DP = ("ylo", "z")
CTX = ("yhi", "x", "core")
N_DP = 8
N_CTX = 16
EXTRA = 128
MESH_ID = pl.DeviceIdType.MESH
ANY = pl.BlockSpec(memory_space=pl.ANY)
VMEM = pl.BlockSpec(memory_space=pltpu.VMEM)
SMEM = pl.BlockSpec(memory_space=pltpu.SMEM)
DMA = pltpu.SemaphoreType.DMA
bf16 = jnp.bfloat16
f32 = jnp.float32
epsilon = 1e-06


def dot(a, b):
    return jnp.dot(a, b, preferred_element_type=f32)


def dot_last(a, b):
    return lax.dot_general(a, b, (((1,), (1,)), ((), ())), preferred_element_type=f32)


def dot_first(a, b):
    return lax.dot_general(a, b, (((0,), (0,)), ((), ())), preferred_element_type=f32)


def my_place():
    return tuple(lax.axis_index(a) for a in AXES)


def device_at(dp, ctx):
    return (
        lax.div(dp, 4),
        lax.rem(dp, 4),
        lax.div(ctx, 8),
        lax.rem(lax.div(ctx, 2), 4),
        lax.rem(ctx, 2),
    )


def beside(place, dy, dx):
    ylo, z, yhi, x, core = place
    return (ylo, z, lax.rem(yhi + dy, 2), lax.rem(x + dx, 4), core)


def ctx_of(place):
    return place[2] * 8 + place[3] * 2 + place[4]


def dp_of(place):
    return place[0] * 4 + place[1]


def sibling_of(place):
    return place[:4] + (1 - place[4],)


def remote(src, dst, send, recv, device):
    return pltpu.make_async_remote_copy(
        src_ref=src, dst_ref=dst, send_sem=send, recv_sem=recv, device_id=device, device_id_type=MESH_ID
    )


def greet(devices):
    barrier = pltpu.get_barrier_semaphore()
    for device in devices:
        pl.semaphore_signal(barrier, inc=1, device_id=device, device_id_type=MESH_ID)
    return barrier


class RowGather:
    scratch = [DMA, DMA((9,)), DMA((9,)), DMA((10,)), DMA((10,))]
    links = [(1, 0), (0, 1), (0, 3), (0, 1), (0, 3), (0, 1), (0, 3), (0, 1), (0, 3)]
    held = [(0, 0), (0, 0), (0, 0), (1, 0), (1, 0), (0, 3), (0, 1), (1, 3), (1, 1)]
    parts = [None, None, None, None, None, 0, 1, 0, 1]
    after = {0: (3, 4), 1: (5,), 2: (6,), 3: (7,), 4: (8,)}

    def __init__(self, place, x_ref, view, half, local, send, recv, fsend, frecv):
        sibling = sibling_of(place)

        def piece(dy, dx, part):
            ref = view(beside(place, dy, dx))
            return ref if part is None else ref.at[pl.ds(part * half, half)]

        self.own = pltpu.make_async_copy(x_ref, view(place), local)
        self.out, self.landed, self.passed = [], [], []
        for n, ((ly, lx), (hy, hx), part) in enumerate(zip(self.links, self.held, self.parts)):
            source = x_ref if n < 3 else piece(hy, hx, part)
            self.out.append(
                remote(source, piece(hy, hx, part), send.at[n], recv.at[n], beside(place, ly, lx))
            )
            here = piece((hy + ly) % 2, (hx + 4 - lx) % 4, part)
            self.landed.append(remote(here, here, send.at[n], recv.at[n], beside(place, ly, lx)))
            self.passed.append(remote(here, here, fsend.at[n], frecv.at[n], sibling))
        self.passed.append(remote(x_ref, view(place), fsend.at[9], frecv.at[9], sibling))
        self.back = []
        for n in range(9):
            (ly, lx), (hy, hx), part = self.links[n], self.held[n], self.parts[n]
            ref = view(sibling_of(beside(place, (hy + ly) % 2, (hx + 4 - lx) % 4)))
            ref = ref if part is None else ref.at[pl.ds(part * half, half)]
            self.back.append(remote(ref, ref, fsend.at[n], frecv.at[n], sibling))
        ref = view(sibling)
        self.back.append(remote(ref, ref, fsend.at[9], frecv.at[9], sibling))

    def start(self):
        for n in range(3):
            self.out[n].start()
        self.passed[9].start()
        self.own.start()

    def step(self, n):
        self.landed[n].wait_recv()
        for m in self.after.get(n, ()):
            self.out[m].start()
        self.passed[n].start()

    def pass_on(self):
        for n in range(9):
            self.step(n)

    def finish(self):
        self.own.wait()
        for n in range(10):
            self.back[n].wait_recv()
        for copy in self.out + self.passed:
            copy.wait_send()


def chip_neighbours(place):
    return [beside(place, 1, 0), beside(place, 0, 1), beside(place, 0, 3), sibling_of(place)]


SPREAD = [(1, 2), (0, 2), (1, 1), (1, 3), (0, 1), (0, 3), (1, 0), (0, 0)]


class RowScatter:
    @staticmethod
    def scratch(rows, width):
        return [
            pltpu.VMEM((8, rows, width), bf16),
            pltpu.VMEM((8, rows, width), bf16),
            pltpu.VMEM((4, rows // 2, width), bf16),
            pltpu.VMEM((4, rows, width), bf16),
            pltpu.VMEM((rows, width), bf16),
            DMA((8,)),
            DMA((8,)),
            DMA((8,)),
            DMA((9,)),
            DMA((9,)),
        ]

    def __init__(self, place, part, own, other, halves, wholes, last, own_sem, fsend, frecv, send, recv):
        self.own, self.other, self.halves, self.wholes, self.last = own, other, halves, wholes, last
        core = place[4]
        half = own.shape[1] // 2
        self.half = half
        self.mine, self.cross = [], []
        for n, (dy, dx) in enumerate(SPREAD):
            chip = lax.div(ctx_of(beside(place, dy, dx)), 2)
            self.mine.append(pltpu.make_async_copy(part(chip, core), own.at[n], own_sem.at[n]))
            self.cross.append(
                remote(part(chip, 1 - core), other.at[n], fsend.at[n], frecv.at[n], sibling_of(place))
            )
        right, left = beside(place, 0, 1), beside(place, 0, 3)
        self.out = []
        for n, (source, target, device) in enumerate(
            [
                (own.at[0, pl.ds(0, half)], halves.at[0], right),
                (own.at[0, pl.ds(half, half)], halves.at[1], left),
                (own.at[1, pl.ds(0, half)], halves.at[2], right),
                (own.at[1, pl.ds(half, half)], halves.at[3], left),
                (own.at[2], wholes.at[0], right),
                (own.at[3], wholes.at[1], left),
                (own.at[4], wholes.at[2], right),
                (own.at[5], wholes.at[3], left),
                (own.at[6], last, beside(place, 1, 0)),
            ]
        ):
            self.out.append(remote(source, target, send.at[n], recv.at[n], device))

    def start(self, n):
        self.cross[n].start()
        self.mine[n].start()

    def release(self):
        for n in range(8):
            self.cross[n].wait_send()

    def join(self, n):
        self.mine[n].wait()
        self.cross[n].wait_recv()
        return self.own[n].astype(f32) + self.other[n].astype(f32)

    def step(self, n):
        if n < 2:
            self.own[n] = self.join(n).astype(bf16)
            self.out[2 * n].start()
            self.out[2 * n + 1].start()
        elif n < 6:
            total = self.join(n)
            half = self.half
            side = pl.ds(0 if n % 2 == 0 else half, half)
            self.out[n - 2].wait_recv()
            self.own[n] = total.astype(bf16)
            first = total[:half] if n % 2 == 0 else total[half:]
            self.own[n, side] = (first + self.halves[n - 2].astype(f32)).astype(bf16)
            self.out[n + 2].start()
        elif n == 6:
            total = self.join(6)
            for m in (0, 1):
                self.out[4 + m].wait_recv()
                total = total + self.wholes[m].astype(f32)
            self.own[6] = total.astype(bf16)
            self.out[8].start()
        else:
            total = self.join(7)
            for m in (2, 3):
                self.out[4 + m].wait_recv()
                total = total + self.wholes[m].astype(f32)
            self.out[8].wait_recv()
            return total + self.last[...].astype(f32)

    def finish(self):
        for copy in self.out:
            copy.wait_send()


def entry_kernel(
    x_ref, q_ref, k_ref, v_ref, small_ref, o_ref, routes_ref, x_out, w_out, o_out, m_out,
    w_pack, o_pad, o_other, o_mid, m_pack, *sems,
):
    row_sems, o_sems, m_sems, rest = sems[:5], sems[5:10], sems[10:15], sems[15:]
    wlocal, wsend, wrecv, psend, precv, xsend, xrecv, osend, orecv = rest
    place = my_place()
    core = place[4]
    dp, ctx = dp_of(place), ctx_of(place)
    barrier = greet(
        [device_at(dp, lax.rem(ctx + k, N_CTX)) for k in range(1, N_CTX)]
        + [device_at(lax.rem(dp + k, N_DP), ctx) for k in range(1, N_DP)]
    )
    pl.semaphore_wait(barrier, 22)
    rows = RowGather(place, x_ref, lambda p: x_out.at[ctx_of(p)], x_ref.shape[0] // 2, *row_sems)
    rows.start()

    out = o_ref[...].astype(f32)
    empty = jnp.zeros_like(out)
    out = jnp.where(core == 0, jnp.concatenate([out, empty], 0), jnp.concatenate([empty, out], 0))
    for s in range(2):
        o_pad[s] = out[:, s * 512 : (s + 1) * 512].astype(bf16)
    swap = remote(o_pad.at[1 - core], o_other, xsend, xrecv, sibling_of(place))
    swap.start()
    query, key, value = (r[...].astype(f32) for r in (q_ref, k_ref, v_ref))
    small = small_ref[...].astype(f32)
    for h in range(HEADS):
        at, pair = slice(h * 64, h * 64 + 64), slice(h // 2 * 64, h // 2 * 64 + 64)
        top = jnp.concatenate([query[:, at], key[:, pair]], axis=1)
        low = jnp.concatenate([value[:, pair], small], axis=1)
        w_pack[h] = jnp.concatenate([top, low], axis=0).astype(bf16)
    first, second, third = [], [], []
    for k in range(1, N_CTX):
        to = lax.rem(ctx + k, N_CTX)
        first.append(
            remote(w_pack.at[to], w_out.at[dp, ctx], wsend.at[k], wrecv.at[k], device_at(dp, to))
        )
    for k in range(1, N_DP):
        device = device_at(lax.rem(dp + k, N_DP), ctx)
        third.append(remote(o_mid.at[dp], o_mid.at[dp], osend.at[k], orecv.at[k], device))
        second.append(remote(w_out.at[dp], w_out.at[dp], psend.at[k], precv.at[k], device))
    for copy in first:
        copy.start()
    own = pltpu.make_async_copy(w_pack.at[ctx], w_out.at[dp, ctx], wlocal)
    own.start()
    swap.wait_recv()
    o_mid[dp] = o_pad[core] + o_other[...]
    for copy in third:
        copy.start()
    routes = routes_ref[...]
    lane = lax.broadcasted_iota(jnp.int32, (ROWS, EXTRA), 1) - 64
    member = jnp.zeros((ROWS, EXTRA), f32)
    for k in range(TOP):
        member = jnp.where(lane == routes[:, k : k + 1], 1.0, member)
    m_pack[...] = member.astype(bf16)
    members = RowGather(place, m_pack, lambda p: m_out.at[ctx_of(p)], ROWS // 2, *m_sems)
    members.start()
    own.wait()
    for copy in first:
        copy.wait_recv()
    for copy in second:
        copy.start()
    for copy in third:
        copy.wait_recv()

    def o_view(p):
        return o_out.at[:, p[2] * 4 + p[3], :, pl.ds(pl.multiple_of(p[4] * 512, 512), 512)]

    outs = RowGather(place, o_mid, o_view, 4, *o_sems)
    outs.start()
    for n in range(5):
        rows.step(n)
    for n in range(9):
        members.step(n)
    for n in range(3):
        outs.step(n)
    for n in range(5, 9):
        rows.step(n)
    for n in range(3, 9):
        outs.step(n)
    rows.finish()
    members.finish()
    outs.finish()
    for copy in second:
        copy.wait_recv()
    swap.wait_send()
    for copy in first + second + third:
        copy.wait_send()


def entry(x, query, key, value, small, out, routes, number):
    return pl.pallas_call(
        entry_kernel,
        out_shape=(
            jax.ShapeDtypeStruct((N_CTX,) + x.shape, bf16),
            jax.ShapeDtypeStruct((N_DP, N_CTX, 16, 128), bf16),
            jax.ShapeDtypeStruct((N_DP, 8, 16, D), bf16),
            jax.ShapeDtypeStruct((N_CTX, ROWS, EXTRA), bf16),
        ),
        in_specs=[ANY] + [VMEM] * 6,
        out_specs=(ANY,) * 4,
        scratch_shapes=[
            pltpu.VMEM((N_CTX, 16, 128), bf16),
            pltpu.VMEM((2, 16, 512), bf16),
            pltpu.VMEM((16, 512), bf16),
            pltpu.VMEM((N_DP, 16, 512), bf16),
            pltpu.VMEM((ROWS, EXTRA), bf16),
        ]
        + RowGather.scratch * 3
        + [DMA, DMA((16,)), DMA((16,)), DMA((8,)), DMA((8,)), DMA, DMA, DMA((8,)), DMA((8,))],
        compiler_params=pltpu.CompilerParams(
            collective_id=number, has_side_effects=True, vmem_limit_bytes=16 * 2**20
        ),
        name="entry_gather",
    )(x, query, key, value, small, out, routes)


def last_kernel(
    d_raw, weight, side, d_branch, d_logits, hidden_ref, att_ref, hid_ref, one_ref, a_out, w_out,
    hidden, att, hid, parts, w_parts, a_pack, landed, part, w_sum, w_landed, w_mine,
    in_sem, wlocal, wsend, wrecv, psend, precv, plocal, osend, orecv, olocal, xsend, xrecv, *scatters,
):
    place = my_place()
    core = place[4]
    dp, ctx = dp_of(place), ctx_of(place)
    barrier = greet(
        [device_at(dp, lax.rem(ctx + k, N_CTX)) for k in range(1, N_CTX)]
        + [device_at(lax.rem(dp + k, N_DP), ctx) for k in range(1, N_DP)]
    )
    loads = [
        pltpu.make_async_copy(att_ref.at[lax.div(ctx, 2), core], att, in_sem.at[0]),
        pltpu.make_async_copy(hid_ref, hid, in_sem.at[1]),
        pltpu.make_async_copy(hidden_ref, hidden, in_sem.at[2]),
    ]
    for load in loads:
        load.start()

    def back(c, _):
        here = pl.ds(pl.multiple_of(c * ROWS, ROWS), ROWS)
        parts[lax.div(c, 2), lax.rem(c, 2)] = dot_last(d_raw[here, :], weight[...]).astype(bf16)
        return 0

    lax.fori_loop(0, N_CTX, back, 0)
    pl.semaphore_wait(barrier, 22)
    rows = RowScatter(place, lambda chip, c: parts.at[chip, c], *scatters[:10])
    outs = RowScatter(place, lambda chip, c: w_parts.at[chip, c], *scatters[10:])
    for n in range(8):
        rows.start(n)
    for load in loads:
        load.wait()

    def heads(k, _):
        here = pl.ds(pl.multiple_of(k * ROWS, ROWS), ROWS)
        grad = dot_first(hidden[:, here], d_raw[...])
        gain = jnp.sum(grad * weight[here, :].astype(f32), axis=1, keepdims=True)
        lane = lax.broadcasted_iota(jnp.int32, (ROWS, 128), 1)
        extra = side[here, :]
        high = grad[:, 128:] + dot_first(hid[:, here], d_logits[...])
        high = jnp.where(lane == 64, gain * extra[:, 0:1], jnp.where(lane == 65, extra[:, 1:2], high))
        a_pack[k, :, :128] = grad[:, :128].astype(bf16)
        a_pack[k, :, 128:] = high.astype(bf16)
        return 0

    lax.fori_loop(0, N_DP, heads, 0)
    first, second, third = [], [], []
    for k in range(1, N_DP):
        to = lax.rem(dp + k, N_DP)
        first.append(remote(a_pack.at[to], landed.at[k], wsend.at[k], wrecv.at[k], device_at(to, ctx)))
        third.append(
            remote(
                w_sum.at[pl.ds(pl.multiple_of(to * 16, 16), 16)],
                w_landed.at[k],
                osend.at[k],
                orecv.at[k],
                device_at(to, ctx),
            )
        )
    for copy in first:
        copy.start()
    own = pltpu.make_async_copy(a_pack.at[dp], landed.at[0], wlocal)
    own.start()
    rows.step(0)
    rows.step(1)

    def products(k, _):
        here = pl.ds(pl.multiple_of(k * ROWS, ROWS), ROWS)
        total = dot_first(att[:, here], d_branch[...]).astype(bf16)
        to = pl.ds(pl.multiple_of(k * 16, 16), 16)
        for g in range(8):
            for c in range(2):
                w_parts[g, c, to, :] = total[g * 16 : (g + 1) * 16, c * 512 : (c + 1) * 512]
        return 0

    lax.fori_loop(0, N_DP, products, 0)
    for n in range(8):
        outs.start(n)
    for n in range(2, 6):
        rows.step(n)
    outs.step(0)
    outs.step(1)
    own.wait()
    for copy in first:
        copy.wait_recv()
    total = landed[0].astype(f32)
    for k in range(1, N_DP):
        total = total + landed[k].astype(f32)
    part[...] = total.reshape(part.shape)
    for k in range(1, N_CTX):
        to = lax.rem(ctx + k, N_CTX)
        second.append(remote(part.at[to], a_out.at[ctx], psend.at[k], precv.at[k], device_at(dp, to)))
    for copy in second:
        copy.start()
    mine = pltpu.make_async_copy(part.at[ctx], a_out.at[ctx], plocal)
    mine.start()
    rows.step(6)
    for n in range(2, 6):
        outs.step(n)
    one_ref[...] = rows.step(7)
    outs.step(6)
    w_sum[...] = outs.step(7)
    for copy in third:
        copy.start()
    own = pltpu.make_async_copy(w_sum.at[pl.ds(pl.multiple_of(dp * 16, 16), 16)], w_landed.at[0], olocal)
    own.start()
    own.wait()
    for copy in third:
        copy.wait_recv()
    total = w_landed[0]
    for k in range(1, N_DP):
        total = total + w_landed[k]
    w_mine[...] = total.reshape(2, 8, 512)
    swap = remote(w_mine.at[1 - core], w_out.at[core], xsend, xrecv, sibling_of(place))
    swap.start()
    keep = pltpu.make_async_copy(w_mine.at[core], w_out.at[core], in_sem.at[0])
    swap_in = remote(w_mine.at[1 - core], w_out.at[1 - core], xsend, xrecv, sibling_of(place))
    swap_in.wait_recv()
    swap.wait_send()
    keep.start()
    keep.wait()
    mine.wait()
    for copy in second:
        copy.wait_recv()
    rows.release()
    outs.release()
    rows.finish()
    outs.finish()
    for copy in first + second + third:
        copy.wait_send()


def last(d_raw, weight, side, d_branch, d_logits, hidden, att, hid, number):
    v = lambda *shape: pltpu.VMEM(shape, bf16)
    return pl.pallas_call(
        last_kernel,
        out_shape=(
            jax.ShapeDtypeStruct((ROWS, D), f32),
            jax.ShapeDtypeStruct((N_CTX, 8, 256), f32),
            jax.ShapeDtypeStruct((2, 8, 512), f32),
        ),
        in_specs=[VMEM] * 5 + [ANY] * 3,
        out_specs=(VMEM,) * 3,
        scratch_shapes=[
            v(SEQ, D),
            v(ROWS, D),
            v(ROWS, D),
            v(8, 2, ROWS, D),
            v(8, 2, ROWS, 512),
            v(N_DP, ROWS, 256),
            v(N_DP, ROWS, 256),
            pltpu.VMEM((N_CTX, 8, 256), f32),
            pltpu.VMEM((ROWS, 512), f32),
            pltpu.VMEM((N_DP, 16, 512), f32),
            pltpu.VMEM((2, 8, 512), f32),
            DMA((3,)),
            DMA,
            DMA((8,)),
            DMA((8,)),
            DMA((16,)),
            DMA((16,)),
            DMA,
            DMA((8,)),
            DMA((8,)),
            DMA,
            DMA,
            DMA,
        ]
        + RowScatter.scratch(ROWS, D)
        + RowScatter.scratch(ROWS, 512),
        compiler_params=pltpu.CompilerParams(
            collective_id=number, has_side_effects=True, vmem_limit_bytes=48 * 2**20
        ),
        name="last_sums",
    )(d_raw, weight, side, d_branch, d_logits, hidden, att, hid)


def second_norm(token, att, wide, gain):
    residual = token.astype(f32) + dot(att[:, :FF], wide[0]) + dot(att[:, FF:], wide[1])
    scale = lax.rsqrt(jnp.mean(residual * residual, axis=1, keepdims=True) + epsilon)
    normed = residual * scale
    return residual, scale, normed, (normed * gain).astype(bf16)


def gates_of(logits, inside):
    logits = jnp.where(inside > 0.5, logits, -1e30)
    weights = jnp.exp(logits - jnp.max(logits, axis=1, keepdims=True))
    weights = jnp.where(inside > 0.5, weights, 0.0)
    return weights / jnp.sum(weights, axis=1, keepdims=True)


def experts_kernel(
    tok_ref, att_ref, wo_ref, m_ref, router_ref, gain_ref, cot_ref, w_ref,
    out_ref, d_ref, g_ref,
    pool, members, win, wide, picks, facts_all, gates_all, logits_all, gate_slot, dg_slot,
    rows, tops, result, hidden, d_mid, in_sem, tok_sem, *scatters,
):
    body = pl.ds(0, D)
    loads = [
        pltpu.make_async_copy(wo_ref, wide, in_sem.at[0]),
        pltpu.make_async_copy(m_ref, members, in_sem.at[1]),
        pltpu.make_async_copy(w_ref, win, in_sem.at[2]),
    ]
    place = my_place()
    ctx = ctx_of(place)

    def tokens_of(i):
        return result.at[i // 3, pl.ds(i % 3 * 256, 256)] if i < 6 else tops.at[0, pl.ds((i - 6) * 256, 256)]

    streams = []
    for i in range(8):
        streams.append(
            (
                pltpu.make_async_copy(tok_ref.at[i], tokens_of(i), tok_sem.at[0, i]),
                pltpu.make_async_copy(att_ref.at[i], pool.at[i, :, 0, :, body], tok_sem.at[1, i]),
            )
        )
    loads[0].start()
    for pair in streams[:2]:
        pair[0].start()
        pair[1].start()
    pl.semaphore_wait(greet(chip_neighbours(place)), 4)
    gather = RowGather(
        place,
        cot_ref,
        lambda p: pool.at[p[2] * 4 + p[3], p[4], 1, :, body],
        ROWS // 2,
        *scatters[20:],
    )
    gather.start()
    for pair in streams[2:]:
        pair[0].start()
        pair[1].start()
    for load in loads[1:]:
        load.start()
    line = lax.broadcasted_iota(jnp.int32, (8, EXTRA), 0)
    lane = lax.broadcasted_iota(jnp.int32, (8, EXTRA), 1)
    chosen = jnp.logical_and(line < 2, lane == 64 + 2 * ctx + line)
    chosen = jnp.where(chosen, 1.0, 0.0).astype(bf16)
    back = jnp.logical_and(line < 4, lane == jnp.where(line < 2, 0, 32) + 2 * ctx + lax.rem(line, 2))
    back = jnp.where(back, 1.0, 0.0).astype(bf16)
    before = lax.broadcasted_iota(jnp.int32, (ROWS, ROWS), 0) < lax.broadcasted_iota(
        jnp.int32, (ROWS, ROWS), 1
    )
    before = jnp.where(before, 1.0, 0.0).astype(bf16)
    slots = lax.broadcasted_iota(jnp.int32, (MOST, ROWS), 0).astype(f32)

    loads[0].wait()
    for i in range(8):
        for copy in streams[i]:
            copy.wait()
        att = pool[i, :, 0, :, :D].reshape(2 * ROWS, D)
        token = (
            result[i // 3, i % 3 * 256 : i % 3 * 256 + 256]
            if i < 6
            else tops[0, (i - 6) * 256 : (i - 5) * 256]
        )
        hid = second_norm(token, att, wide, gain_ref[...])[3]
        pool[i, :, 0, :, :D] = hid.reshape(2, ROWS, D)
        logits_all[i * 256 : (i + 1) * 256] = dot(hid, router_ref[...])
        if i == 2:
            gather.step(0)
    gather.step(1)
    gather.step(2)
    loads[1].wait()
    for half in range(2):
        inside = members[8 * half : 8 * half + 8].reshape(8 * ROWS, EXTRA)
        gates = gates_of(logits_all[1024 * half : 1024 * (half + 1)], inside.astype(f32))
        high = gates.astype(bf16)
        rest = (gates - high.astype(f32)).astype(bf16)
        facts = dot_last(chosen, inside)
        lines = dot_last(chosen, high) + dot_last(chosen, rest)
        for c in range(8):
            facts_all[8 * half + c] = facts[:, c * ROWS : (c + 1) * ROWS]
            gates_all[8 * half + c] = lines[:, c * ROWS : (c + 1) * ROWS]

    def pick(i, _):
        for k in range(4):
            c = i * 4 + k
            facts, lines = facts_all[c], gates_all[c]
            order = dot(facts.astype(bf16), before)
            here = pl.ds(pl.multiple_of(c * MOST, MOST), MOST)
            both = []
            for e in range(2):
                member = facts[e : e + 1]
                onehot = jnp.where(jnp.logical_and(order[e : e + 1] == slots, member > 0.5), 1.0, 0.0)
                gate_slot[e, here] = jnp.sum(onehot * lines[e : e + 1], axis=1, keepdims=True)
                both.append(onehot.astype(bf16))
            both = jnp.concatenate(both, axis=0)
            picks[c] = both
            taken = dot(both, pool[i * 2 + k // 2, k % 2, 0, :, :D]).astype(bf16)
            rows[0, here] = taken[:MOST]
            rows[1, here] = taken[MOST:]
        return 0

    lax.fori_loop(0, 4, pick, 0)
    for n in range(3, 5):
        gather.step(n)
    loads[2].wait()
    for e in range(2):
        for k in range(N_DP):
            for q in range(8):
                wide[e, q * 64 : (q + 1) * 64, k * ROWS : (k + 1) * ROWS] = win[
                    k, e, ROWS:, q * ROWS : (q + 1) * ROWS
                ]
    tile = 256

    def pick_tops(i, _):
        for k in range(4):
            c = i * 4 + k
            here = pl.ds(pl.multiple_of(c * MOST, MOST), MOST)
            taken = dot(picks[c], pool[i * 2 + k // 2, k % 2, 1, :, :D]).astype(bf16)
            tops[0, here] = taken[:MOST]
            tops[1, here] = taken[MOST:]
        return 0

    def forth(e, t):
        here = pl.ds(t * tile, tile)
        both = dot(rows[e, here], win[:, e, :ROWS].reshape(D, 2 * FF))
        gate_part, up_part = both[:, :FF], both[:, FF:]
        sigmoid = 1.0 / (1.0 + jnp.exp(-gate_part))
        silu = gate_part * sigmoid
        middle = (silu * up_part).astype(bf16)
        hidden[e, here] = middle
        d_mid[e, here, :FF] = (up_part * (sigmoid * (1.0 + gate_part * (1.0 - sigmoid)))).astype(bf16)
        d_mid[e, here, FF:] = silu.astype(bf16)
        result[e, here] = dot(middle, wide[e]).astype(bf16)

    def backward(e, t):
        here = pl.ds(t * tile, tile)
        top = tops[e, here].astype(f32)
        dg_slot[e, here] = jnp.sum(top * result[e, here].astype(f32), axis=1, keepdims=True)
        d_result = (top * gate_slot[e, here]).astype(bf16)
        tops[e, here] = d_result
        d_middle = dot_last(d_result, wide[e])
        d_mid[e, here, :FF] = (d_middle * d_mid[e, here, :FF].astype(f32)).astype(bf16)
        d_mid[e, here, FF:] = (d_middle * d_mid[e, here, FF:].astype(f32)).astype(bf16)
        weight = win[:, e, :ROWS].reshape(D, 2 * FF)
        result[e, here] = dot_last(d_mid[e, here], weight).astype(bf16)

    def combine_out(i, _):
        for k in range(4):
            c = i * 4 + k
            here = pl.ds(pl.multiple_of(c * MOST, MOST), MOST)
            found = [(result[e, here].astype(f32) * gate_slot[e, here]).astype(bf16) for e in range(2)]
            found = jnp.concatenate(found, axis=0)
            pool[i * 2 + k // 2, k % 2, 0, :, :D] = dot_first(picks[c], found).astype(bf16)
        return 0

    def combine_back(i, _):
        for k in range(4):
            c = i * 4 + k
            here = pl.ds(pl.multiple_of(c * MOST, MOST), MOST)
            both = picks[c]
            found = jnp.concatenate([result[0, here], result[1, here]], axis=0)
            pool[i * 2 + k // 2, k % 2, 1, :, :D] = dot_first(both, found).astype(bf16)
            lines = [
                jnp.sum(
                    both[e * MOST : (e + 1) * MOST].astype(f32) * dg_slot[e, here], axis=0, keepdims=True
                )
                for e in range(2)
            ]
            high = [v.astype(bf16).astype(f32) for v in lines]
            rest = [v - h for v, h in zip(lines, high)]
            lines = jnp.concatenate(high + rest + [jnp.zeros((4, ROWS), f32)], axis=0).astype(bf16)
            pool[i * 2 + k // 2, k % 2, 1, :, D:] = dot_first(lines, back).astype(bf16)
        return 0

    for e in range(2):
        for t in range(3):
            forth(e, t)
            if e == 0 and t < 2:
                gather.step(5 + 2 * t)
                gather.step(6 + 2 * t)
    lax.fori_loop(0, 4, combine_out, 0)
    first = RowScatter(place, lambda h, c: pool.at[h, c, 0, :, body], *scatters[:10])
    second = RowScatter(place, lambda h, c: pool.at[h, c, 1], *scatters[10:20])
    for n in range(8):
        first.start(n)
    gather.finish()
    first.step(0)
    first.step(1)
    lax.fori_loop(0, 4, pick_tops, 0)
    plan = [(), (), (2, 3), (4, 5), (), ()]
    for e in range(2):
        for t in range(3):
            backward(e, t)
            for n in plan[3 * e + t]:
                first.step(n)
    lax.fori_loop(0, 4, combine_back, 0)
    for n in range(8):
        second.start(n)
    first.step(6)
    second.step(0)
    second.step(1)
    def weights(e, k):
        here = pl.ds(k * 256, 256)
        total = dot_first(rows[e, :, here], d_mid[e]).astype(bf16)
        win[2 * k, e, :ROWS] = total[:ROWS]
        win[2 * k + 1, e, :ROWS] = total[ROWS:]
        total = dot_first(hidden[e], tops[e, :, here]).astype(bf16)
        for q in range(8):
            win[2 * k, e, ROWS:, q * ROWS : (q + 1) * ROWS] = total[q * 64 : (q + 1) * 64, :ROWS]
            win[2 * k + 1, e, ROWS:, q * ROWS : (q + 1) * ROWS] = total[q * 64 : (q + 1) * 64, ROWS:]

    plan = [(), (), (), (), (2, 3), (), (4, 5), ()]
    for e in range(2):
        for k in range(4):
            weights(e, k)
            for n in plan[4 * e + k]:
                second.step(n)
    save = pltpu.make_async_copy(win, g_ref, in_sem.at[2])
    save.start()
    second.step(6)
    out_ref[...] = first.step(7)
    d_ref[...] = second.step(7)
    save.wait()
    first.finish()
    second.finish()
    first.release()
    second.release()


def turn_kernel(
    total_ref, router_ref, gain_ref, tok_ref, att_ref, wo_ref, m_ref, cot_ref,
    res_ref, d_res_ref, d_branch_ref, d_logits_ref, hid_ref, gain_grad_ref, heads_ref,
    wide, own_rows, inside, d_heads, in_sem, hsend, hrecv,
):
    place = my_place()
    core = place[4]
    dp, ctx = dp_of(place), ctx_of(place)
    chip = lax.div(ctx, 2)
    loads = [
        pltpu.make_async_copy(wo_ref, wide, in_sem.at[0]),
        pltpu.make_async_copy(cot_ref, own_rows.at[0], in_sem.at[1]),
        pltpu.make_async_copy(tok_ref.at[chip, core], own_rows.at[1], in_sem.at[2]),
        pltpu.make_async_copy(att_ref.at[chip, core], own_rows.at[2], in_sem.at[3]),
        pltpu.make_async_copy(m_ref.at[ctx], inside, in_sem.at[4]),
    ]
    for load in loads:
        load.start()
    barrier = greet([device_at(dp, lax.rem(ctx + k, N_CTX)) for k in range(1, N_CTX)])
    for load in loads:
        load.wait()
    residual, scale, normed, hid = second_norm(own_rows[1], own_rows[2], wide, gain_ref[...])
    res_ref[...] = residual
    hid_ref[...] = hid
    gates = gates_of(dot(hid, router_ref[...]), inside[...].astype(f32))
    extra = total_ref[:, D:]
    d_gates = pltpu.roll(extra, 64, 1) + pltpu.roll(extra, 32, 1)
    d_picked = gates * (d_gates - jnp.sum(gates * d_gates, axis=1, keepdims=True))
    d_logits = d_picked.astype(bf16)
    d_logits_ref[...] = pltpu.roll(d_picked, 2, 1).astype(bf16)
    d_hid = total_ref[:, :D] + dot_last(d_logits, router_ref[...])
    gain_grad_ref[...] = jnp.sum(d_hid * normed, axis=0, keepdims=True)
    d_normed = d_hid * gain_ref[...]
    inner = jnp.mean(d_normed * normed, axis=1, keepdims=True)
    d_res = own_rows[0].astype(f32) + scale * (d_normed - normed * inner)
    d_res_ref[...] = d_res
    d_branch = d_res.astype(bf16)
    d_branch_ref[...] = d_branch
    for s in range(2):
        d_att = dot_last(d_branch, wide[s]).astype(bf16)
        for g in range(4):
            d_heads[4 * s + g] = d_att[:, g * 128 : (g + 1) * 128]
    pl.semaphore_wait(barrier, 15)
    copies = []
    for k in range(1, N_CTX):
        to = lax.rem(ctx + k, N_CTX)
        copies.append(
            remote(
                d_heads.at[lax.div(to, 2)], heads_ref.at[ctx], hsend.at[k], hrecv.at[k], device_at(dp, to)
            )
        )
    for copy in copies:
        copy.start()
    own = pltpu.make_async_copy(d_heads.at[chip], heads_ref.at[ctx], in_sem.at[0])
    own.start()
    own.wait()
    for copy in copies:
        copy.wait_recv()
    for copy in copies:
        copy.wait_send()


def turn(total, router, gain, tok, att, wo, members, cot, number):
    v = lambda *shape: pltpu.VMEM(shape, bf16)
    blocks = (8, 2, ROWS, D)
    return pl.pallas_call(
        turn_kernel,
        out_shape=(
            jax.ShapeDtypeStruct((ROWS, D), f32),
            jax.ShapeDtypeStruct((ROWS, D), f32),
            jax.ShapeDtypeStruct((ROWS, D), bf16),
            jax.ShapeDtypeStruct((ROWS, EXTRA), bf16),
            jax.ShapeDtypeStruct((ROWS, D), bf16),
            jax.ShapeDtypeStruct((1, D), f32),
            jax.ShapeDtypeStruct((N_CTX, ROWS, 128), bf16),
        ),
        in_specs=[VMEM] * 3 + [ANY] * 5,
        out_specs=(VMEM,) * 6 + (ANY,),
        scratch_shapes=[
            v(2, FF, D),
            v(3, ROWS, D),
            v(ROWS, EXTRA),
            v(8, ROWS, 128),
            DMA((5,)),
            DMA((16,)),
            DMA((16,)),
        ],
        compiler_params=pltpu.CompilerParams(
            collective_id=number, has_side_effects=True, vmem_limit_bytes=24 * 2**20
        ),
        name="turn_back",
    )(total, router, gain, tok.reshape(blocks), att.reshape(blocks), wo.reshape(2, FF, D), members, cot)


def experts(tok, att, wo, members, router, gain, cot, weights, number):
    slots = N_CTX * MOST
    v = lambda *shape: pltpu.VMEM(shape, bf16)
    column = pltpu.VMEM((2, slots, 1), f32)
    blocks = (8, 2, ROWS, D)
    return pl.pallas_call(
        experts_kernel,
        out_shape=(
            jax.ShapeDtypeStruct((ROWS, D), f32),
            jax.ShapeDtypeStruct((ROWS, D + EXTRA), f32),
            jax.ShapeDtypeStruct(weights.shape, bf16),
        ),
        in_specs=[ANY] * 4 + [VMEM] * 2 + [ANY] * 2,
        out_specs=(VMEM, VMEM, ANY),
        scratch_shapes=[
            v(8, 2, 2, ROWS, D + EXTRA),
            v(N_CTX, ROWS, EXTRA),
            v(*weights.shape),
            v(2, FF, D),
            v(N_CTX, 2 * MOST, ROWS),
            pltpu.VMEM((N_CTX, 8, ROWS), f32),
            pltpu.VMEM((N_CTX, 8, ROWS), f32),
            pltpu.VMEM((SEQ, EXTRA), f32),
            column,
            column,
            v(2, slots, D),
            v(2, slots, D),
            v(2, slots, D),
            v(2, slots, FF),
            v(2, slots, 2 * FF),
            DMA((3,)),
            DMA((2, 8)),
        ]
        + RowScatter.scratch(ROWS, D)
        + RowScatter.scratch(ROWS, D + EXTRA)
        + RowGather.scratch,
        compiler_params=pltpu.CompilerParams(
            collective_id=number, has_side_effects=True, vmem_limit_bytes=61 * 2**20
        ),
        cost_estimate=pl.CostEstimate(flops=15 * 10**9, bytes_accessed=30 * 2**20, transcendentals=2**20),
        name="experts_both_ways",
    )(tok.reshape(8, 2 * ROWS, D), att.reshape(blocks), wo.reshape(2, FF, D), members, router, gain, cot, weights)


def swap_halves(u):
    lane = lax.broadcasted_iota(jnp.int32, u.shape, 1)
    return jnp.where(lax.rem(lane, 64) < 32, pltpu.roll(u, 96, 1), pltpu.roll(u, 32, 1))


def attend_kernel(
    src, order, weight_ref, gain_ref, cos_ref, sin_ref, tok_ref,
    o_ref, padded, q_ref, k_ref, v_ref, lse_ref, hidden_ref, out_nat, raw_ref, tok, tok_sem,
):
    core = lax.axis_index("core")
    loads = [pltpu.make_async_copy(tok_ref.at[i], tok.at[i], tok_sem.at[i]) for i in range(8)]
    for load in loads:
        load.start()
    for i in range(8):
        loads[i].wait()
        token = tok[i].astype(f32)
        scale = lax.rsqrt(jnp.mean(token * token, axis=1, keepdims=True) + epsilon)
        hid = (token * scale * gain_ref[...]).astype(bf16)
        hidden_ref[i * 256 : (i + 1) * 256] = hid
        raw_ref[i * 256 : (i + 1) * 256] = dot(hid, weight_ref[...])
    for b in range(SEQ // BLOCK):
        rows = pl.ds(pl.multiple_of(src[b] * BLOCK, BLOCK), BLOCK)
        here = pl.ds(b * BLOCK, BLOCK)
        qk = raw_ref[rows, 0:128]
        qk = qk * cos_ref[here, :] + swap_halves(qk) * sin_ref[here, :]
        q_ref[here, :] = (qk[:, 0:64]).astype(bf16)
        k_ref[here, :] = (qk[:, 64:128]).astype(bf16)
        v_ref[here, :] = raw_ref[rows, 128:192].astype(bf16)
    step = 256
    for i in range(SEQ // step):
        length = (i + 1) * step
        here = pl.ds(i * step, step)
        scores = dot_last(q_ref[here, :], k_ref[0:length, :]) * 0.125
        row = i * step + lax.broadcasted_iota(jnp.int32, (step, length), 0)
        column = lax.broadcasted_iota(jnp.int32, (step, length), 1)
        scores = jnp.where(column <= row, scores, -1e30)
        top = jnp.max(scores, axis=1, keepdims=True)
        weights = jnp.exp(scores - top)
        total = jnp.sum(weights, axis=1, keepdims=True)
        lse_ref[here, :] = top + jnp.log(total)
        probs = (weights * (1.0 / total)).astype(bf16)
        out_nat[here, :] = dot(probs, v_ref[0:length, :])
    for b in range(SEQ // BLOCK):
        rows = pl.ds(pl.multiple_of(order[b] * BLOCK, BLOCK), BLOCK)
        here = pl.ds(b * BLOCK, BLOCK)
        out = out_nat[rows, :].astype(bf16)
        o_ref[here, :] = out
        empty = jnp.zeros_like(out)
        padded[here, :] = jnp.where(
            core == 0, jnp.concatenate([out, empty], axis=1), jnp.concatenate([empty, out], axis=1)
        )


def attend(src, order, weight, gain, cosine, sine, tok):
    head = jax.ShapeDtypeStruct((SEQ, HEAD_DIM), bf16)
    return pl.pallas_call(
        attend_kernel,
        out_shape=(
            head,
            jax.ShapeDtypeStruct((SEQ, 128), bf16),
            head,
            head,
            head,
            jax.ShapeDtypeStruct((SEQ, 1), f32),
            jax.ShapeDtypeStruct((SEQ, D), bf16),
        ),
        in_specs=[SMEM, SMEM, VMEM, VMEM, VMEM, VMEM, ANY],
        out_specs=(VMEM,) * 7,
        scratch_shapes=[
            pltpu.VMEM((SEQ, HEAD_DIM), f32),
            pltpu.VMEM((SEQ, 256), f32),
            pltpu.VMEM((8, 256, D), bf16),
            DMA((8,)),
        ],
        compiler_params=pltpu.CompilerParams(vmem_limit_bytes=56 * 2**20),
        cost_estimate=pl.CostEstimate(flops=2 * 10**9, bytes_accessed=12 * 2**20, transcendentals=2**21),
        name="attention_forward",
    )(src, order, weight, gain, cosine, sine, tok)


def heads_kernel(padded, att_out, mine, other, merged, msem, xsend, xrecv, *sems):
    place = my_place()
    core = place[4]
    pl.semaphore_wait(greet(chip_neighbours(place)), 4)
    half = SEQ // 2
    swap = remote(
        padded.at[pl.ds(pl.multiple_of((1 - core) * half, half), half)], other, xsend, xrecv,
        sibling_of(place),
    )
    swap.start()
    own = pltpu.make_async_copy(padded.at[pl.ds(pl.multiple_of(core * half, half), half)], mine, msem)
    own.start()
    own.wait()
    swap.wait_recv()
    merged[...] = mine[...] + other[...]

    def view(p):
        chip = p[2] * 4 + p[3]
        return att_out.at[
            pl.ds(pl.multiple_of(p[4] * half, half), half), pl.ds(pl.multiple_of(chip * 128, 128), 128)
        ]

    heads = RowGather(place, merged, view, half // 2, *sems)
    heads.start()
    heads.pass_on()
    heads.finish()
    swap.wait_send()


def gather_heads(padded, number):
    return pl.pallas_call(
        heads_kernel,
        out_shape=jax.ShapeDtypeStruct((SEQ, D), bf16),
        in_specs=[ANY],
        out_specs=ANY,
        scratch_shapes=[pltpu.VMEM((SEQ // 2, 128), bf16)] * 3 + [DMA] * 3 + RowGather.scratch,
        compiler_params=pltpu.CompilerParams(collective_id=number, has_side_effects=True),
        name="gather_heads",
    )(padded)


def attend_back_kernel(
    src, order, q_ref, k_ref, v_ref, lse_ref, do_ref, cos_ref, sin_ref, out_ref, do_nat, acc, done
):
    core = lax.axis_index("core")
    for b in range(SEQ // BLOCK):
        rows = pl.ds(pl.multiple_of(src[b] * BLOCK, BLOCK), BLOCK)
        pair = do_ref[rows, :].astype(f32)
        do_nat[pl.ds(b * BLOCK, BLOCK), :] = jnp.where(core == 0, pair[:, :64], pair[:, 64:])
    acc[...] = jnp.zeros_like(acc)
    step = 256
    for i in range(SEQ // step):
        length = (i + 1) * step
        here = pl.ds(i * step, step)
        query, d_out = q_ref[here, :], do_nat[here, :].astype(bf16)
        keys = k_ref[0:length, :]
        scores = dot_last(query, keys) * 0.125
        row = i * step + lax.broadcasted_iota(jnp.int32, (step, length), 0)
        column = lax.broadcasted_iota(jnp.int32, (step, length), 1)
        probs = jnp.where(column <= row, jnp.exp(scores - lse_ref[here, :]), 0.0)
        d_probs = dot_last(d_out, v_ref[0:length, :])
        delta = jnp.sum(probs * d_probs, axis=1, keepdims=True)
        d_scores = (probs * (d_probs - delta)).astype(bf16)
        acc[here, 0:64] = dot(d_scores, keys) * 0.125
        acc[0:length, 64:128] += dot_first(d_scores, query) * 0.125
        acc[0:length, 128:192] += dot_first(probs.astype(bf16), d_out)
    for b in range(SEQ // BLOCK):
        here = pl.ds(b * BLOCK, BLOCK)
        qk = acc[here, 0:128]
        qk = qk * cos_ref[here, :] - swap_halves(qk) * sin_ref[here, :]
        done[here, 0:128] = qk
        done[here, 128:256] = acc[here, 128:256]
    for b in range(SEQ // BLOCK):
        rows = pl.ds(pl.multiple_of(order[b] * BLOCK, BLOCK), BLOCK)
        out_ref[pl.ds(b * BLOCK, BLOCK), :] = done[rows, :].astype(bf16)


def attend_back(src, order, q, k, v, lse, d_out, cosine, sine):
    return pl.pallas_call(
        attend_back_kernel,
        out_shape=jax.ShapeDtypeStruct((SEQ, 256), bf16),
        in_specs=[SMEM, SMEM] + [VMEM] * 7,
        out_specs=VMEM,
        scratch_shapes=[
            pltpu.VMEM((SEQ, HEAD_DIM), f32),
            pltpu.VMEM((SEQ, 256), f32),
            pltpu.VMEM((SEQ, 256), f32),
        ],
        compiler_params=pltpu.CompilerParams(vmem_limit_bytes=56 * 2**20),
        cost_estimate=pl.CostEstimate(flops=3 * 10**9, bytes_accessed=6 * 2**20, transcendentals=2**21),
        name="attention_backward",
    )(src, order, q, k, v, lse, d_out, cosine, sine)


def rotary_tables():
    inverse = 10000.0 ** (-np.arange(32, dtype=np.float64) * 2.0 / HEAD_DIM)
    angles = np.arange(SEQ, dtype=np.float64)[:, None] * inverse[None, :]
    cosine, sine = np.cos(angles), np.sin(angles)
    return (
        np.tile(cosine, (1, 4)).astype(np.float32),
        np.concatenate([-sine, sine, -sine, sine], axis=1).astype(np.float32),
    )


def normalize(inputs, gain_values):
    scale_rows = lax.rsqrt(jnp.mean(inputs * inputs, axis=-1, keepdims=True) + epsilon)
    normed = inputs * scale_rows
    return (scale_rows, normed, (normed * gain_values.astype(f32)).astype(bf16))


def norm_backward(grad_in, normed, scale_rows, gain_values):
    grad_normed = grad_in * gain_values.astype(f32)
    inner = jnp.mean(grad_normed * normed, axis=-1, keepdims=True)
    return (scale_rows * (grad_normed - normed * inner), jnp.sum(grad_in * normed, axis=0))


def halves(value):
    high = lax.reduce_precision(value, 8, 7)
    return high.astype(bf16), (value - high).astype(bf16)


def local(
    tokens,
    cotangent,
    block_order,
    routes,
    norm_one,
    w_query,
    w_key,
    w_value,
    w_out,
    norm_two,
    w_router,
    expert_in,
    expert_out,
):
    ctx = lax.axis_index(CTX)
    cosine, sine = (jnp.asarray(t) for t in rotary_tables())
    order = jnp.stack([block_order, 2 * N_CTX - 1 - block_order], axis=1).reshape(-1)
    spots = jnp.arange(2 * N_CTX, dtype=jnp.int32)
    src = jnp.sum(jnp.where(order[None, :] == spots[:, None], spots[None, :], 0), axis=1)

    small = jnp.concatenate(
        [w_router, norm_one[:, None], norm_two[:, None], jnp.zeros((8, 30), bf16)], axis=1
    )
    tokens_all, packed_all, out_all, members = entry(
        tokens, w_query, w_key, w_value, small, w_out, routes, 0
    )
    down_packed = expert_out.reshape(2, 8, 64, ROWS).swapaxes(1, 2).reshape(2, 64, D)
    expert_all = lax.all_gather(jnp.concatenate([expert_in, down_packed], axis=1), DP, axis=0)
    low = packed_all[:, :, 8:, :].reshape(D, 128)
    weight = jnp.concatenate(
        [packed_all[:, :, :8, :].reshape(D, 128), low[:, :64], jnp.zeros((D, 64), bf16)], axis=1
    )
    router_weight, gain_one, gain_two = low[:, 64:96], low[:, 96], low[:, 97]
    out_weight = out_all.reshape(D, D)
    head_weight = lax.dynamic_slice_in_dim(out_weight, ctx * HEAD_DIM, HEAD_DIM, axis=0)

    tokens_float = tokens.astype(f32)
    scale_one, normed_one, _ = normalize(tokens_float, gain_one)
    _, padded, query, key, value, lse, hidden_one = attend(
        src, order, weight, gain_one.astype(f32)[None, :], cosine, sine, tokens_all.reshape(8, 256, D)
    )
    attended_all = gather_heads(padded, 1)

    router_wide = jnp.pad(router_weight, ((0, 0), (64, 32)))
    gain_row = gain_two.astype(f32)[None, :]
    out_sum, d_sum, grad_experts = experts(
        tokens_all,
        attended_all,
        out_weight,
        members,
        router_wide,
        gain_row,
        cotangent,
        expert_all,
        3,
    )
    residual, d_residual, d_branch, d_logits, hidden_two, grad_gain_two, d_heads = turn(
        d_sum, router_wide, gain_row, tokens_all, attended_all, out_weight, members, cotangent, 6
    )
    output = residual + out_sum
    grad_experts = lax.psum_scatter(grad_experts, DP, scatter_dimension=0).astype(f32)
    grad_in = grad_experts[:, :ROWS]
    grad_down = grad_experts[:, ROWS:].reshape(2, 64, 8, ROWS).swapaxes(1, 2).reshape(2, FF, ROWS)

    d_raw = attend_back(src, order, query, key, value, lse, d_heads.reshape(SEQ, 128), cosine, sine)
    side = jnp.stack([1.0 / gain_one.astype(f32), grad_gain_two[0]], axis=1)
    side = jnp.pad(side, ((0, 0), (0, 126)))
    blocks = (8, 2, ROWS, D)
    d_hidden_one, a, b = last(
        d_raw,
        weight,
        side,
        d_branch,
        d_logits,
        hidden_one,
        attended_all.reshape(blocks),
        hidden_two,
        5,
    )
    d_norm_one, _ = norm_backward(d_hidden_one, normed_one, scale_one, gain_one)
    input_grad = d_residual + d_norm_one

    side_by_side = lambda v: jnp.moveaxis(v, 0, 1).reshape(8, -1)
    pairs = a.reshape(KV_HEADS, 2, 8, 256).sum(axis=1)
    common = jnp.sum(a[:, :, 192:], axis=0)
    return (
        output,
        input_grad,
        common[:, 0],
        side_by_side(a[:, :, 0:64]),
        side_by_side(pairs[:, :, 64:128]),
        side_by_side(pairs[:, :, 128:192]),
        side_by_side(b),
        common[:, 1],
        common[:, 2:34],
        grad_in,
        grad_down,
    )


def solution(mesh):
    split = Mesh(mesh.devices.reshape(2, 4, 2, 4, 2), AXES)
    rows = P(AXES, None)
    line = P(AXES)
    return jax.shard_map(
        local,
        mesh=split,
        in_specs=(
            rows,
            rows,
            P(),
            rows,
            line,
            rows,
            rows,
            rows,
            rows,
            line,
            rows,
            P(CTX, DP, None),
            P(CTX, None, DP),
        ),
        out_specs=(
            rows,
            rows,
            line,
            rows,
            rows,
            rows,
            rows,
            line,
            rows,
            P(CTX, DP, None),
            P(CTX, None, DP),
        ),
        check_vma=False,
    )
```
